32 devices in a mesh: lon: 8 (over z, x), probe: 4 (over y, core).
Axes of the slice: x: 2, y: 2, z: 4, core: 2. Of those that a mesh axis runs over, the one named last changes fastest.
Arguments:
- increments: float32 [64, 192, 8, 256], P('probe', 'lon'), may hold values from -6 to 6
- winds: float32 [2, 192, 8, 256], P(None, 'lon'), may hold values from -0.2 to 0.2
- obs_weight: float32 [192, 8, 256], P('lon'), may hold values from 0.1 to 10
Outputs:
- basis: float32 [64, 48, 512], P('probe', 'lon')
- upper: float32 [64, 64], replicated
The draws below stay inside these ranges and needn't reach their ends.
All inputs are finite; a program needn't handle non-finite values.
Results may differ from the reference program's by a relative error of at most 0.00011.
Values sent between devices are 32-bit elements; how exact they have to be, the bound alone decides.
No kernel may reach another device: no remote copies, remote signals or barrier semaphores. Data moves between devices by JAX's collectives and lax.ppermute only.
A program may use at most 128 MiB of HBM per device.

```python
import math
import jax
import jax.numpy as jnp
from jax import lax

PROBES = 64
LEV = 8
NLAT = 256
NLON = 192


def shard_levels(stream_key, shape, shards, smallest, largest):
    def one(position, blocks):
        steps = jax.random.uniform(jax.random.fold_in(jax.random.fold_in(stream_key, 6), position), (blocks,), jnp.float32, smallest / len(shards), largest / len(shards))
        return jnp.repeat(jnp.exp(steps), shape[position] // blocks).reshape((-1,) + (1,) * (len(shape) - position - 1))

    factor_of = one(*shards[0])
    for cut in shards[1:]:
        factor_of = factor_of * one(*cut)
    return factor_of


def normal_values(rng, extent, width, limit, split=(), kind=jnp.bfloat16):
    drawn = width * jax.random.normal(rng, extent, jnp.float32)
    if split:
        drawn = drawn * shard_levels(rng, extent, split, -0.22, 0.18)
    return jnp.clip(drawn, -limit, limit).astype(kind)


def setup_inputs(seed: int = 0) -> dict:
    seeds = jax.random.split(jax.random.key(seed), 4)
    return {
        "increments": normal_values(seeds[0], (PROBES, NLON, LEV, NLAT), 1.0, 6.0, ((0, 4), (1, 8)), jnp.float32),
        "winds": jnp.clip(jax.random.uniform(seeds[1], (2, NLON, LEV, NLAT), jnp.float32, -0.2, 0.2) * shard_levels(seeds[1], (2, NLON, LEV, NLAT), ((1, 8),), -0.4, 0.0), -0.2, 0.2),
        "obs_weight": jnp.clip(jnp.exp(math.log(10.0) - 4.6051702 * jax.random.uniform(seeds[2], (NLON, LEV, NLAT), jnp.float32) ** shard_levels(seeds[2], (NLON, LEV, NLAT), ((0, 8),), -0.2, 0.2)), 0.1, 10.0),
    }


def lat_mask(field):
    rows = lax.broadcasted_iota(jnp.int32, field.shape, field.ndim - 1)
    return jnp.where(rows > 0, field, jnp.zeros_like(field))

def below(field):
    return jnp.concatenate([jnp.zeros_like(field[..., :1]), field[..., :-1]], axis=-1)

def above(field):
    return jnp.concatenate([field[..., 1:], jnp.zeros_like(field[..., :1])], axis=-1)

def forward_step(field, east, north):
    a_pos = jnp.maximum(east, 0.0)
    b_neg = jnp.minimum(east, 0.0)
    c_pos = jnp.maximum(north, 0.0)
    d_neg = jnp.minimum(north, 0.0)
    flux_w = a_pos * jnp.roll(field, 1, axis=1) + b_neg * field
    flux_e = jnp.roll(flux_w, -1, axis=1)
    flux_s = c_pos * below(field) + d_neg * field
    flux_n = above(flux_s)
    return field - (flux_e - flux_w) - (flux_n - flux_s)

def adjoint_step(field, east, north):
    a_pos = jnp.maximum(east, 0.0)
    b_neg = jnp.minimum(east, 0.0)
    c_pos = jnp.maximum(north, 0.0)
    d_neg = jnp.minimum(north, 0.0)
    a_east = jnp.roll(a_pos, -1, axis=0)
    c_north = above(c_pos)
    west_val = jnp.roll(field, 1, axis=1)
    east_val = jnp.roll(field, -1, axis=1)
    return field * (1.0 - a_east + b_neg - c_north + d_neg) - b_neg * west_val + a_east * east_val - d_neg * below(field) + c_north * above(field)

def reference(increments, winds, obs_weight):
    east = winds[0]
    north = lat_mask(winds[1])
    probe_count = increments.shape[0]
    blocks = increments.reshape((probe_count // 8, 8) + increments.shape[1:])

    def apply_block(block):
        state = forward_step(forward_step(block, east, north), east, north)
        state = obs_weight * state
        state = adjoint_step(adjoint_step(state, east, north), east, north)
        sketch = block + state
        shape_now = sketch.shape
        coarse = jnp.mean(sketch.reshape(shape_now[0], shape_now[1] // 4, 4, shape_now[2], shape_now[3] // 4, 4), axis=(2, 5))
        return coarse
    coarse = lax.map(apply_block, blocks)
    coarse = coarse.reshape(probe_count, -1)
    gram = jnp.dot(coarse.astype(jnp.float32), coarse.T.astype(jnp.float32), precision=lax.Precision.HIGHEST, preferred_element_type=jnp.float32)
    lower = jnp.linalg.cholesky(gram)
    ident = jnp.eye(probe_count, dtype=jnp.float32)
    inverse = lax.linalg.triangular_solve(lower, ident, left_side=True, lower=True)
    basis = jnp.dot(inverse.astype(jnp.float32), coarse.astype(jnp.float32), precision=lax.Precision.HIGHEST, preferred_element_type=jnp.float32)
    basis = basis.reshape(probe_count, increments.shape[1] // 4, -1)
    return (basis, lower.T)
```

```python
import functools

import jax
import jax.numpy as jnp
from jax import lax
from jax.experimental import pallas as pl
from jax.experimental.pallas import tpu as pltpu
from jax.sharding import PartitionSpec as P

F32 = jnp.float32
BF16 = jnp.bfloat16
HALF = 128
DIAG, EAST, WEST, SOUTH_UP, SOUTH_DOWN, NORTH_UP, NORTH_DOWN = range(7)
PLANES = 7


def halves(ref, *index):
    return [ref[index + (slice(None), slice(h * HALF, (h + 1) * HALF))] for h in (0, 1)]


def store(ref, value, *index):
    for h in (0, 1):
        ref[index + (slice(None), slice(h * HALF, (h + 1) * HALF))] = value[h]


class Lanes:
    def __init__(self):
        lane = lax.broadcasted_iota(jnp.int32, (8, HALF), 1)
        self.first = lane == 0
        self.last = lane == HALF - 1
        self.phase = lane & 3
        self.even = ((lane >> 2) & 1) == 0
        self.third = [lax.rem((lane + h * HALF) >> 2, 3) for h in (0, 1)]
        low = self.phase < 2
        self.near = [lax.rem(t + jnp.where(low, 2, 1), 3) for t in self.third]
        self.far = [lax.rem(t + jnp.where(low, 1, 2), 3) for t in self.third]

    def below(self, f):
        r0, r1 = pltpu.roll(f[0], 1, 1), pltpu.roll(f[1], 1, 1)
        return [r0, jnp.where(self.first, r0, r1)]

    def above(self, f):
        r0, r1 = pltpu.roll(f[0], HALF - 1, 1), pltpu.roll(f[1], HALF - 1, 1)
        return [jnp.where(self.last, r1, r0), r1]


def write_coefficients(coef, slot, u, u_next, v, lanes):
    v = [jnp.where(lanes.first, 0.0, v[0]), v[1]]
    south_up = [jnp.maximum(x, 0.0) for x in v]
    south_down = [jnp.maximum(-x, 0.0) for x in v]
    north = []
    for field in (south_up, south_down):
        r0, r1 = pltpu.roll(field[0], HALF - 1, 1), pltpu.roll(field[1], HALF - 1, 1)
        north.append([jnp.where(lanes.last, r1, r0), jnp.where(lanes.last, r0, r1)])
    east = [jnp.maximum(x, 0.0) for x in u]
    west = [jnp.maximum(-x, 0.0) for x in u]
    diag = [
        1.0 - jnp.maximum(u_next[h], 0.0) - west[h] - north[0][h] - south_down[h] for h in (0, 1)
    ]
    for plane, value in (
        (DIAG, diag),
        (EAST, east),
        (WEST, west),
        (SOUTH_UP, south_up),
        (SOUTH_DOWN, south_down),
        (NORTH_UP, north[0]),
        (NORTH_DOWN, north[1]),
    ):
        store(coef, value, plane, slot)


def stencil(lanes, field, r, get, forward):
    total = [None, None]

    def add(coefficient, value):
        for h in (0, 1):
            term = coefficient[h] * value[h]
            total[h] = term if total[h] is None else total[h] + term

    if r in field:
        here = field[r]
        add(get(DIAG, r), here)
        add(get(SOUTH_UP if forward else SOUTH_DOWN, r), lanes.below(here))
        add(get(NORTH_DOWN if forward else NORTH_UP, r), lanes.above(here))
    if r - 1 in field:
        add(get(EAST if forward else WEST, r), field[r - 1])
    if r + 1 in field:
        add(get(WEST if forward else EAST, r + 1), field[r + 1])
    return total


def block_weights(lanes, get, get_obs, first, last):
    state = [{}, {}]
    for r in range(max(first - 3, -1), min(last + 3, 4) + 1):
        if r == -1:
            own = get(WEST, 0)
            other = None
        elif r == 4:
            own = get(EAST, 4)
            other = None
        else:
            own = get(DIAG, r)
            if r > 0:
                own = [x + y for x, y in zip(own, get(EAST, r))]
            if r < 3:
                own = [x + y for x, y in zip(own, get(WEST, r + 1))]
            south, north = get(SOUTH_UP, r), get(NORTH_DOWN, r)
            inner_south = [jnp.where(lanes.phase == 0, 0.0, x) for x in south]
            inner_north = [jnp.where(lanes.phase == 3, 0.0, x) for x in north]
            own = [x + y + z for x, y, z in zip(own, inner_south, inner_north)]
            other = [
                jnp.where(lanes.phase == 0, x, jnp.where(lanes.phase == 3, y, 0.0))
                for x, y in zip(south, north)
            ]
        for colour in (0, 1):
            mine = lanes.even if colour == 0 else jnp.logical_not(lanes.even)
            state[colour][r] = [
                jnp.where(mine, own[h], 0.0 if other is None else other[h]) for h in (0, 1)
            ]
    wide = [{}, {}, {}]
    for r in range(max(first - 2, -2), min(last + 2, 5) + 1):
        obs = get_obs(r)
        pair = [stencil(lanes, state[colour], r, get, True) for colour in (0, 1)]
        pair = [[obs[h] * value[h] for h in (0, 1)] for value in pair]
        own = [jnp.where(lanes.even, pair[0][h], pair[1][h]) for h in (0, 1)]
        other = [jnp.where(lanes.even, pair[1][h], pair[0][h]) for h in (0, 1)]
        for colour in range(3):
            wide[colour][r] = [
                jnp.where(
                    lanes.third[h] == colour,
                    own[h],
                    jnp.where(lanes.near[h] == colour, other[h], 0.0),
                )
                for h in (0, 1)
            ]
    once = [
        {
            r: stencil(lanes, wide[colour], r, get, False)
            for r in range(max(first - 1, -3), min(last + 1, 6) + 1)
        }
        for colour in range(3)
    ]
    weights = {}
    for r in range(first, last + 1):
        twice = [stencil(lanes, once[colour], r, get, False) for colour in range(3)]

        def pick(index):
            return [
                jnp.where(
                    index[h] == 0, twice[0][h], jnp.where(index[h] == 1, twice[1][h], twice[2][h])
                )
                for h in (0, 1)
            ]

        own = pick(lanes.third)
        if 0 <= r <= 3:
            own = [x + 1.0 for x in own]
        weights[r, 0] = own
        if -3 <= r <= 6:
            weights[r, 1] = pick(lanes.near)
        if -1 <= r <= 4:
            weights[r, 2] = pick(lanes.far)
    return weights


def apply_weights(keys, read_weight, read_field, write, probes):
    count = len(probes)
    sums = {}
    for r in sorted({r for r, _ in keys}):
        fields = [read_field(probe, r) for probe in probes]
        for part in range(3):
            if (r, part) not in keys:
                continue
            weight = read_weight(r, part)
            for n in range(count):
                for h in (0, 1):
                    term = weight[h] * fields[n][h]
                    key = (n, part, h)
                    sums[key] = sums[key] + term if key in sums else term
    for n, probe in enumerate(probes):
        for part in range(3):
            for h in (0, 1):
                if (n, part, h) in sums:
                    write(probe, part, h, sums[n, part, h])
                else:
                    write(probe, part, h, jnp.zeros((8, HALF), F32))


def pooling(parity):
    row = lax.broadcasted_iota(jnp.int32, (3 * 256, HALF), 0)
    column = lax.broadcasted_iota(jnp.int32, (3 * 256, HALF), 1) - 64 * parity
    part, lat = row >> 8, row & 255
    low = (lat & 3) < 2
    shift = jnp.where(
        part == 0, 0, jnp.where(part == 1, jnp.where(low, -1, 1), jnp.where(low, 1, -1))
    )
    hit = (column >= 0) & (column < 64) & ((lat >> 2) + shift == column)
    return jnp.where(hit, 1.0 / 16.0, 0.0).astype(BF16)


def split3(x):
    high = x.astype(BF16)
    rest = x - high.astype(F32)
    middle = rest.astype(BF16)
    low = (rest - middle.astype(F32)).astype(BF16)
    return high, middle, low


def pool_into(sums, rows, count, write):
    total = None
    for parity in (0, 1):
        matrix = pooling(parity)
        pieces = [
            jnp.concatenate(
                [
                    sums[piece, pl.ds(n * count * 8 + 2 * pair + parity, count, stride=8), :]
                    for piece in range(6)
                ],
                axis=1,
            )
            for n in range(rows)
            for pair in range(4)
        ]
        for part in split3(jnp.concatenate(pieces, axis=0)):
            term = jnp.dot(part, matrix, preferred_element_type=F32)
            total = term if total is None else total + term
    for n in range(rows):
        for pair in range(4):
            start = (n * 4 + pair) * count
            write(n, pair, total[start : start + count])


GROUP = 4


def interior_kernel(winds, obs, field_hbm, out, coef, weights, sums, field, sem):
    count, lons = field.shape[0], field.shape[1]
    blocks = lons // 4 - 2
    fetch = pltpu.make_async_copy(field_hbm, field, sem)
    fetch.start()
    lanes = Lanes()

    def coefficients(lon, carry):
        write_coefficients(
            coef,
            lon,
            halves(winds, 0, lon),
            halves(winds, 0, jnp.minimum(lon + 1, lons - 1)),
            halves(winds, 1, lon),
            lanes,
        )
        return carry

    lax.fori_loop(0, lons, coefficients, 0)

    def weigh(block, carry):
        base = (block + 1) * 4

        def get(plane, r):
            return halves(coef, plane, base + r)

        result = block_weights(lanes, get, lambda r: halves(obs, base + r), -4, 7)
        for (r, part), value in result.items():
            store(weights, value, block, part, r + 4)
        return carry

    lax.fori_loop(0, blocks, weigh, 0)
    fetch.wait()
    keys = [(r, 0) for r in range(-4, 8)]
    keys += [(r, 1) for r in range(-3, 7)]
    keys += [(r, 2) for r in range(-1, 5)]
    groups = count // GROUP

    def sweep(step, carry):
        block = step // groups
        start = (step % groups) * GROUP

        def write(probe, part, h, value):
            row = pl.multiple_of((block * count + probe) * 8, 8)
            sums[2 * part + h, pl.ds(row, 8), :] = value

        apply_weights(
            keys,
            lambda r, part: halves(weights, block, part, r + 4),
            lambda probe, r: halves(field, probe, block * 4 + 4 + r),
            write,
            [start + n for n in range(GROUP)],
        )
        return carry

    lax.fori_loop(0, blocks * groups, sweep, 0)

    def put(n, pair, value):
        column = (n * 4 + pair) * HALF
        out[:, column : column + HALF] = value

    pool_into(sums, blocks, count, put)


def edge_kernel(
    winds, obs, from_low, from_high, field_hbm, out, coef, weights, sums, field, sems
):
    count, lons = field_hbm.shape[0], field_hbm.shape[1]
    fetches = [
        pltpu.make_async_copy(
            field_hbm.at[:, pl.ds(start, 8)], field.at[:, pl.ds(8 * side, 8)], sems.at[side]
        )
        for side, start in ((0, 0), (1, lons - 8))
    ]
    for fetch in fetches:
        fetch.start()
    lanes = Lanes()

    def wind(which, lon):
        if lon < 0:
            return halves(from_low, 3 * which + lon + 3)
        if lon >= lons:
            return halves(from_high, 4 * which + lon - lons)
        return halves(winds, which, lon)

    def weight_at(lon):
        if lon < 0:
            return halves(from_low, 6 + lon + 2)
        if lon >= lons:
            return halves(from_high, 8 + lon - lons)
        return halves(obs, lon)

    slots = {}
    for lon in list(range(-3, 8)) + list(range(lons - 8, lons + 4)):
        slots[lon] = len(slots)
        last = lon == lons + 3
        write_coefficients(
            coef, slots[lon], wind(0, lon), wind(0, lon if last else lon + 1), wind(1, lon), lanes
        )
    jobs = (
        (-4, 4, 7),
        (0, 0, 7),
        (lons - 4, -4, 3),
        (lons, -4, -1),
    )
    kept = []
    for n, (base, first, last) in enumerate(jobs):
        result = block_weights(
            lanes,
            lambda plane, r: halves(coef, plane, slots[base + r]),
            lambda r: weight_at(base + r),
            first,
            last,
        )
        for (r, part), value in result.items():
            store(weights, value, n, part, r + 4)
        kept.append(set(result))
    for fetch in fetches:
        fetch.wait()

    def sweep(step, carry):
        start = step * GROUP
        for n, (base, first, last) in enumerate(jobs):

            def write(probe, part, h, value):
                row = pl.multiple_of((n * count + probe) * 8, 8)
                sums[2 * part + h, pl.ds(row, 8), :] = value

            def read(probe, r):
                lon = base + r
                return halves(field, probe, lon if lon < 8 else lon - (lons - 16))

            apply_weights(
                kept[n],
                lambda r, part: halves(weights, n, part, r + 4),
                read,
                write,
                [start + k for k in range(GROUP)],
            )
        return carry

    lax.fori_loop(0, count // GROUP, sweep, 0)

    def put(n, pair, value):
        column = (n * 4 + pair) * HALF
        out[:, column : column + HALF] = value

    pool_into(sums, 4, count, put)


def factor_kernel(where, grams, panel, basis, upper, inverse):
    size = grams.shape[1]
    gram = grams[0]
    for n in range(1, grams.shape[0]):
        gram = gram + grams[n]
    row = lax.broadcasted_iota(jnp.int32, (size, size), 0)
    column = lax.broadcasted_iota(jnp.int32, (size, size), 1)
    state = jnp.concatenate([gram, jnp.where(row == column, 1.0, 0.0).astype(F32)], axis=1)
    tiles = [state[8 * t : 8 * t + 8] for t in range(size // 8)]
    sub = lax.broadcasted_iota(jnp.int32, (8, 2 * size), 0)
    scales = []
    for k in range(size):
        own, at = k // 8, k % 8
        pivot_row = jnp.broadcast_to(tiles[own][at : at + 1], (8, 2 * size))
        pivot = jnp.broadcast_to(pivot_row[:, k : k + 1], (8, 2 * size))
        scaled = pivot_row / pivot
        for t in range(own, size // 8):
            factor = jnp.broadcast_to(tiles[t][:, k : k + 1], (8, 2 * size))
            update = factor * scaled
            if t == own:
                update = jnp.where(sub > at, update, 0.0)
            tiles[t] = tiles[t] - update
        scales.append(lax.rsqrt(pivot))
    for t in range(size // 8):
        scale = scales[8 * t]
        for at in range(1, 8):
            scale = jnp.where(sub == at, scales[8 * t + at], scale)
        rows = tiles[t] * scale
        column = lax.broadcasted_iota(jnp.int32, (8, size), 1)
        here = lax.broadcasted_iota(jnp.int32, (8, size), 0) + 8 * t
        upper[8 * t : 8 * t + 8] = jnp.where(column >= here, rows[:, :size], 0.0)
        inverse[8 * t : 8 * t + 8] = rows[:, size:]
    count = basis.shape[0]
    own_rows = inverse[pl.ds(pl.multiple_of(where[0] * count, 8), count)]
    width = basis.shape[2]
    for n in range(basis.shape[1]):
        basis[:, n, :] = jnp.dot(
            own_rows,
            panel[:, n * width : (n + 1) * width],
            precision=lax.Precision.HIGHEST,
            preferred_element_type=F32,
        )


VMEM = pl.BlockSpec(memory_space=pltpu.VMEM)
SMEM = pl.BlockSpec(memory_space=pltpu.SMEM)
ANY = pl.BlockSpec(memory_space=pl.ANY)
LIMIT = 48 * 1024 * 1024


def body(increments, winds, obs_weight):
    count, lons, levels, lats = increments.shape
    blocks = lons // 4
    ring = lax.axis_size("lon")
    up = [(i, (i + 1) % ring) for i in range(ring)]
    down = [(i, (i - 1) % ring) for i in range(ring)]
    pack_up = jnp.concatenate([winds[0, -3:], winds[1, -3:], obs_weight[-2:]], axis=0)
    pack_down = jnp.concatenate([winds[0, :4], winds[1, :4], obs_weight[:2]], axis=0)
    from_low = lax.ppermute(pack_up, "lon", up)
    from_high = lax.ppermute(pack_down, "lon", down)
    inner = pl.pallas_call(
        interior_kernel,
        out_shape=jax.ShapeDtypeStruct((count, (blocks - 2) * 512), F32),
        in_specs=[VMEM, VMEM, ANY],
        out_specs=VMEM,
        scratch_shapes=[
            pltpu.VMEM((PLANES, lons, levels, lats), F32),
            pltpu.VMEM((blocks - 2, 3, 12, levels, lats), F32),
            pltpu.VMEM((6, (blocks - 2) * count * 8, HALF), F32),
            pltpu.VMEM((count, lons, levels, lats), F32),
            pltpu.SemaphoreType.DMA,
        ],
        compiler_params=pltpu.CompilerParams(vmem_limit_bytes=LIMIT),
        name="interior",
    )(winds, obs_weight, increments)
    edges = pl.pallas_call(
        edge_kernel,
        out_shape=jax.ShapeDtypeStruct((count, 4 * 512), F32),
        in_specs=[VMEM, VMEM, VMEM, VMEM, ANY],
        out_specs=VMEM,
        scratch_shapes=[
            pltpu.VMEM((PLANES, 23, levels, lats), F32),
            pltpu.VMEM((4, 3, 12, levels, lats), F32),
            pltpu.VMEM((6, 4 * count * 8, HALF), F32),
            pltpu.VMEM((count, 16, levels, lats), F32),
            pltpu.SemaphoreType.DMA((2,)),
        ],
        compiler_params=pltpu.CompilerParams(vmem_limit_bytes=LIMIT),
        name="edges",
    )(winds, obs_weight, from_low, from_high, increments)
    to_low, own_low, own_high, to_high = jnp.split(edges, 4, axis=1)
    own_low = own_low + lax.ppermute(to_high, "lon", up)
    own_high = own_high + lax.ppermute(to_low, "lon", down)
    coarse = jnp.concatenate([own_low, inner, own_high], axis=1)
    panel = lax.all_gather(coarse, "probe", axis=0, tiled=True)
    gram = jnp.dot(
        panel, panel.T, precision=lax.Precision.HIGHEST, preferred_element_type=F32
    )
    grams = lax.all_to_all(
        jnp.broadcast_to(gram[None], (ring,) + gram.shape), "lon", 0, 0, tiled=True
    )
    probes = panel.shape[0]
    basis, upper = pl.pallas_call(
        factor_kernel,
        out_shape=(
            jax.ShapeDtypeStruct((count, blocks, 512), F32),
            jax.ShapeDtypeStruct((probes, probes), F32),
        ),
        in_specs=[SMEM, VMEM, VMEM],
        out_specs=(VMEM, VMEM),
        scratch_shapes=[pltpu.VMEM((probes, probes), F32)],
        compiler_params=pltpu.CompilerParams(vmem_limit_bytes=LIMIT),
        name="factor",
    )(lax.axis_index("probe").reshape(1).astype(jnp.int32), grams, panel)
    return basis, upper


def solution(mesh):
    in_specs = (P("probe", "lon", None, None), P(None, "lon", None, None), P("lon", None, None))
    out_specs = (P("probe", "lon", None), P())
    return jax.shard_map(body, mesh=mesh, in_specs=in_specs, out_specs=out_specs, check_vma=False)
```

```python
import functools

import jax
import jax.numpy as jnp
from jax import lax
from jax.experimental import pallas as pl
from jax.experimental.pallas import tpu as pltpu
from jax.sharding import PartitionSpec as P

F32 = jnp.float32
BF16 = jnp.bfloat16
HALF = 128
DIAG, EAST, WEST, SOUTH_UP, SOUTH_DOWN, NORTH_UP, NORTH_DOWN = range(7)
PLANES = 7


def halves(ref, *index):
    return [ref[index + (slice(None), slice(h * HALF, (h + 1) * HALF))] for h in (0, 1)]


def store(ref, value, *index):
    for h in (0, 1):
        ref[index + (slice(None), slice(h * HALF, (h + 1) * HALF))] = value[h]


class Lanes:
    def __init__(self):
        lane = lax.broadcasted_iota(jnp.int32, (8, HALF), 1)
        self.first = lane == 0
        self.last = lane == HALF - 1
        self.phase = lane & 3
        self.even = ((lane >> 2) & 1) == 0
        self.third = [lax.rem((lane + h * HALF) >> 2, 3) for h in (0, 1)]
        low = self.phase < 2
        self.near = [lax.rem(t + jnp.where(low, 2, 1), 3) for t in self.third]
        self.far = [lax.rem(t + jnp.where(low, 1, 2), 3) for t in self.third]

    def below(self, f):
        r0, r1 = pltpu.roll(f[0], 1, 1), pltpu.roll(f[1], 1, 1)
        return [r0, jnp.where(self.first, r0, r1)]

    def above(self, f):
        r0, r1 = pltpu.roll(f[0], HALF - 1, 1), pltpu.roll(f[1], HALF - 1, 1)
        return [jnp.where(self.last, r1, r0), r1]


def write_coefficients(coef, slot, u, u_next, v, lanes):
    v = [jnp.where(lanes.first, 0.0, v[0]), v[1]]
    south_up = [jnp.maximum(x, 0.0) for x in v]
    south_down = [jnp.maximum(-x, 0.0) for x in v]
    north = []
    for field in (south_up, south_down):
        r0, r1 = pltpu.roll(field[0], HALF - 1, 1), pltpu.roll(field[1], HALF - 1, 1)
        north.append([jnp.where(lanes.last, r1, r0), jnp.where(lanes.last, r0, r1)])
    east = [jnp.maximum(x, 0.0) for x in u]
    west = [jnp.maximum(-x, 0.0) for x in u]
    diag = [
        1.0 - jnp.maximum(u_next[h], 0.0) - west[h] - north[0][h] - south_down[h] for h in (0, 1)
    ]
    for plane, value in (
        (DIAG, diag),
        (EAST, east),
        (WEST, west),
        (SOUTH_UP, south_up),
        (SOUTH_DOWN, south_down),
        (NORTH_UP, north[0]),
        (NORTH_DOWN, north[1]),
    ):
        store(coef, value, plane, slot)


def stencil(lanes, field, r, get, forward):
    total = [None, None]

    def add(coefficient, value):
        for h in (0, 1):
            term = coefficient[h] * value[h]
            total[h] = term if total[h] is None else total[h] + term

    if r in field:
        here = field[r]
        add(get(DIAG, r), here)
        add(get(SOUTH_UP if forward else SOUTH_DOWN, r), lanes.below(here))
        add(get(NORTH_DOWN if forward else NORTH_UP, r), lanes.above(here))
    if r - 1 in field:
        add(get(EAST if forward else WEST, r), field[r - 1])
    if r + 1 in field:
        add(get(WEST if forward else EAST, r + 1), field[r + 1])
    return total


def block_weights(lanes, get, get_obs, first, last):
    state = [{}, {}]
    for r in range(max(first - 3, -1), min(last + 3, 4) + 1):
        if r == -1:
            own = get(WEST, 0)
            other = None
        elif r == 4:
            own = get(EAST, 4)
            other = None
        else:
            own = get(DIAG, r)
            if r > 0:
                own = [x + y for x, y in zip(own, get(EAST, r))]
            if r < 3:
                own = [x + y for x, y in zip(own, get(WEST, r + 1))]
            south, north = get(SOUTH_UP, r), get(NORTH_DOWN, r)
            inner_south = [jnp.where(lanes.phase == 0, 0.0, x) for x in south]
            inner_north = [jnp.where(lanes.phase == 3, 0.0, x) for x in north]
            own = [x + y + z for x, y, z in zip(own, inner_south, inner_north)]
            other = [
                jnp.where(lanes.phase == 0, x, jnp.where(lanes.phase == 3, y, 0.0))
                for x, y in zip(south, north)
            ]
        for colour in (0, 1):
            mine = lanes.even if colour == 0 else jnp.logical_not(lanes.even)
            state[colour][r] = [
                jnp.where(mine, own[h], 0.0 if other is None else other[h]) for h in (0, 1)
            ]
    wide = [{}, {}, {}]
    for r in range(max(first - 2, -2), min(last + 2, 5) + 1):
        obs = get_obs(r)
        pair = [stencil(lanes, state[colour], r, get, True) for colour in (0, 1)]
        pair = [[obs[h] * value[h] for h in (0, 1)] for value in pair]
        own = [jnp.where(lanes.even, pair[0][h], pair[1][h]) for h in (0, 1)]
        other = [jnp.where(lanes.even, pair[1][h], pair[0][h]) for h in (0, 1)]
        for colour in range(3):
            wide[colour][r] = [
                jnp.where(
                    lanes.third[h] == colour,
                    own[h],
                    jnp.where(lanes.near[h] == colour, other[h], 0.0),
                )
                for h in (0, 1)
            ]
    once = [
        {
            r: stencil(lanes, wide[colour], r, get, False)
            for r in range(max(first - 1, -3), min(last + 1, 6) + 1)
        }
        for colour in range(3)
    ]
    weights = {}
    for r in range(first, last + 1):
        twice = [stencil(lanes, once[colour], r, get, False) for colour in range(3)]

        def pick(index):
            return [
                jnp.where(
                    index[h] == 0, twice[0][h], jnp.where(index[h] == 1, twice[1][h], twice[2][h])
                )
                for h in (0, 1)
            ]

        own = pick(lanes.third)
        if 0 <= r <= 3:
            own = [x + 1.0 for x in own]
        weights[r, 0] = own
        if -3 <= r <= 6:
            weights[r, 1] = pick(lanes.near)
        if -1 <= r <= 4:
            weights[r, 2] = pick(lanes.far)
    return weights


def apply_weights(keys, read_weight, read_field, write, probes):
    count = len(probes)
    sums = {}
    for r in sorted({r for r, _ in keys}):
        fields = [read_field(probe, r) for probe in probes]
        for part in range(3):
            if (r, part) not in keys:
                continue
            weight = read_weight(r, part)
            for n in range(count):
                for h in (0, 1):
                    term = weight[h] * fields[n][h]
                    key = (n, part, h)
                    sums[key] = sums[key] + term if key in sums else term
    for n, probe in enumerate(probes):
        for part in range(3):
            for h in (0, 1):
                if (n, part, h) in sums:
                    write(probe, part, h, sums[n, part, h])
                else:
                    write(probe, part, h, jnp.zeros((8, HALF), F32))


def pooling(parity):
    row = lax.broadcasted_iota(jnp.int32, (3 * 256, HALF), 0)
    column = lax.broadcasted_iota(jnp.int32, (3 * 256, HALF), 1) - 64 * parity
    part, lat = row >> 8, row & 255
    low = (lat & 3) < 2
    shift = jnp.where(
        part == 0, 0, jnp.where(part == 1, jnp.where(low, -1, 1), jnp.where(low, 1, -1))
    )
    hit = (column >= 0) & (column < 64) & ((lat >> 2) + shift == column)
    return jnp.where(hit, 1.0 / 16.0, 0.0).astype(BF16)


def split3(x):
    high = x.astype(BF16)
    rest = x - high.astype(F32)
    middle = rest.astype(BF16)
    low = (rest - middle.astype(F32)).astype(BF16)
    return high, middle, low


def pool_into(sums, rows, count, write):
    total = None
    for parity in (0, 1):
        matrix = pooling(parity)
        pieces = [
            jnp.concatenate(
                [
                    sums[piece, pl.ds(n * count * 8 + 2 * pair + parity, count, stride=8), :]
                    for piece in range(6)
                ],
                axis=1,
            )
            for n in range(rows)
            for pair in range(4)
        ]
        for part in split3(jnp.concatenate(pieces, axis=0)):
            term = jnp.dot(part, matrix, preferred_element_type=F32)
            total = term if total is None else total + term
    for n in range(rows):
        for pair in range(4):
            start = (n * 4 + pair) * count
            write(n, pair, total[start : start + count])


GROUP = 4


def fetch_all(copies):
    for copy in copies:
        copy.start()
    return copies


def pack_kernel(winds, obs, low, high, sems):
    lons = obs.shape[0]
    copies = fetch_all(
        [
            pltpu.make_async_copy(winds.at[0, pl.ds(lons - 3, 3)], low.at[pl.ds(0, 3)], sems.at[0]),
            pltpu.make_async_copy(winds.at[1, pl.ds(lons - 3, 3)], low.at[pl.ds(3, 3)], sems.at[1]),
            pltpu.make_async_copy(obs.at[pl.ds(lons - 2, 2)], low.at[pl.ds(6, 2)], sems.at[2]),
            pltpu.make_async_copy(winds.at[0, pl.ds(0, 4)], high.at[pl.ds(0, 4)], sems.at[3]),
            pltpu.make_async_copy(winds.at[1, pl.ds(0, 4)], high.at[pl.ds(4, 4)], sems.at[4]),
            pltpu.make_async_copy(obs.at[pl.ds(0, 2)], high.at[pl.ds(8, 2)], sems.at[5]),
        ]
    )
    for copy in copies:
        copy.wait()


def interior_kernel(
    winds_hbm, obs_hbm, field_hbm, out, winds, obs, coef, weights, sums, field, sems
):
    count, lons = field.shape[0], field.shape[1]
    blocks = lons // 4 - 2
    wind_copy, obs_copy, field_copy = fetch_all(
        [
            pltpu.make_async_copy(winds_hbm, winds, sems.at[0]),
            pltpu.make_async_copy(obs_hbm, obs, sems.at[1]),
            pltpu.make_async_copy(field_hbm, field, sems.at[2]),
        ]
    )
    lanes = Lanes()
    wind_copy.wait()

    def coefficients(lon, carry):
        write_coefficients(
            coef,
            lon,
            halves(winds, 0, lon),
            halves(winds, 0, jnp.minimum(lon + 1, lons - 1)),
            halves(winds, 1, lon),
            lanes,
        )
        return carry

    lax.fori_loop(0, lons, coefficients, 0)
    obs_copy.wait()

    def weigh(block, carry):
        base = (block + 1) * 4

        def get(plane, r):
            return halves(coef, plane, base + r)

        result = block_weights(lanes, get, lambda r: halves(obs, base + r), -4, 7)
        for (r, part), value in result.items():
            store(weights, value, block, part, r + 4)
        return carry

    lax.fori_loop(0, blocks, weigh, 0)
    field_copy.wait()
    keys = [(r, 0) for r in range(-4, 8)]
    keys += [(r, 1) for r in range(-3, 7)]
    keys += [(r, 2) for r in range(-1, 5)]
    groups = count // GROUP

    def sweep(step, carry):
        block = step // groups
        start = (step % groups) * GROUP

        def write(probe, part, h, value):
            row = pl.multiple_of((block * count + probe) * 8, 8)
            sums[2 * part + h, pl.ds(row, 8), :] = value

        apply_weights(
            keys,
            lambda r, part: halves(weights, block, part, r + 4),
            lambda probe, r: halves(field, probe, block * 4 + 4 + r),
            write,
            [start + n for n in range(GROUP)],
        )
        return carry

    lax.fori_loop(0, blocks * groups, sweep, 0)

    def put(n, pair, value):
        column = (n * 4 + pair) * HALF
        out[:, column : column + HALF] = value

    pool_into(sums, blocks, count, put)


def edge_kernel(
    winds_hbm, obs_hbm, from_low, from_high, field_hbm,
    to_low, own_low, own_high, to_high,
    winds, obs, coef, weights, sums, field, sems,
):
    count, lons = field_hbm.shape[0], field_hbm.shape[1]
    sides = ((0, 0), (1, lons - 8))
    copies = fetch_all(
        [
            pltpu.make_async_copy(
                winds_hbm.at[:, pl.ds(start, 8)], winds.at[:, pl.ds(8 * side, 8)], sems.at[side]
            )
            for side, start in sides
        ]
        + [
            pltpu.make_async_copy(
                obs_hbm.at[pl.ds(start, 8)], obs.at[pl.ds(8 * side, 8)], sems.at[2 + side]
            )
            for side, start in sides
        ]
        + [
            pltpu.make_async_copy(
                field_hbm.at[:, pl.ds(start, 8)], field.at[:, pl.ds(8 * side, 8)], sems.at[4 + side]
            )
            for side, start in sides
        ]
    )
    lanes = Lanes()
    for copy in copies[:4]:
        copy.wait()

    def near(lon):
        return lon if lon < 8 else lon - (lons - 16)

    def wind(which, lon):
        if lon < 0:
            return halves(from_low, 3 * which + lon + 3)
        if lon >= lons:
            return halves(from_high, 4 * which + lon - lons)
        return halves(winds, which, near(lon))

    def weight_at(lon):
        if lon < 0:
            return halves(from_low, 6 + lon + 2)
        if lon >= lons:
            return halves(from_high, 8 + lon - lons)
        return halves(obs, near(lon))

    slots = {}
    for lon in list(range(-3, 8)) + list(range(lons - 8, lons + 4)):
        slots[lon] = len(slots)
        last = lon in (7, lons + 3)
        write_coefficients(
            coef, slots[lon], wind(0, lon), wind(0, lon if last else lon + 1), wind(1, lon), lanes
        )
    jobs = (
        (-4, 4, 7),
        (0, 0, 7),
        (lons - 4, -4, 3),
        (lons, -4, -1),
    )
    kept = []
    for n, (base, first, last) in enumerate(jobs):
        result = block_weights(
            lanes,
            lambda plane, r: halves(coef, plane, slots[base + r]),
            lambda r: weight_at(base + r),
            first,
            last,
        )
        for (r, part), value in result.items():
            store(weights, value, n, part, r + 4)
        kept.append(set(result))
    for copy in copies[4:]:
        copy.wait()

    def sweep(step, carry):
        start = step * GROUP
        for n, (base, first, last) in enumerate(jobs):

            def write(probe, part, h, value):
                row = pl.multiple_of((n * count + probe) * 8, 8)
                sums[2 * part + h, pl.ds(row, 8), :] = value

            apply_weights(
                kept[n],
                lambda r, part: halves(weights, n, part, r + 4),
                lambda probe, r: halves(field, probe, near(base + r)),
                write,
                [start + k for k in range(GROUP)],
            )
        return carry

    lax.fori_loop(0, count // GROUP, sweep, 0)
    outs = (to_low, own_low, own_high, to_high)

    def put(n, pair, value):
        outs[n][:, pair * HALF : (pair + 1) * HALF] = value

    pool_into(sums, 4, count, put)


def self_product(panel):
    return lax.dot_general(
        panel,
        panel,
        (((1,), (1,)), ((), ())),
        precision=lax.Precision.HIGHEST,
        preferred_element_type=F32,
    )


def inner_gram_kernel(panel, out):
    out[...] = self_product(panel[...])


def gram_kernel(panel, inner, out):
    gram = self_product(panel[...]) + inner[...]
    half = gram.shape[0] // 2
    packed = jnp.concatenate([gram[:half], gram[half:]], axis=1)
    for n in range(out.shape[0]):
        out[n] = packed


def factor_kernel(where, grams, inner, edge, basis, upper, inverse):
    packed = grams[0]
    for n in range(1, grams.shape[0]):
        packed = packed + grams[n]
    size = 2 * packed.shape[0]
    gram = jnp.concatenate([packed[:, :size], packed[:, size:]], axis=0)
    row = lax.broadcasted_iota(jnp.int32, (size, size), 0)
    column = lax.broadcasted_iota(jnp.int32, (size, size), 1)
    state = jnp.concatenate([gram, jnp.where(row == column, 1.0, 0.0).astype(F32)], axis=1)
    tiles = [state[8 * t : 8 * t + 8] for t in range(size // 8)]
    full = (8, 2 * size)
    sub = lax.broadcasted_iota(jnp.int32, full, 0)
    scales = []
    for own in range(size // 8):
        spread = {
            (t, j): jnp.broadcast_to(tiles[t][:, 8 * own + j : 8 * own + j + 1], full)
            for t in range(own, size // 8)
            for j in range(8)
        }
        pivots = {
            (i, j): jnp.broadcast_to(spread[own, j][i : i + 1], full)
            for i in range(8)
            for j in range(i + 1)
        }
        rows = [jnp.broadcast_to(tiles[own][j : j + 1], full) for j in range(8)]
        inverses = []
        for j in range(8):
            inverses.append(1.0 / pivots[j, j])
            scales.append(lax.rsqrt(pivots[j, j]))
            for i in range(j + 1, 8):
                ratio = pivots[i, j] * inverses[j]
                for m in range(i, 8):
                    pivots[m, i] = pivots[m, i] - ratio * pivots[m, j]
                rows[i] = rows[i] - ratio * rows[j]
                for t in range(own + 1, size // 8):
                    spread[t, i] = spread[t, i] - ratio * spread[t, j]
        for t in range(own + 1, size // 8):
            update = (spread[t, 0] * inverses[0]) * rows[0]
            for j in range(1, 8):
                update = update + (spread[t, j] * inverses[j]) * rows[j]
            tiles[t] = tiles[t] - update
        for j in range(8):
            tiles[own] = jnp.where(sub == j, rows[j], tiles[own])
    for t in range(size // 8):
        scale = scales[8 * t]
        for at in range(1, 8):
            scale = jnp.where(sub == at, scales[8 * t + at], scale)
        scaled = tiles[t] * scale
        column = lax.broadcasted_iota(jnp.int32, (8, size), 1)
        here = lax.broadcasted_iota(jnp.int32, (8, size), 0) + 8 * t
        upper[8 * t : 8 * t + 8] = jnp.where(column >= here, scaled[:, :size], 0.0)
        inverse[8 * t : 8 * t + 8] = scaled[:, size:]
    blocks, count, width = basis.shape
    own_rows = inverse[pl.ds(pl.multiple_of(where[0] * count, 8), count)]

    def project(columns):
        return jnp.dot(
            own_rows, columns, precision=lax.Precision.HIGHEST, preferred_element_type=F32
        )

    basis[0] = project(edge[:, :width])
    for n in range(blocks - 2):
        basis[n + 1] = project(inner[:, n * width : (n + 1) * width])
    basis[blocks - 1] = project(edge[:, width:])


VMEM = pl.BlockSpec(memory_space=pltpu.VMEM)
SMEM = pl.BlockSpec(memory_space=pltpu.SMEM)
HBM = pl.BlockSpec(memory_space=pltpu.HBM)
MIB = 1024 * 1024


def shape(*dims):
    return jax.ShapeDtypeStruct(dims, F32)


def call(kernel, name, out_shape, in_specs, scratch=(), flops=0):
    return pl.pallas_call(
        kernel,
        out_shape=out_shape,
        in_specs=in_specs,
        out_specs=jax.tree.map(lambda _: VMEM, out_shape),
        scratch_shapes=scratch,
        compiler_params=pltpu.CompilerParams(vmem_limit_bytes=32 * MIB),
        cost_estimate=pl.CostEstimate(flops=flops, bytes_accessed=4_000_000, transcendentals=0),
        name=name,
    )


def body(increments, winds, obs_weight):
    count, lons, levels, lats = increments.shape
    blocks = lons // 4
    probes = count * lax.axis_size("probe")
    ring = lax.axis_size("lon")
    up = [(i, (i + 1) % ring) for i in range(ring)]
    down = [(i, (i - 1) % ring) for i in range(ring)]
    dma = pltpu.SemaphoreType.DMA
    increments, winds, obs_weight = (
        pltpu.with_memory_space_constraint(x, pltpu.HBM) for x in (increments, winds, obs_weight)
    )
    pack_up, pack_down = call(
        pack_kernel,
        "pack",
        (shape(8, levels, lats), shape(10, levels, lats)),
        [HBM, HBM],
        [dma((6,))],
    )(winds, obs_weight)
    from_low = lax.ppermute(pack_up, "lon", up)
    from_high = lax.ppermute(pack_down, "lon", down)
    inner = call(
        interior_kernel,
        "interior",
        shape(count, (blocks - 2) * 512),
        [HBM, HBM, HBM],
        [
            pltpu.VMEM((2, lons, levels, lats), F32),
            pltpu.VMEM((lons, levels, lats), F32),
            pltpu.VMEM((PLANES, lons, levels, lats), F32),
            pltpu.VMEM((blocks - 2, 3, 12, levels, lats), F32),
            pltpu.VMEM((6, (blocks - 2) * count * 8, HALF), F32),
            pltpu.VMEM((count, lons, levels, lats), F32),
            dma((3,)),
        ],
        200_000_000,
    )(winds, obs_weight, increments)
    edges = call(
        edge_kernel,
        "edges",
        (shape(count, 512),) * 4,
        [HBM, HBM, VMEM, VMEM, HBM],
        [
            pltpu.VMEM((2, 16, levels, lats), F32),
            pltpu.VMEM((16, levels, lats), F32),
            pltpu.VMEM((PLANES, 23, levels, lats), F32),
            pltpu.VMEM((4, 3, 12, levels, lats), F32),
            pltpu.VMEM((6, 4 * count * 8, HALF), F32),
            pltpu.VMEM((count, 16, levels, lats), F32),
            dma((6,)),
        ],
        100_000_000,
    )(winds, obs_weight, from_low, from_high, increments)
    to_low, own_low, own_high, to_high = edges
    inner, own_low = lax.optimization_barrier((inner, own_low))
    own_low = own_low + lax.ppermute(to_high, "lon", up)
    own_high = own_high + lax.ppermute(to_low, "lon", down)
    inner_panel = lax.all_gather(inner, "probe", axis=0, tiled=True)
    inner_gram = call(
        inner_gram_kernel, "inner_gram", shape(probes, probes), [VMEM], (), 25_000_000
    )(inner_panel)
    edge_panel = lax.all_gather(
        jnp.concatenate([own_low, own_high], axis=1), "probe", axis=0, tiled=True
    )
    grams = call(
        gram_kernel, "gram", shape(ring, probes // 2, 2 * probes), [VMEM, VMEM], (), 10_000_000
    )(edge_panel, inner_gram)
    grams = lax.all_to_all(grams, "lon", 0, 0, tiled=True)
    basis, upper = call(
        factor_kernel,
        "factor",
        (shape(blocks, count, 512), shape(probes, probes)),
        [SMEM, VMEM, VMEM, VMEM],
        [pltpu.VMEM((probes, probes), F32)],
        10_000_000,
    )(lax.axis_index("probe").reshape(1).astype(jnp.int32), grams, inner_panel, edge_panel)
    return basis.transpose(1, 0, 2), upper


def solution(mesh):
    in_specs = (P("probe", "lon", None, None), P(None, "lon", None, None), P("lon", None, None))
    out_specs = (P("probe", "lon", None), P())
    return jax.shard_map(body, mesh=mesh, in_specs=in_specs, out_specs=out_specs, check_vma=False)
```

```python
import functools

import jax
import jax.numpy as jnp
from jax import lax
from jax.experimental import pallas as pl
from jax.experimental.pallas import tpu as pltpu
from jax.sharding import PartitionSpec as P

F32 = jnp.float32
BF16 = jnp.bfloat16
HALF = 128
DIAG, EAST, WEST, SOUTH_UP, SOUTH_DOWN, NORTH_UP, NORTH_DOWN = range(7)
PLANES = 7


def halves(ref, *index):
    return [ref[index + (slice(None), slice(h * HALF, (h + 1) * HALF))] for h in (0, 1)]


def store(ref, value, *index):
    for h in (0, 1):
        ref[index + (slice(None), slice(h * HALF, (h + 1) * HALF))] = value[h]


class Lanes:
    def __init__(self):
        lane = lax.broadcasted_iota(jnp.int32, (8, HALF), 1)
        self.first = lane == 0
        self.last = lane == HALF - 1
        self.phase = lane & 3
        self.even = ((lane >> 2) & 1) == 0
        self.third = [lax.rem((lane + h * HALF) >> 2, 3) for h in (0, 1)]
        low = self.phase < 2
        self.near = [lax.rem(t + jnp.where(low, 2, 1), 3) for t in self.third]
        self.far = [lax.rem(t + jnp.where(low, 1, 2), 3) for t in self.third]

    def below(self, f):
        r0, r1 = pltpu.roll(f[0], 1, 1), pltpu.roll(f[1], 1, 1)
        return [r0, jnp.where(self.first, r0, r1)]

    def above(self, f):
        r0, r1 = pltpu.roll(f[0], HALF - 1, 1), pltpu.roll(f[1], HALF - 1, 1)
        return [jnp.where(self.last, r1, r0), r1]


def write_coefficients(coef, slot, u, u_next, v, lanes):
    v = [jnp.where(lanes.first, 0.0, v[0]), v[1]]
    south_up = [jnp.maximum(x, 0.0) for x in v]
    south_down = [jnp.maximum(-x, 0.0) for x in v]
    north = []
    for field in (south_up, south_down):
        r0, r1 = pltpu.roll(field[0], HALF - 1, 1), pltpu.roll(field[1], HALF - 1, 1)
        north.append([jnp.where(lanes.last, r1, r0), jnp.where(lanes.last, r0, r1)])
    east = [jnp.maximum(x, 0.0) for x in u]
    west = [jnp.maximum(-x, 0.0) for x in u]
    diag = [
        1.0 - jnp.maximum(u_next[h], 0.0) - west[h] - north[0][h] - south_down[h] for h in (0, 1)
    ]
    for plane, value in (
        (DIAG, diag),
        (EAST, east),
        (WEST, west),
        (SOUTH_UP, south_up),
        (SOUTH_DOWN, south_down),
        (NORTH_UP, north[0]),
        (NORTH_DOWN, north[1]),
    ):
        store(coef, value, plane, slot)


def stencil(lanes, field, r, get, forward):
    total = [None, None]

    def add(coefficient, value):
        for h in (0, 1):
            term = coefficient[h] * value[h]
            total[h] = term if total[h] is None else total[h] + term

    if r in field:
        here = field[r]
        add(get(DIAG, r), here)
        add(get(SOUTH_UP if forward else SOUTH_DOWN, r), lanes.below(here))
        add(get(NORTH_DOWN if forward else NORTH_UP, r), lanes.above(here))
    if r - 1 in field:
        add(get(EAST if forward else WEST, r), field[r - 1])
    if r + 1 in field:
        add(get(WEST if forward else EAST, r + 1), field[r + 1])
    return total


def block_weights(lanes, get, get_obs, first, last):
    state = [{}, {}]
    for r in range(max(first - 3, -1), min(last + 3, 4) + 1):
        if r == -1:
            own = get(WEST, 0)
            other = None
        elif r == 4:
            own = get(EAST, 4)
            other = None
        else:
            own = get(DIAG, r)
            if r > 0:
                own = [x + y for x, y in zip(own, get(EAST, r))]
            if r < 3:
                own = [x + y for x, y in zip(own, get(WEST, r + 1))]
            south, north = get(SOUTH_UP, r), get(NORTH_DOWN, r)
            inner_south = [jnp.where(lanes.phase == 0, 0.0, x) for x in south]
            inner_north = [jnp.where(lanes.phase == 3, 0.0, x) for x in north]
            own = [x + y + z for x, y, z in zip(own, inner_south, inner_north)]
            other = [
                jnp.where(lanes.phase == 0, x, jnp.where(lanes.phase == 3, y, 0.0))
                for x, y in zip(south, north)
            ]
        for colour in (0, 1):
            mine = lanes.even if colour == 0 else jnp.logical_not(lanes.even)
            state[colour][r] = [
                jnp.where(mine, own[h], 0.0 if other is None else other[h]) for h in (0, 1)
            ]
    wide = [{}, {}, {}]
    for r in range(max(first - 2, -2), min(last + 2, 5) + 1):
        obs = get_obs(r)
        pair = [stencil(lanes, state[colour], r, get, True) for colour in (0, 1)]
        pair = [[obs[h] * value[h] for h in (0, 1)] for value in pair]
        own = [jnp.where(lanes.even, pair[0][h], pair[1][h]) for h in (0, 1)]
        other = [jnp.where(lanes.even, pair[1][h], pair[0][h]) for h in (0, 1)]
        for colour in range(3):
            wide[colour][r] = [
                jnp.where(
                    lanes.third[h] == colour,
                    own[h],
                    jnp.where(lanes.near[h] == colour, other[h], 0.0),
                )
                for h in (0, 1)
            ]
    once = [
        {
            r: stencil(lanes, wide[colour], r, get, False)
            for r in range(max(first - 1, -3), min(last + 1, 6) + 1)
        }
        for colour in range(3)
    ]
    weights = {}
    for r in range(first, last + 1):
        twice = [stencil(lanes, once[colour], r, get, False) for colour in range(3)]

        def pick(index):
            return [
                jnp.where(
                    index[h] == 0, twice[0][h], jnp.where(index[h] == 1, twice[1][h], twice[2][h])
                )
                for h in (0, 1)
            ]

        own = pick(lanes.third)
        if 0 <= r <= 3:
            own = [x + 1.0 for x in own]
        weights[r, 0] = own
        if -3 <= r <= 6:
            weights[r, 1] = pick(lanes.near)
        if -1 <= r <= 4:
            weights[r, 2] = pick(lanes.far)
    return weights


def apply_weights(lanes, keys, read_weight, read_field, write, probes):
    sums = {}
    for r in sorted({r for r, _ in keys}):
        fields = [read_field(probe, r) for probe in probes]
        for part in range(3):
            if (r, part) not in keys:
                continue
            weight = read_weight(r, part)
            for n in range(len(probes)):
                for h in (0, 1):
                    term = weight[h] * fields[n][h]
                    key = (n, part, h)
                    sums[key] = sums[key] + term if key in sums else term
    low = lanes.phase < 2
    for n, probe in enumerate(probes):
        own, near, far = ([sums.get((n, part, h)) for h in (0, 1)] for part in range(3))
        if far[0] is None:
            down = [jnp.where(low, x, 0.0) for x in near]
            up = [jnp.where(low, 0.0, x) for x in near]
        else:
            down = [jnp.where(low, x, y) for x, y in zip(near, far)]
            up = [jnp.where(low, y, x) for x, y in zip(near, far)]
        for h in (0, 1):
            write(probe, 0, h, own[h])
            write(probe, 1, h, down[h])
            write(probe, 2, h, up[h])


def pooling(parity):
    row = lax.broadcasted_iota(jnp.int32, (256, HALF), 0)
    column = lax.broadcasted_iota(jnp.int32, (256, HALF), 1)
    return jnp.where((row >> 2) + 64 * parity == column, 1.0 / 16.0, 0.0).astype(BF16)


def split3(x):
    high = x.astype(BF16)
    rest = x - high.astype(F32)
    middle = rest.astype(BF16)
    low = (rest - middle.astype(F32)).astype(BF16)
    return high, middle, low


def pool_into(lanes, sums, rows, count, write):
    total = None
    for parity in (0, 1):
        matrix = pooling(parity)
        own, down, up = (
            [
                jnp.concatenate(
                    [
                        sums[2 * part + h, pl.ds(n * count * 8 + 2 * pair + parity, count, stride=8), :]
                        for n in range(rows)
                        for pair in range(4)
                    ],
                    axis=0,
                )
                for h in (0, 1)
            ]
            for part in range(3)
        )
        lane = lax.broadcasted_iota(jnp.int32, own[0].shape, 1)
        d0, d1 = (pltpu.roll(x, HALF - 4, 1) for x in down)
        u0, u1 = (pltpu.roll(x, 4, 1) for x in up)
        low = own[0] + (jnp.where(lane >= HALF - 4, d1, d0) + jnp.where(lane < 4, u1, u0))
        high = own[1] + (jnp.where(lane >= HALF - 4, d0, d1) + jnp.where(lane < 4, u0, u1))
        for part in split3(jnp.concatenate([low, high], axis=1)):
            term = jnp.dot(part, matrix, preferred_element_type=F32)
            total = term if total is None else total + term
    for n in range(rows):
        for pair in range(4):
            start = (n * 4 + pair) * count
            write(n, pair, total[start : start + count])


GROUP = 8


def fetch_all(copies):
    for copy in copies:
        copy.start()
    return copies


def pack_kernel(winds_hbm, obs_hbm, up, down, winds, obs, sems):
    lons = obs.shape[0]
    copies = fetch_all(
        [
            pltpu.make_async_copy(winds_hbm, winds, sems.at[0]),
            pltpu.make_async_copy(obs_hbm, obs, sems.at[1]),
        ]
    )
    for copy in copies:
        copy.wait()
    up[0:3] = winds[0, lons - 3 :]
    up[3:6] = winds[1, lons - 3 :]
    up[6:8] = obs[lons - 2 :]
    up[8:] = obs[lons - 4 :]
    down[0:4] = winds[0, 0:4]
    down[4:8] = winds[1, 0:4]
    down[8:10] = obs[0:2]


def interior_kernel(
    winds, obs, field_hbm, out, coef, weights, sums, field, sem
):
    count, lons = field.shape[0], field.shape[1]
    blocks = lons // 4 - 2
    field_copy = pltpu.make_async_copy(field_hbm, field, sem)
    field_copy.start()
    lanes = Lanes()

    def coefficients(lon, carry):
        write_coefficients(
            coef,
            lon,
            halves(winds, 0, lon),
            halves(winds, 0, jnp.minimum(lon + 1, lons - 1)),
            halves(winds, 1, lon),
            lanes,
        )
        return carry

    lax.fori_loop(0, lons, coefficients, 0, unroll=4)

    def weigh(block, carry):
        base = (block + 1) * 4

        def get(plane, r):
            return halves(coef, plane, base + r)

        result = block_weights(lanes, get, lambda r: halves(obs, base + r), -4, 7)
        for (r, part), value in result.items():
            store(weights, value, block, part, r + 4)
        return carry

    lax.fori_loop(0, blocks, weigh, 0)
    field_copy.wait()
    keys = [(r, 0) for r in range(-4, 8)]
    keys += [(r, 1) for r in range(-3, 7)]
    keys += [(r, 2) for r in range(-1, 5)]
    groups = count // GROUP

    def sweep(step, carry):
        block = step // groups
        start = (step % groups) * GROUP

        def write(probe, part, h, value):
            row = pl.multiple_of((block * count + probe) * 8, 8)
            sums[2 * part + h, pl.ds(row, 8), :] = value

        apply_weights(
            lanes,
            keys,
            lambda r, part: halves(weights, block, part, r + 4),
            lambda probe, r: halves(field, probe, block * 4 + 4 + r),
            write,
            [start + n for n in range(GROUP)],
        )
        return carry

    lax.fori_loop(0, blocks * groups, sweep, 0)

    def put(n, pair, value):
        column = (n * 4 + pair) * HALF
        out[:, column : column + HALF] = value

    pool_into(lanes, sums, blocks, count, put)


def edge_kernel(
    winds, obs, from_low, from_high, field_hbm,
    to_low, own_low, own_high, to_high,
    coef, weights, sums, field, sems,
):
    count, lons = field_hbm.shape[0], field_hbm.shape[1]
    def fetch(side):
        return pltpu.make_async_copy(
            field_hbm.at[:, pl.ds(side * (lons - 8), 8)],
            field.at[:, pl.ds(8 * side, 8)],
            sems.at[side],
        )

    @pl.loop(0, 2)
    def _(side):
        fetch(side).start()

    lanes = Lanes()

    def near(lon):
        return lon if lon < 8 else lon - (lons - 16)

    def wind(which, lon):
        if lon < 0:
            return halves(from_low, 3 * which + lon + 3)
        if lon >= lons:
            return halves(from_high, 4 * which + lon - lons)
        return halves(winds, which, lon)

    def weight_at(lon):
        if lon < 0:
            return halves(from_low, 6 + lon + 2)
        if lon >= lons:
            return halves(from_high, 8 + lon - lons)
        return halves(obs, lon)

    slots = {}
    for lon in list(range(-3, 8)) + list(range(lons - 8, lons + 4)):
        slots[lon] = len(slots)
        last = lon in (7, lons + 3)
        write_coefficients(
            coef, slots[lon], wind(0, lon), wind(0, lon if last else lon + 1), wind(1, lon), lanes
        )
    jobs = (
        (-4, 4, 7),
        (0, 0, 7),
        (lons - 4, -4, 3),
        (lons, -4, -1),
    )
    kept = []
    for n, (base, first, last) in enumerate(jobs):
        result = block_weights(
            lanes,
            lambda plane, r: halves(coef, plane, slots[base + r]),
            lambda r: weight_at(base + r),
            first,
            last,
        )
        for (r, part), value in result.items():
            store(weights, value, n, part, r + 4)
        kept.append(set(result))

    @pl.loop(0, 2)
    def _(side):
        fetch(side).wait()

    def sweep(n, base, step, carry):
        def write(probe, part, h, value):
            row = pl.multiple_of((n * count + probe) * 8, 8)
            sums[2 * part + h, pl.ds(row, 8), :] = value

        apply_weights(
            lanes,
            kept[n],
            lambda r, part: halves(weights, n, part, r + 4),
            lambda probe, r: halves(field, probe, near(base + r)),
            write,
            [step * GROUP + k for k in range(GROUP)],
        )
        return carry

    for n, (base, _, _) in enumerate(jobs):
        lax.fori_loop(0, count // GROUP, functools.partial(sweep, n, base), 0)
    outs = (to_low, own_low, own_high, to_high)

    def put(n, pair, value):
        outs[n][:, pair * HALF : (pair + 1) * HALF] = value

    pool_into(lanes, sums, 4, count, put)


def self_product(panel):
    return lax.dot_general(
        panel,
        panel,
        (((1,), (1,)), ((), ())),
        precision=lax.Precision.HIGHEST,
        preferred_element_type=F32,
    )


def assemble(where, pieces, panel):
    rows = pieces[0].shape[0]
    for k, piece in enumerate(pieces):
        at = pl.multiple_of(lax.bitwise_xor(where[0], jnp.int32(k)) * rows, 8)
        panel[pl.ds(at, rows)] = piece[...]


def inner_gram_kernel(where, *refs):
    pieces, (panel, out) = refs[:-2], refs[-2:]
    assemble(where, pieces, panel)
    out[...] = self_product(panel[...])


def gram_kernel(where, inner, *refs):
    pieces, (panel, out) = refs[:-2], refs[-2:]
    assemble(where, pieces, panel)
    gram = self_product(panel[...]) + inner[...]
    half = gram.shape[0] // 2
    packed = jnp.concatenate([gram[:half], gram[half:]], axis=1)
    for n in range(out.shape[0]):
        out[n] = packed


def factor_kernel(where, grams, inner, edge, basis, upper, inverse):
    packed = grams[0]
    for n in range(1, grams.shape[0]):
        packed = packed + grams[n]
    size = 2 * packed.shape[0]
    gram = jnp.concatenate([packed[:, :size], packed[:, size:]], axis=0)
    row = lax.broadcasted_iota(jnp.int32, (size, size), 0)
    column = lax.broadcasted_iota(jnp.int32, (size, size), 1)
    state = jnp.concatenate([gram, jnp.where(row == column, 1.0, 0.0).astype(F32)], axis=1)
    tiles = [state[8 * t : 8 * t + 8] for t in range(size // 8)]
    full = (8, 2 * size)
    sub = lax.broadcasted_iota(jnp.int32, full, 0)
    scales = []
    for own in range(size // 8):
        spread = {
            (t, j): jnp.broadcast_to(tiles[t][:, 8 * own + j : 8 * own + j + 1], full)
            for t in range(own, size // 8)
            for j in range(8)
        }
        pivots = {
            (i, j): jnp.broadcast_to(spread[own, j][i : i + 1], full)
            for i in range(8)
            for j in range(i + 1)
        }
        rows = [jnp.broadcast_to(tiles[own][j : j + 1], full) for j in range(8)]
        inverses = []
        for j in range(8):
            inverses.append(1.0 / pivots[j, j])
            scales.append(lax.rsqrt(pivots[j, j]))
            for i in range(j + 1, 8):
                ratio = pivots[i, j] * inverses[j]
                for m in range(i, 8):
                    pivots[m, i] = pivots[m, i] - ratio * pivots[m, j]
                rows[i] = rows[i] - ratio * rows[j]
                for t in range(own + 1, size // 8):
                    spread[t, i] = spread[t, i] - ratio * spread[t, j]
        for t in range(own + 1, size // 8):
            update = (spread[t, 0] * inverses[0]) * rows[0]
            for j in range(1, 8):
                update = update + (spread[t, j] * inverses[j]) * rows[j]
            tiles[t] = tiles[t] - update
        for j in range(8):
            tiles[own] = jnp.where(sub == j, rows[j], tiles[own])
    for t in range(size // 8):
        scale = scales[8 * t]
        for at in range(1, 8):
            scale = jnp.where(sub == at, scales[8 * t + at], scale)
        scaled = tiles[t] * scale
        column = lax.broadcasted_iota(jnp.int32, (8, size), 1)
        here = lax.broadcasted_iota(jnp.int32, (8, size), 0) + 8 * t
        upper[8 * t : 8 * t + 8] = jnp.where(column >= here, scaled[:, :size], 0.0)
        inverse[8 * t : 8 * t + 8] = scaled[:, size:]
    blocks, count, width = basis.shape
    own_rows = inverse[pl.ds(pl.multiple_of(where[0] * count, 8), count)]

    def project(columns):
        return jnp.dot(
            own_rows, columns, precision=lax.Precision.HIGHEST, preferred_element_type=F32
        )

    basis[0] = project(edge[:, :width])
    for n in range(blocks - 2):
        basis[n + 1] = project(inner[:, n * width : (n + 1) * width])
    basis[blocks - 1] = project(edge[:, width:])


VMEM = pl.BlockSpec(memory_space=pltpu.VMEM)
SMEM = pl.BlockSpec(memory_space=pltpu.SMEM)
HBM = pl.BlockSpec(memory_space=pltpu.HBM)
MIB = 1024 * 1024


def shape(*dims):
    return jax.ShapeDtypeStruct(dims, F32)


def call(kernel, name, out_shape, in_specs, scratch=(), flops=0):
    return pl.pallas_call(
        kernel,
        out_shape=out_shape,
        in_specs=in_specs,
        out_specs=jax.tree.map(lambda _: VMEM, out_shape),
        scratch_shapes=scratch,
        compiler_params=pltpu.CompilerParams(vmem_limit_bytes=32 * MIB),
        cost_estimate=pl.CostEstimate(flops=flops, bytes_accessed=4_000_000, transcendentals=0),
        name=name,
    )


def gather_pieces(rows):
    size = lax.axis_size("probe")
    pieces = [rows]
    for k in range(1, size):
        source, step = (pieces[k - 1], 1) if k > 1 and k & 1 else (rows, k)
        pieces.append(lax.ppermute(source, "probe", [(i, i ^ step) for i in range(size)]))
    return pieces


def body(increments, winds, obs_weight):
    count, lons, levels, lats = increments.shape
    blocks = lons // 4
    probes = count * lax.axis_size("probe")
    ring = lax.axis_size("lon")
    up = [(i, (i + 1) % ring) for i in range(ring)]
    down = [(i, (i - 1) % ring) for i in range(ring)]
    where = lax.axis_index("probe").reshape(1).astype(jnp.int32)
    dma = pltpu.SemaphoreType.DMA
    increments, winds, obs_weight = (
        pltpu.with_memory_space_constraint(x, pltpu.HBM) for x in (increments, winds, obs_weight)
    )
    pack_up, pack_down, winds, obs_weight = call(
        pack_kernel,
        "pack",
        (
            shape(12, levels, lats),
            shape(10, levels, lats),
            shape(2, lons, levels, lats),
            shape(lons, levels, lats),
        ),
        [HBM, HBM],
        [dma((2,))],
    )(winds, obs_weight)
    from_low = lax.ppermute(pack_up, "lon", up)
    from_high = lax.ppermute(pack_down, "lon", down)
    inner = call(
        interior_kernel,
        "interior",
        shape(count, (blocks - 2) * 512),
        [VMEM, VMEM, HBM],
        [
            pltpu.VMEM((PLANES, lons, levels, lats), F32),
            pltpu.VMEM((blocks - 2, 3, 12, levels, lats), F32),
            pltpu.VMEM((6, (blocks - 2) * count * 8, HALF), F32),
            pltpu.VMEM((count, lons, levels, lats), F32),
            dma,
        ],
        200_000_000,
    )(winds, obs_weight, increments)
    inner, from_low, from_high = lax.optimization_barrier((inner, from_low, from_high))
    inner_pieces = gather_pieces(inner)
    edges = call(
        edge_kernel,
        "edges",
        (shape(count, 512),) * 4,
        [VMEM, VMEM, VMEM, VMEM, HBM],
        [
            pltpu.VMEM((PLANES, 23, levels, lats), F32),
            pltpu.VMEM((4, 3, 12, levels, lats), F32),
            pltpu.VMEM((6, 4 * count * 8, HALF), F32),
            pltpu.VMEM((count, 16, levels, lats), F32),
            dma((2,)),
        ],
        100_000_000,
    )(winds, obs_weight, from_low, from_high, increments)
    to_low, own_low, own_high, to_high = edges
    own_low = own_low + lax.ppermute(to_high, "lon", up)
    own_high = own_high + lax.ppermute(to_low, "lon", down)
    edge_pieces = gather_pieces(jnp.concatenate([own_low, own_high], axis=1))
    inner_panel, inner_gram = call(
        inner_gram_kernel,
        "inner_gram",
        (shape(probes, inner.shape[1]), shape(probes, probes)),
        [SMEM] + [VMEM] * len(inner_pieces),
        (),
        25_000_000,
    )(where, *inner_pieces)
    edge_panel, grams = call(
        gram_kernel,
        "gram",
        (shape(probes, 1024), shape(ring, probes // 2, 2 * probes)),
        [SMEM, VMEM] + [VMEM] * len(edge_pieces),
        (),
        10_000_000,
    )(where, inner_gram, *edge_pieces)
    grams = lax.all_to_all(grams, "lon", 0, 0, tiled=True)
    basis, upper = call(
        factor_kernel,
        "factor",
        (shape(blocks, count, 512), shape(probes, probes)),
        [SMEM, VMEM, VMEM, VMEM],
        [pltpu.VMEM((probes, probes), F32)],
        10_000_000,
    )(where, grams, inner_panel, edge_panel)
    return basis.transpose(1, 0, 2), upper


def solution(mesh):
    in_specs = (P("probe", "lon", None, None), P(None, "lon", None, None), P("lon", None, None))
    out_specs = (P("probe", "lon", None), P())
    return jax.shard_map(body, mesh=mesh, in_specs=in_specs, out_specs=out_specs, check_vma=False)
```

```python
import functools

import jax
import jax.numpy as jnp
from jax import lax
from jax.experimental import pallas as pl
from jax.experimental.pallas import tpu as pltpu
from jax.sharding import PartitionSpec as P

F32 = jnp.float32
BF16 = jnp.bfloat16
HALF = 128
DIAG, EAST, WEST, SOUTH_UP, SOUTH_DOWN, NORTH_UP, NORTH_DOWN = range(7)
PLANES = 7


def halves(ref, *index):
    return [ref[index + (slice(None), slice(h * HALF, (h + 1) * HALF))] for h in (0, 1)]


def store(ref, value, *index):
    for h in (0, 1):
        ref[index + (slice(None), slice(h * HALF, (h + 1) * HALF))] = value[h]


class Lanes:
    def __init__(self):
        lane = lax.broadcasted_iota(jnp.int32, (8, HALF), 1)
        self.first = lane == 0
        self.last = lane == HALF - 1
        self.phase = lane & 3
        self.even = ((lane >> 2) & 1) == 0
        self.third = [lax.rem((lane + h * HALF) >> 2, 3) for h in (0, 1)]
        low = self.phase < 2
        self.near = [lax.rem(t + jnp.where(low, 2, 1), 3) for t in self.third]
        self.far = [lax.rem(t + jnp.where(low, 1, 2), 3) for t in self.third]

    def below(self, f):
        r0, r1 = pltpu.roll(f[0], 1, 1), pltpu.roll(f[1], 1, 1)
        return [r0, jnp.where(self.first, r0, r1)]

    def above(self, f):
        r0, r1 = pltpu.roll(f[0], HALF - 1, 1), pltpu.roll(f[1], HALF - 1, 1)
        return [jnp.where(self.last, r1, r0), r1]


def write_coefficients(coef, slot, u, u_next, v, lanes):
    v = [jnp.where(lanes.first, 0.0, v[0]), v[1]]
    south_up = [jnp.maximum(x, 0.0) for x in v]
    south_down = [jnp.maximum(-x, 0.0) for x in v]
    north = []
    for field in (south_up, south_down):
        r0, r1 = pltpu.roll(field[0], HALF - 1, 1), pltpu.roll(field[1], HALF - 1, 1)
        north.append([jnp.where(lanes.last, r1, r0), jnp.where(lanes.last, r0, r1)])
    east = [jnp.maximum(x, 0.0) for x in u]
    west = [jnp.maximum(-x, 0.0) for x in u]
    diag = [
        1.0 - jnp.maximum(u_next[h], 0.0) - west[h] - north[0][h] - south_down[h] for h in (0, 1)
    ]
    for plane, value in (
        (DIAG, diag),
        (EAST, east),
        (WEST, west),
        (SOUTH_UP, south_up),
        (SOUTH_DOWN, south_down),
        (NORTH_UP, north[0]),
        (NORTH_DOWN, north[1]),
    ):
        store(coef, value, plane, slot)


def stencil(lanes, field, r, get, forward):
    total = [None, None]

    def add(coefficient, value):
        for h in (0, 1):
            term = coefficient[h] * value[h]
            total[h] = term if total[h] is None else total[h] + term

    if r in field:
        here = field[r]
        add(get(DIAG, r), here)
        add(get(SOUTH_UP if forward else SOUTH_DOWN, r), lanes.below(here))
        add(get(NORTH_DOWN if forward else NORTH_UP, r), lanes.above(here))
    if r - 1 in field:
        add(get(EAST if forward else WEST, r), field[r - 1])
    if r + 1 in field:
        add(get(WEST if forward else EAST, r + 1), field[r + 1])
    return total


def block_weights(lanes, get, get_obs, first, last):
    state = [{}, {}]
    for r in range(max(first - 3, -1), min(last + 3, 4) + 1):
        if r == -1:
            own = get(WEST, 0)
            other = None
        elif r == 4:
            own = get(EAST, 4)
            other = None
        else:
            own = get(DIAG, r)
            if r > 0:
                own = [x + y for x, y in zip(own, get(EAST, r))]
            if r < 3:
                own = [x + y for x, y in zip(own, get(WEST, r + 1))]
            south, north = get(SOUTH_UP, r), get(NORTH_DOWN, r)
            inner_south = [jnp.where(lanes.phase == 0, 0.0, x) for x in south]
            inner_north = [jnp.where(lanes.phase == 3, 0.0, x) for x in north]
            own = [x + y + z for x, y, z in zip(own, inner_south, inner_north)]
            other = [
                jnp.where(lanes.phase == 0, x, jnp.where(lanes.phase == 3, y, 0.0))
                for x, y in zip(south, north)
            ]
        for colour in (0, 1):
            mine = lanes.even if colour == 0 else jnp.logical_not(lanes.even)
            state[colour][r] = [
                jnp.where(mine, own[h], 0.0 if other is None else other[h]) for h in (0, 1)
            ]
    wide = [{}, {}, {}]
    for r in range(max(first - 2, -2), min(last + 2, 5) + 1):
        obs = get_obs(r)
        pair = [stencil(lanes, state[colour], r, get, True) for colour in (0, 1)]
        pair = [[obs[h] * value[h] for h in (0, 1)] for value in pair]
        own = [jnp.where(lanes.even, pair[0][h], pair[1][h]) for h in (0, 1)]
        other = [jnp.where(lanes.even, pair[1][h], pair[0][h]) for h in (0, 1)]
        for colour in range(3):
            wide[colour][r] = [
                jnp.where(
                    lanes.third[h] == colour,
                    own[h],
                    jnp.where(lanes.near[h] == colour, other[h], 0.0),
                )
                for h in (0, 1)
            ]
    once = [
        {
            r: stencil(lanes, wide[colour], r, get, False)
            for r in range(max(first - 1, -3), min(last + 1, 6) + 1)
        }
        for colour in range(3)
    ]
    weights = {}
    for r in range(first, last + 1):
        twice = [stencil(lanes, once[colour], r, get, False) for colour in range(3)]

        def pick(index):
            return [
                jnp.where(
                    index[h] == 0, twice[0][h], jnp.where(index[h] == 1, twice[1][h], twice[2][h])
                )
                for h in (0, 1)
            ]

        own = pick(lanes.third)
        if 0 <= r <= 3:
            own = [x + 1.0 for x in own]
        weights[r, 0] = own
        if -3 <= r <= 6:
            weights[r, 1] = pick(lanes.near)
        if -1 <= r <= 4:
            weights[r, 2] = pick(lanes.far)
    return weights


def apply_weights(lanes, keys, read_weight, read_field, write, probes):
    sums = {}
    for r in sorted({r for r, _ in keys}):
        fields = [read_field(probe, r) for probe in probes]
        for part in range(3):
            if (r, part) not in keys:
                continue
            weight = read_weight(r, part)
            for n in range(len(probes)):
                for h in (0, 1):
                    term = weight[h] * fields[n][h]
                    key = (n, part, h)
                    sums[key] = sums[key] + term if key in sums else term
    low = lanes.phase < 2
    for n, probe in enumerate(probes):
        own, near, far = ([sums.get((n, part, h)) for h in (0, 1)] for part in range(3))
        if far[0] is None:
            down = [jnp.where(low, x, 0.0) for x in near]
            up = [jnp.where(low, 0.0, x) for x in near]
        else:
            down = [jnp.where(low, x, y) for x, y in zip(near, far)]
            up = [jnp.where(low, y, x) for x, y in zip(near, far)]
        for h in (0, 1):
            write(probe, 0, h, own[h])
            write(probe, 1, h, down[h])
            write(probe, 2, h, up[h])


def pooling(parity):
    row = lax.broadcasted_iota(jnp.int32, (256, HALF), 0)
    column = lax.broadcasted_iota(jnp.int32, (256, HALF), 1)
    return jnp.where((row >> 2) + 64 * parity == column, 1.0 / 16.0, 0.0).astype(BF16)


def split3(x):
    high = x.astype(BF16)
    rest = x - high.astype(F32)
    middle = rest.astype(BF16)
    low = (rest - middle.astype(F32)).astype(BF16)
    return high, middle, low


def pool_into(lanes, sums, rows, count, write):
    total = None
    for parity in (0, 1):
        matrix = pooling(parity)
        own, down, up = (
            [
                jnp.concatenate(
                    [
                        sums[2 * part + h, pl.ds(n * count * 8 + 2 * pair + parity, count, stride=8), :]
                        for n in range(rows)
                        for pair in range(4)
                    ],
                    axis=0,
                )
                for h in (0, 1)
            ]
            for part in range(3)
        )
        lane = lax.broadcasted_iota(jnp.int32, own[0].shape, 1)
        d0, d1 = (pltpu.roll(x, HALF - 4, 1) for x in down)
        u0, u1 = (pltpu.roll(x, 4, 1) for x in up)
        low = own[0] + (jnp.where(lane >= HALF - 4, d1, d0) + jnp.where(lane < 4, u1, u0))
        high = own[1] + (jnp.where(lane >= HALF - 4, d0, d1) + jnp.where(lane < 4, u0, u1))
        for part in split3(jnp.concatenate([low, high], axis=1)):
            term = jnp.dot(part, matrix, preferred_element_type=F32)
            total = term if total is None else total + term
    for n in range(rows):
        for pair in range(4):
            start = (n * 4 + pair) * count
            write(n, pair, total[start : start + count])


GROUP = 8


def weight_keys(first, last):
    reach = {0: (-4, 7), 1: (-3, 6), 2: (-1, 4)}
    return [
        (r, part)
        for part, (low, high) in reach.items()
        for r in range(max(first, low), min(last, high) + 1)
    ]


def fetch_all(copies):
    for copy in copies:
        copy.start()
    return copies


def pack_kernel(winds_hbm, obs_hbm, up, down, winds, obs, sems):
    lons = obs.shape[0]
    copies = fetch_all(
        [
            pltpu.make_async_copy(winds_hbm, winds, sems.at[0]),
            pltpu.make_async_copy(obs_hbm, obs, sems.at[1]),
        ]
    )
    for copy in copies:
        copy.wait()
    up[0:3] = winds[0, lons - 3 :]
    up[3:6] = winds[1, lons - 3 :]
    up[6:8] = obs[lons - 2 :]
    up[8:] = obs[lons - 4 :]
    down[0:4] = winds[0, 0:4]
    down[4:8] = winds[1, 0:4]
    down[8:10] = obs[0:2]


def interior_kernel(
    winds, obs, field_hbm, out, part_low, part_high, sides, coef, weights, sums, field, sems
):
    count, lons = field.shape[0], field.shape[1]
    blocks = lons // 4
    field_copy = pltpu.make_async_copy(field_hbm, field, sems.at[0])
    field_copy.start()
    side_copies = [
        pltpu.make_async_copy(
            field_hbm.at[:, pl.ds(start, 4)], sides.at[:, pl.ds(4 * n, 4)], sems.at[1 + n]
        )
        for n, start in enumerate((0, lons - 4))
    ]
    for copy in side_copies:
        copy.start()
    lanes = Lanes()

    def coefficients(lon, carry):
        write_coefficients(
            coef,
            lon,
            halves(winds, 0, lon),
            halves(winds, 0, jnp.minimum(lon + 1, lons - 1)),
            halves(winds, 1, lon),
            lanes,
        )
        return carry

    lax.fori_loop(0, lons, coefficients, 0, unroll=4)

    def weigh(first, last, block, carry):
        base = block * 4

        def get(plane, r):
            return halves(coef, plane, base + r)

        result = block_weights(lanes, get, lambda r: halves(obs, base + r), first, last)
        for (r, part), value in result.items():
            store(weights, value, block, part, r + 4)
        return carry

    spans = ((0, 1, 2, 7), (1, blocks - 1, -4, 7), (blocks - 1, blocks, -4, -1))
    for start, stop, first, last in spans:
        lax.fori_loop(start, stop, functools.partial(weigh, first, last), 0)
    field_copy.wait()
    groups = count // GROUP

    def sweep(first, last, step, carry):
        block = step // groups
        start = (step % groups) * GROUP

        def write(probe, part, h, value):
            row = pl.multiple_of((block * count + probe) * 8, 8)
            sums[2 * part + h, pl.ds(row, 8), :] = value

        apply_weights(
            lanes,
            weight_keys(first, last),
            lambda r, part: halves(weights, block, part, r + 4),
            lambda probe, r: halves(field, probe, block * 4 + r),
            write,
            [start + n for n in range(GROUP)],
        )
        return carry

    for start, stop, first, last in spans:
        lax.fori_loop(start * groups, stop * groups, functools.partial(sweep, first, last), 0)

    def put(n, pair, value):
        if n == 0:
            part_low[:, pair * HALF : (pair + 1) * HALF] = value
        elif n == blocks - 1:
            part_high[:, pair * HALF : (pair + 1) * HALF] = value
        else:
            column = ((n - 1) * 4 + pair) * HALF
            out[:, column : column + HALF] = value

    pool_into(lanes, sums, blocks, count, put)
    for copy in side_copies:
        copy.wait()


def edge_sums(winds, obs, from_low, from_high, field, coef, weights, sums, spans, jobs, put):
    count, lons = field.shape[0], obs.shape[0]
    lanes = Lanes()

    def wind(which, lon):
        if lon < 0:
            return halves(from_low, 3 * which + lon + 3)
        if lon >= lons:
            return halves(from_high, 4 * which + lon - lons)
        return halves(winds, which, lon)

    def weight_at(lon):
        if lon < 0:
            return halves(from_low, 6 + lon + 2)
        if lon >= lons:
            return halves(from_high, 8 + lon - lons)
        return halves(obs, lon)

    slots = {}
    for start, stop in spans:
        for lon in range(start, stop + 1):
            slots[lon] = len(slots)
            write_coefficients(
                coef, slots[lon], wind(0, lon), wind(0, min(lon + 1, stop)), wind(1, lon), lanes
            )
    for n, (base, first, last) in enumerate(jobs):
        result = block_weights(
            lanes,
            lambda plane, r: halves(coef, plane, slots[base + r]),
            lambda r: weight_at(base + r),
            first,
            last,
        )
        for (r, part), value in result.items():
            store(weights, value, n, part, r + 4)

    def sweep(step, carry):
        for n, (base, first, last) in enumerate(jobs):

            def write(probe, part, h, value):
                row = pl.multiple_of((n * count + probe) * 8, 8)
                sums[2 * part + h, pl.ds(row, 8), :] = value

            def read(probe, r):
                lon = base + r
                return halves(field, probe, lon if lon < 4 else lon - (lons - 8))

            apply_weights(
                lanes,
                weight_keys(first, last),
                lambda r, part: halves(weights, n, part, r + 4),
                read,
                write,
                [step * GROUP + k for k in range(GROUP)],
            )
        return carry

    lax.fori_loop(0, count // GROUP, sweep, 0)
    pool_into(lanes, sums, len(jobs), count, put)


def share_kernel(winds, obs, from_low, from_high, field, to_low, to_high, coef, weights, sums):
    lons = obs.shape[0]

    def put(n, pair, value):
        (to_low, to_high)[n][:, pair * HALF : (pair + 1) * HALF] = value

    edge_sums(
        winds, obs, from_low, from_high, field, coef, weights, sums,
        ((-3, 3), (lons - 3, lons + 3)),
        ((-4, 4, 7), (lons, -4, -1)),
        put,
    )


def rest_kernel(
    winds, obs, from_low, from_high, field, part_low, part_high, after,
    own_low, own_high, coef, weights, sums,
):
    lons = obs.shape[0]

    def put(n, pair, value):
        columns = slice(pair * HALF, (pair + 1) * HALF)
        (own_low, own_high)[n][:, columns] = value + (part_low, part_high)[n][:, columns]

    edge_sums(
        winds, obs, from_low, from_high, field, coef, weights, sums,
        ((-2, 4), (lons - 5, lons + 1)),
        ((0, 0, 1), (lons - 4, 0, 3)),
        put,
    )


def self_product(panel):
    return lax.dot_general(
        panel,
        panel,
        (((1,), (1,)), ((), ())),
        precision=lax.Precision.HIGHEST,
        preferred_element_type=F32,
    )


def assemble(where, pieces, panel):
    rows = pieces[0].shape[0]
    for k, piece in enumerate(pieces):
        at = pl.multiple_of(lax.bitwise_xor(where[0], jnp.int32(k)) * rows, 8)
        panel[pl.ds(at, rows)] = piece[...]


def inner_gram_kernel(where, *refs):
    pieces, (panel, out) = refs[:-2], refs[-2:]
    assemble(where, pieces, panel)
    out[...] = self_product(panel[...])


def gram_kernel(where, inner, *refs):
    pieces, (panel, out) = refs[:-2], refs[-2:]
    assemble(where, pieces, panel)
    gram = self_product(panel[...]) + inner[...]
    half = gram.shape[0] // 2
    packed = jnp.concatenate([gram[:half], gram[half:]], axis=1)
    for n in range(out.shape[0]):
        out[n] = packed


def factor_kernel(where, grams, inner, edge, basis, upper, inverse):
    packed = grams[0]
    for n in range(1, grams.shape[0]):
        packed = packed + grams[n]
    size = 2 * packed.shape[0]
    gram = jnp.concatenate([packed[:, :size], packed[:, size:]], axis=0)
    row = lax.broadcasted_iota(jnp.int32, (size, size), 0)
    column = lax.broadcasted_iota(jnp.int32, (size, size), 1)
    state = jnp.concatenate([gram, jnp.where(row == column, 1.0, 0.0).astype(F32)], axis=1)
    tiles = [state[8 * t : 8 * t + 8] for t in range(size // 8)]
    full = (8, 2 * size)
    sub = lax.broadcasted_iota(jnp.int32, full, 0)
    scales = []
    for own in range(size // 8):
        spread = {
            (t, j): jnp.broadcast_to(tiles[t][:, 8 * own + j : 8 * own + j + 1], full)
            for t in range(own, size // 8)
            for j in range(8)
        }
        pivots = {
            (i, j): jnp.broadcast_to(spread[own, j][i : i + 1], full)
            for i in range(8)
            for j in range(i + 1)
        }
        rows = [jnp.broadcast_to(tiles[own][j : j + 1], full) for j in range(8)]
        inverses = []
        for j in range(8):
            inverses.append(1.0 / pivots[j, j])
            scales.append(lax.rsqrt(pivots[j, j]))
            for i in range(j + 1, 8):
                ratio = pivots[i, j] * inverses[j]
                for m in range(i, 8):
                    pivots[m, i] = pivots[m, i] - ratio * pivots[m, j]
                rows[i] = rows[i] - ratio * rows[j]
                for t in range(own + 1, size // 8):
                    spread[t, i] = spread[t, i] - ratio * spread[t, j]
        for t in range(own + 1, size // 8):
            update = (spread[t, 0] * inverses[0]) * rows[0]
            for j in range(1, 8):
                update = update + (spread[t, j] * inverses[j]) * rows[j]
            tiles[t] = tiles[t] - update
        for j in range(8):
            tiles[own] = jnp.where(sub == j, rows[j], tiles[own])
    for t in range(size // 8):
        scale = scales[8 * t]
        for at in range(1, 8):
            scale = jnp.where(sub == at, scales[8 * t + at], scale)
        scaled = tiles[t] * scale
        column = lax.broadcasted_iota(jnp.int32, (8, size), 1)
        here = lax.broadcasted_iota(jnp.int32, (8, size), 0) + 8 * t
        upper[8 * t : 8 * t + 8] = jnp.where(column >= here, scaled[:, :size], 0.0)
        inverse[8 * t : 8 * t + 8] = scaled[:, size:]
    blocks, count, width = basis.shape
    own_rows = inverse[pl.ds(pl.multiple_of(where[0] * count, 8), count)]

    def project(columns):
        return jnp.dot(
            own_rows, columns, precision=lax.Precision.HIGHEST, preferred_element_type=F32
        )

    basis[0] = project(edge[:, :width])
    for n in range(blocks - 2):
        basis[n + 1] = project(inner[:, n * width : (n + 1) * width])
    basis[blocks - 1] = project(edge[:, width:])


VMEM = pl.BlockSpec(memory_space=pltpu.VMEM)
SMEM = pl.BlockSpec(memory_space=pltpu.SMEM)
HBM = pl.BlockSpec(memory_space=pltpu.HBM)
ANY = pl.BlockSpec(memory_space=pl.ANY)
MIB = 1024 * 1024
COST = 1_000_000


def shape(*dims):
    return jax.ShapeDtypeStruct(dims, F32)


def call(kernel, name, out_shape, in_specs, scratch=(), flops=1_000_000):
    return pl.pallas_call(
        kernel,
        out_shape=out_shape,
        in_specs=in_specs,
        out_specs=jax.tree.map(lambda _: VMEM, out_shape),
        scratch_shapes=scratch,
        compiler_params=pltpu.CompilerParams(vmem_limit_bytes=32 * MIB),
        cost_estimate=pl.CostEstimate(flops=flops, bytes_accessed=100_000, transcendentals=0),
        name=name,
    )


def swap_probes(value, step):
    return lax.ppermute(value, "probe", [(i, i ^ step) for i in range(lax.axis_size("probe"))])


def body(increments, winds, obs_weight):
    count, lons, levels, lats = increments.shape
    blocks = lons // 4
    probes = count * lax.axis_size("probe")
    ring = lax.axis_size("lon")
    up = [(i, (i + 1) % ring) for i in range(ring)]
    down = [(i, (i - 1) % ring) for i in range(ring)]
    where = lax.axis_index("probe").reshape(1).astype(jnp.int32)
    dma = pltpu.SemaphoreType.DMA
    increments, winds, obs_weight = (
        pltpu.with_memory_space_constraint(x, pltpu.HBM) for x in (increments, winds, obs_weight)
    )
    pack_up, pack_down, winds, obs_weight = call(
        pack_kernel,
        "pack",
        (
            shape(12, levels, lats),
            shape(10, levels, lats),
            shape(2, lons, levels, lats),
            shape(lons, levels, lats),
        ),
        [HBM, HBM],
        [dma((2,))],
    )(winds, obs_weight)
    from_low = lax.ppermute(pack_up, "lon", up)
    from_high = lax.ppermute(pack_down, "lon", down)
    inner, part_low, part_high, sides = call(
        interior_kernel,
        "interior",
        (
            shape(count, (blocks - 2) * 512),
            shape(count, 512),
            shape(count, 512),
            shape(count, 8, levels, lats),
        ),
        [VMEM, VMEM, HBM],
        [
            pltpu.VMEM((PLANES, lons, levels, lats), F32),
            pltpu.VMEM((blocks, 3, 12, levels, lats), F32),
            pltpu.VMEM((6, blocks * count * 8, HALF), F32),
            pltpu.VMEM((count, lons, levels, lats), F32),
            dma((3,)),
        ],
        COST,
    )(winds, obs_weight, increments)
    edge_scratch = [
        pltpu.VMEM((PLANES, 14, levels, lats), F32),
        pltpu.VMEM((2, 3, 12, levels, lats), F32),
        pltpu.VMEM((6, 2 * count * 8, HALF), F32),
    ]
    to_low, to_high = call(
        share_kernel, "share", (shape(count, 512),) * 2, [VMEM] * 5, edge_scratch
    )(winds, obs_weight, from_low, from_high, sides)
    own_low, own_high = call(
        rest_kernel, "rest", (shape(count, 512),) * 2, [VMEM] * 7 + [ANY], edge_scratch
    )(winds, obs_weight, from_low, from_high, sides, part_low, part_high, to_low)
    from_below = lax.ppermute(to_high, "lon", up)
    from_above = lax.ppermute(to_low, "lon", down)
    inner, own_low = lax.optimization_barrier((inner, own_low))
    size = lax.axis_size("probe")
    inner_pieces = [inner] + [swap_probes(inner, k) for k in range(1, size) if k & (k - 1) == 0]
    edge = jnp.concatenate([own_low + from_below, own_high + from_above], axis=1)
    edge_pieces = [edge] + [swap_probes(edge, k) for k in range(1, size) if k & (k - 1) == 0]
    inner_pieces, edge_pieces = lax.optimization_barrier((inner_pieces, edge_pieces))
    inner_pieces.append(swap_probes(inner_pieces[2], 1))
    edge_pieces.append(swap_probes(edge_pieces[2], 1))
    inner_panel, inner_gram = call(
        inner_gram_kernel,
        "inner_gram",
        (shape(probes, inner.shape[1]), shape(probes, probes)),
        [SMEM] + [VMEM] * len(inner_pieces),
        (),
        COST,
    )(where, *inner_pieces)
    edge_panel, grams = call(
        gram_kernel,
        "gram",
        (shape(probes, 1024), shape(ring, probes // 2, 2 * probes)),
        [SMEM, VMEM] + [VMEM] * len(edge_pieces),
        (),
        COST,
    )(where, inner_gram, *edge_pieces)
    grams = lax.all_to_all(grams, "lon", 0, 0, tiled=True)
    basis, upper = call(
        factor_kernel,
        "factor",
        (shape(blocks, count, 512), shape(probes, probes)),
        [SMEM, VMEM, VMEM, VMEM],
        [pltpu.VMEM((probes, probes), F32)],
        COST,
    )(where, grams, inner_panel, edge_panel)
    return basis.transpose(1, 0, 2), upper


def solution(mesh):
    in_specs = (P("probe", "lon", None, None), P(None, "lon", None, None), P("lon", None, None))
    out_specs = (P("probe", "lon", None), P())
    return jax.shard_map(body, mesh=mesh, in_specs=in_specs, out_specs=out_specs, check_vma=False)
```

```python
import functools

import jax
import jax.numpy as jnp
from jax import lax
from jax.experimental import pallas as pl
from jax.experimental.pallas import tpu as pltpu
from jax.sharding import PartitionSpec as P

F32 = jnp.float32
BF16 = jnp.bfloat16
HALF = 128
DIAG, EAST, WEST, SOUTH_UP, SOUTH_DOWN, NORTH_UP, NORTH_DOWN = range(7)
PLANES = 7


def halves(ref, *index):
    return [ref[index + (slice(None), slice(h * HALF, (h + 1) * HALF))] for h in (0, 1)]


def store(ref, value, *index):
    for h in (0, 1):
        ref[index + (slice(None), slice(h * HALF, (h + 1) * HALF))] = value[h]


class Lanes:
    def __init__(self):
        lane = lax.broadcasted_iota(jnp.int32, (8, HALF), 1)
        self.first = lane == 0
        self.last = lane == HALF - 1
        self.phase = lane & 3
        self.even = ((lane >> 2) & 1) == 0
        self.third = [lax.rem((lane + h * HALF) >> 2, 3) for h in (0, 1)]
        low = self.phase < 2
        self.near = [lax.rem(t + jnp.where(low, 2, 1), 3) for t in self.third]
        self.far = [lax.rem(t + jnp.where(low, 1, 2), 3) for t in self.third]

    def below(self, f):
        r0, r1 = pltpu.roll(f[0], 1, 1), pltpu.roll(f[1], 1, 1)
        return [r0, jnp.where(self.first, r0, r1)]

    def above(self, f):
        r0, r1 = pltpu.roll(f[0], HALF - 1, 1), pltpu.roll(f[1], HALF - 1, 1)
        return [jnp.where(self.last, r1, r0), r1]


def write_coefficients(coef, slot, u, u_next, v, lanes):
    v = [jnp.where(lanes.first, 0.0, v[0]), v[1]]
    south_up = [jnp.maximum(x, 0.0) for x in v]
    south_down = [jnp.maximum(-x, 0.0) for x in v]
    north = []
    for field in (south_up, south_down):
        r0, r1 = pltpu.roll(field[0], HALF - 1, 1), pltpu.roll(field[1], HALF - 1, 1)
        north.append([jnp.where(lanes.last, r1, r0), jnp.where(lanes.last, r0, r1)])
    east = [jnp.maximum(x, 0.0) for x in u]
    west = [jnp.maximum(-x, 0.0) for x in u]
    diag = [
        1.0 - jnp.maximum(u_next[h], 0.0) - west[h] - north[0][h] - south_down[h] for h in (0, 1)
    ]
    for plane, value in (
        (DIAG, diag),
        (EAST, east),
        (WEST, west),
        (SOUTH_UP, south_up),
        (SOUTH_DOWN, south_down),
        (NORTH_UP, north[0]),
        (NORTH_DOWN, north[1]),
    ):
        store(coef, value, plane, slot)


def stencil(lanes, field, r, get, forward):
    total = [None, None]

    def add(coefficient, value):
        for h in (0, 1):
            term = coefficient[h] * value[h]
            total[h] = term if total[h] is None else total[h] + term

    if r in field:
        here = field[r]
        add(get(DIAG, r), here)
        add(get(SOUTH_UP if forward else SOUTH_DOWN, r), lanes.below(here))
        add(get(NORTH_DOWN if forward else NORTH_UP, r), lanes.above(here))
    if r - 1 in field:
        add(get(EAST if forward else WEST, r), field[r - 1])
    if r + 1 in field:
        add(get(WEST if forward else EAST, r + 1), field[r + 1])
    return total


def block_weights(lanes, get, get_obs, first, last):
    state = [{}, {}]
    for r in range(max(first - 3, -1), min(last + 3, 4) + 1):
        if r == -1:
            own = get(WEST, 0)
            other = None
        elif r == 4:
            own = get(EAST, 4)
            other = None
        else:
            own = get(DIAG, r)
            if r > 0:
                own = [x + y for x, y in zip(own, get(EAST, r))]
            if r < 3:
                own = [x + y for x, y in zip(own, get(WEST, r + 1))]
            south, north = get(SOUTH_UP, r), get(NORTH_DOWN, r)
            inner_south = [jnp.where(lanes.phase == 0, 0.0, x) for x in south]
            inner_north = [jnp.where(lanes.phase == 3, 0.0, x) for x in north]
            own = [x + y + z for x, y, z in zip(own, inner_south, inner_north)]
            other = [
                jnp.where(lanes.phase == 0, x, jnp.where(lanes.phase == 3, y, 0.0))
                for x, y in zip(south, north)
            ]
        for colour in (0, 1):
            mine = lanes.even if colour == 0 else jnp.logical_not(lanes.even)
            state[colour][r] = [
                jnp.where(mine, own[h], 0.0 if other is None else other[h]) for h in (0, 1)
            ]
    wide = [{}, {}, {}]
    for r in range(max(first - 2, -2), min(last + 2, 5) + 1):
        obs = get_obs(r)
        pair = [stencil(lanes, state[colour], r, get, True) for colour in (0, 1)]
        pair = [[obs[h] * value[h] for h in (0, 1)] for value in pair]
        own = [jnp.where(lanes.even, pair[0][h], pair[1][h]) for h in (0, 1)]
        other = [jnp.where(lanes.even, pair[1][h], pair[0][h]) for h in (0, 1)]
        for colour in range(3):
            wide[colour][r] = [
                jnp.where(
                    lanes.third[h] == colour,
                    own[h],
                    jnp.where(lanes.near[h] == colour, other[h], 0.0),
                )
                for h in (0, 1)
            ]
    once = [
        {
            r: stencil(lanes, wide[colour], r, get, False)
            for r in range(max(first - 1, -3), min(last + 1, 6) + 1)
        }
        for colour in range(3)
    ]
    weights = {}
    for r in range(first, last + 1):
        twice = [stencil(lanes, once[colour], r, get, False) for colour in range(3)]

        def pick(index):
            return [
                jnp.where(
                    index[h] == 0, twice[0][h], jnp.where(index[h] == 1, twice[1][h], twice[2][h])
                )
                for h in (0, 1)
            ]

        own = pick(lanes.third)
        if 0 <= r <= 3:
            own = [x + 1.0 for x in own]
        weights[r, 0] = own
        if -3 <= r <= 6:
            weights[r, 1] = pick(lanes.near)
        if -1 <= r <= 4:
            weights[r, 2] = pick(lanes.far)
    return weights


def apply_weights(lanes, keys, read_weight, read_field, write, probes):
    sums = {}
    for r in sorted({r for r, _ in keys}):
        fields = [read_field(probe, r) for probe in probes]
        for part in range(3):
            if (r, part) not in keys:
                continue
            weight = read_weight(r, part)
            for n in range(len(probes)):
                for h in (0, 1):
                    term = weight[h] * fields[n][h]
                    key = (n, part, h)
                    sums[key] = sums[key] + term if key in sums else term
    low = lanes.phase < 2
    for n, probe in enumerate(probes):
        own, near, far = ([sums.get((n, part, h)) for h in (0, 1)] for part in range(3))
        if far[0] is None:
            down = [jnp.where(low, x, 0.0) for x in near]
            up = [jnp.where(low, 0.0, x) for x in near]
        else:
            down = [jnp.where(low, x, y) for x, y in zip(near, far)]
            up = [jnp.where(low, y, x) for x, y in zip(near, far)]
        for h in (0, 1):
            write(probe, 0, h, own[h])
            write(probe, 1, h, down[h])
            write(probe, 2, h, up[h])


def pooling(parity):
    row = lax.broadcasted_iota(jnp.int32, (256, HALF), 0)
    column = lax.broadcasted_iota(jnp.int32, (256, HALF), 1)
    return jnp.where((row >> 2) + 64 * parity == column, 1.0 / 16.0, 0.0).astype(BF16)


def split3(x):
    high = x.astype(BF16)
    rest = x - high.astype(F32)
    middle = rest.astype(BF16)
    low = (rest - middle.astype(F32)).astype(BF16)
    return high, middle, low


def pool_into(lanes, sums, rows, count, write):
    total = None
    for parity in (0, 1):
        matrix = pooling(parity)
        own, down, up = (
            [
                jnp.concatenate(
                    [
                        sums[2 * part + h, pl.ds(n * count * 8 + 2 * pair + parity, count, stride=8), :]
                        for n in range(rows)
                        for pair in range(4)
                    ],
                    axis=0,
                )
                for h in (0, 1)
            ]
            for part in range(3)
        )
        lane = lax.broadcasted_iota(jnp.int32, own[0].shape, 1)
        d0, d1 = (pltpu.roll(x, HALF - 4, 1) for x in down)
        u0, u1 = (pltpu.roll(x, 4, 1) for x in up)
        low = own[0] + (jnp.where(lane >= HALF - 4, d1, d0) + jnp.where(lane < 4, u1, u0))
        high = own[1] + (jnp.where(lane >= HALF - 4, d0, d1) + jnp.where(lane < 4, u0, u1))
        for part in split3(jnp.concatenate([low, high], axis=1)):
            term = jnp.dot(part, matrix, preferred_element_type=F32)
            total = term if total is None else total + term
    for n in range(rows):
        for pair in range(4):
            start = (n * 4 + pair) * count
            write(n, pair, total[start : start + count])


GROUP = 8


def weight_keys(first, last):
    reach = {0: (-4, 7), 1: (-3, 6), 2: (-1, 4)}
    return [
        (r, part)
        for part, (low, high) in reach.items()
        for r in range(max(first, low), min(last, high) + 1)
    ]


def fetch_all(copies):
    for copy in copies:
        copy.start()
    return copies


def pack_kernel(winds_hbm, obs_hbm, up, down, winds, obs, sems):
    lons = obs.shape[0]
    copies = fetch_all(
        [
            pltpu.make_async_copy(winds_hbm, winds, sems.at[0]),
            pltpu.make_async_copy(obs_hbm, obs, sems.at[1]),
        ]
    )
    for copy in copies:
        copy.wait()
    up[0:3] = winds[0, lons - 3 :]
    up[3:6] = winds[1, lons - 3 :]
    up[6:8] = obs[lons - 2 :]
    up[8:] = obs[lons - 4 :]
    down[0:4] = winds[0, 0:4]
    down[4:8] = winds[1, 0:4]
    down[8:10] = obs[0:2]


def interior_kernel(
    winds, obs, field_hbm, out, part_low, part_high, sides, coef, weights, sums, field, sems
):
    count, lons = field.shape[0], field.shape[1]
    blocks = lons // 4
    field_copy = pltpu.make_async_copy(field_hbm, field, sems.at[0])
    field_copy.start()
    side_copies = [
        pltpu.make_async_copy(
            field_hbm.at[:, pl.ds(start, 4)], sides.at[:, pl.ds(4 * n, 4)], sems.at[1 + n]
        )
        for n, start in enumerate((0, lons - 4))
    ]
    for copy in side_copies:
        copy.start()
    lanes = Lanes()

    def coefficients(lon, carry):
        write_coefficients(
            coef,
            lon,
            halves(winds, 0, lon),
            halves(winds, 0, jnp.minimum(lon + 1, lons - 1)),
            halves(winds, 1, lon),
            lanes,
        )
        return carry

    lax.fori_loop(0, lons, coefficients, 0, unroll=8)

    def weigh(first, last, block, carry):
        base = block * 4

        def get(plane, r):
            return halves(coef, plane, base + r)

        result = block_weights(lanes, get, lambda r: halves(obs, base + r), first, last)
        for (r, part), value in result.items():
            store(weights, value, block, part, r + 4)
        return carry

    spans = ((0, 1, 2, 7), (1, blocks - 1, -4, 7), (blocks - 1, blocks, -4, -1))
    for start, stop, first, last in spans:
        lax.fori_loop(start, stop, functools.partial(weigh, first, last), 0, unroll=stop - start)
    field_copy.wait()
    groups = count // GROUP

    def sweep(first, last, step, carry):
        block = step // groups
        start = (step % groups) * GROUP

        def write(probe, part, h, value):
            row = pl.multiple_of((block * count + probe) * 8, 8)
            sums[2 * part + h, pl.ds(row, 8), :] = value

        apply_weights(
            lanes,
            weight_keys(first, last),
            lambda r, part: halves(weights, block, part, r + 4),
            lambda probe, r: halves(field, probe, block * 4 + r),
            write,
            [start + n for n in range(GROUP)],
        )
        return carry

    for start, stop, first, last in spans:
        lax.fori_loop(start * groups, stop * groups, functools.partial(sweep, first, last), 0)

    def put(n, pair, value):
        if n == 0:
            part_low[:, pair * HALF : (pair + 1) * HALF] = value
        elif n == blocks - 1:
            part_high[:, pair * HALF : (pair + 1) * HALF] = value
        else:
            column = ((n - 1) * 4 + pair) * HALF
            out[:, column : column + HALF] = value

    pool_into(lanes, sums, blocks, count, put)
    for copy in side_copies:
        copy.wait()


def edge_sums(winds, obs, from_low, from_high, field, coef, weights, sums, spans, jobs, put):
    count, lons = field.shape[0], obs.shape[0]
    lanes = Lanes()

    def wind(which, lon):
        if lon < 0:
            return halves(from_low, 3 * which + lon + 3)
        if lon >= lons:
            return halves(from_high, 4 * which + lon - lons)
        return halves(winds, which, lon)

    def weight_at(lon):
        if lon < 0:
            return halves(from_low, 6 + lon + 2)
        if lon >= lons:
            return halves(from_high, 8 + lon - lons)
        return halves(obs, lon)

    slots = {}
    for start, stop in spans:
        for lon in range(start, stop + 1):
            slots[lon] = len(slots)
            write_coefficients(
                coef, slots[lon], wind(0, lon), wind(0, min(lon + 1, stop)), wind(1, lon), lanes
            )
    for n, (base, first, last) in enumerate(jobs):
        result = block_weights(
            lanes,
            lambda plane, r: halves(coef, plane, slots[base + r]),
            lambda r: weight_at(base + r),
            first,
            last,
        )
        for (r, part), value in result.items():
            store(weights, value, n, part, r + 4)

    def sweep(step, carry):
        for n, (base, first, last) in enumerate(jobs):

            def write(probe, part, h, value):
                row = pl.multiple_of((n * count + probe) * 8, 8)
                sums[2 * part + h, pl.ds(row, 8), :] = value

            def read(probe, r):
                lon = base + r
                return halves(field, probe, lon if lon < 4 else lon - (lons - 8))

            apply_weights(
                lanes,
                weight_keys(first, last),
                lambda r, part: halves(weights, n, part, r + 4),
                read,
                write,
                [step * GROUP + k for k in range(GROUP)],
            )
        return carry

    lax.fori_loop(0, count // GROUP, sweep, 0)
    pool_into(lanes, sums, len(jobs), count, put)


def split_by_core(where, values, mine, other):
    first = lax.rem(where[0], 2) == 0
    for pair in range(4):
        columns = slice(pair * HALF, (pair + 1) * HALF)
        a, b = values[0, pair], values[1, pair]
        mine[:, columns] = jnp.where(first, a, b)
        other[:, columns] = jnp.where(first, b, a)


def share_kernel(
    where, winds, obs, from_low, from_high, field, mine, other, coef, weights, sums
):
    lons = obs.shape[0]
    values = {}

    def put(n, pair, value):
        values[1 - n, pair] = value

    edge_sums(
        winds, obs, from_low, from_high, field, coef, weights, sums,
        ((-3, 3), (lons - 3, lons + 3)),
        ((-4, 4, 7), (lons, -4, -1)),
        put,
    )
    split_by_core(where, values, mine, other)


def rest_kernel(
    where, winds, obs, from_low, from_high, field, part_low, part_high, after,
    mine, other, coef, weights, sums,
):
    lons = obs.shape[0]
    values = {}

    def put(n, pair, value):
        columns = slice(pair * HALF, (pair + 1) * HALF)
        values[n, pair] = value + (part_low, part_high)[n][:, columns]

    edge_sums(
        winds, obs, from_low, from_high, field, coef, weights, sums,
        ((-2, 4), (lons - 5, lons + 1)),
        ((0, 0, 1), (lons - 4, 0, 3)),
        put,
    )
    split_by_core(where, values, mine, other)


def self_product(panel):
    return lax.dot_general(
        panel,
        panel,
        (((1,), (1,)), ((), ())),
        precision=lax.Precision.HIGHEST,
        preferred_element_type=F32,
    )


def assemble(where, pieces, panel):
    rows = pieces[0].shape[0]
    for k, piece in enumerate(pieces):
        at = pl.multiple_of(lax.bitwise_xor(where[0], jnp.int32(k)) * rows, 8)
        panel[pl.ds(at, rows)] = piece[...]


def inner_gram_kernel(where, *refs):
    pieces, (panel, out) = refs[:-2], refs[-2:]
    assemble(where, pieces, panel)
    out[...] = self_product(panel[...])


def gram_kernel(where, inner, chip, far, chip_other, far_other, panel, out):
    rows = chip.shape[0] // 2
    core = lax.rem(where[0], 2)
    for side, pieces, flip in ((core, (chip, far), 0), (1 - core, (chip_other, far_other), 1)):
        for k in range(4):
            at = pl.multiple_of(lax.bitwise_xor(where[0], jnp.int32(k ^ flip)) * rows, 8)
            panel[side, pl.ds(at, rows)] = pieces[k // 2][(k % 2) * rows : (k % 2 + 1) * rows]
    gram = self_product(panel[0]) + self_product(panel[1]) + inner[...]
    half = gram.shape[0] // 2
    packed = jnp.concatenate([gram[:half], gram[half:]], axis=1)
    for n in range(out.shape[0]):
        out[n] = packed


def factor_kernel(where, grams, inner, edge, basis, upper, inverse):
    packed = grams[0]
    for n in range(1, grams.shape[0]):
        packed = packed + grams[n]
    size = 2 * packed.shape[0]
    gram = jnp.concatenate([packed[:, :size], packed[:, size:]], axis=0)
    row = lax.broadcasted_iota(jnp.int32, (size, size), 0)
    column = lax.broadcasted_iota(jnp.int32, (size, size), 1)
    state = jnp.concatenate([gram, jnp.where(row == column, 1.0, 0.0).astype(F32)], axis=1)
    tiles = [state[8 * t : 8 * t + 8] for t in range(size // 8)]
    full = (8, 2 * size)
    sub = lax.broadcasted_iota(jnp.int32, full, 0)
    scales = []
    for own in range(size // 8):
        spread = {
            (t, j): jnp.broadcast_to(tiles[t][:, 8 * own + j : 8 * own + j + 1], full)
            for t in range(own, size // 8)
            for j in range(8)
        }
        pivots = {
            (i, j): jnp.broadcast_to(spread[own, j][i : i + 1], full)
            for i in range(8)
            for j in range(i + 1)
        }
        rows = [jnp.broadcast_to(tiles[own][j : j + 1], full) for j in range(8)]
        inverses = []
        for j in range(8):
            inverses.append(1.0 / pivots[j, j])
            scales.append(lax.rsqrt(pivots[j, j]))
            for i in range(j + 1, 8):
                ratio = pivots[i, j] * inverses[j]
                for m in range(i, 8):
                    pivots[m, i] = pivots[m, i] - ratio * pivots[m, j]
                rows[i] = rows[i] - ratio * rows[j]
                for t in range(own + 1, size // 8):
                    spread[t, i] = spread[t, i] - ratio * spread[t, j]
        for t in range(own + 1, size // 8):
            update = (spread[t, 0] * inverses[0]) * rows[0]
            for j in range(1, 8):
                update = update + (spread[t, j] * inverses[j]) * rows[j]
            tiles[t] = tiles[t] - update
        for j in range(8):
            tiles[own] = jnp.where(sub == j, rows[j], tiles[own])
    for t in range(size // 8):
        scale = scales[8 * t]
        for at in range(1, 8):
            scale = jnp.where(sub == at, scales[8 * t + at], scale)
        scaled = tiles[t] * scale
        column = lax.broadcasted_iota(jnp.int32, (8, size), 1)
        here = lax.broadcasted_iota(jnp.int32, (8, size), 0) + 8 * t
        upper[8 * t : 8 * t + 8] = jnp.where(column >= here, scaled[:, :size], 0.0)
        inverse[8 * t : 8 * t + 8] = scaled[:, size:]
    blocks, count, width = basis.shape
    own_rows = inverse[pl.ds(pl.multiple_of(where[0] * count, 8), count)]

    def project(columns):
        return jnp.dot(
            own_rows, columns, precision=lax.Precision.HIGHEST, preferred_element_type=F32
        )

    basis[0] = project(edge[0])
    for n in range(blocks - 2):
        basis[n + 1] = project(inner[:, n * width : (n + 1) * width])
    basis[blocks - 1] = project(edge[1])


VMEM = pl.BlockSpec(memory_space=pltpu.VMEM)
SMEM = pl.BlockSpec(memory_space=pltpu.SMEM)
HBM = pl.BlockSpec(memory_space=pltpu.HBM)
ANY = pl.BlockSpec(memory_space=pl.ANY)
MIB = 1024 * 1024
COST = 1_000_000


def shape(*dims):
    return jax.ShapeDtypeStruct(dims, F32)


def call(kernel, name, out_shape, in_specs, scratch=(), flops=1_000_000):
    return pl.pallas_call(
        kernel,
        out_shape=out_shape,
        in_specs=in_specs,
        out_specs=jax.tree.map(lambda _: VMEM, out_shape),
        scratch_shapes=scratch,
        compiler_params=pltpu.CompilerParams(vmem_limit_bytes=32 * MIB),
        cost_estimate=pl.CostEstimate(flops=flops, bytes_accessed=100_000, transcendentals=0),
        name=name,
    )


def swap_probes(value, step):
    return lax.ppermute(value, "probe", [(i, i ^ step) for i in range(lax.axis_size("probe"))])


def body(increments, winds, obs_weight):
    count, lons, levels, lats = increments.shape
    blocks = lons // 4
    probes = count * lax.axis_size("probe")
    ring = lax.axis_size("lon")
    up = [(i, (i + 1) % ring) for i in range(ring)]
    down = [(i, (i - 1) % ring) for i in range(ring)]
    where = lax.axis_index("probe").reshape(1).astype(jnp.int32)
    dma = pltpu.SemaphoreType.DMA
    increments, winds, obs_weight = (
        pltpu.with_memory_space_constraint(x, pltpu.HBM) for x in (increments, winds, obs_weight)
    )
    pack_up, pack_down, winds, obs_weight = call(
        pack_kernel,
        "pack",
        (
            shape(12, levels, lats),
            shape(10, levels, lats),
            shape(2, lons, levels, lats),
            shape(lons, levels, lats),
        ),
        [HBM, HBM],
        [dma((2,))],
    )(winds, obs_weight)
    from_low = lax.ppermute(pack_up, "lon", up)
    from_high = lax.ppermute(pack_down, "lon", down)
    inner, part_low, part_high, sides = call(
        interior_kernel,
        "interior",
        (
            shape(count, (blocks - 2) * 512),
            shape(count, 512),
            shape(count, 512),
            shape(count, 8, levels, lats),
        ),
        [VMEM, VMEM, HBM],
        [
            pltpu.VMEM((PLANES, lons, levels, lats), F32),
            pltpu.VMEM((blocks, 3, 12, levels, lats), F32),
            pltpu.VMEM((6, blocks * count * 8, HALF), F32),
            pltpu.VMEM((count, lons, levels, lats), F32),
            dma((3,)),
        ],
        COST,
    )(winds, obs_weight, increments)
    edge_scratch = [
        pltpu.VMEM((PLANES, 14, levels, lats), F32),
        pltpu.VMEM((2, 3, 12, levels, lats), F32),
        pltpu.VMEM((6, 2 * count * 8, HALF), F32),
    ]
    share, share_other = call(
        share_kernel, "share", (shape(count, 512),) * 2, [SMEM] + [VMEM] * 5, edge_scratch
    )(where, winds, obs_weight, from_low, from_high, sides)
    share = jnp.concatenate([share, swap_probes(share_other, 1)], axis=0)
    size = lax.axis_size("probe")
    arrived = lax.ppermute(
        share,
        ("lon", "probe"),
        [
            (i * size + p, (up, down)[p & 1][i][1] * size + p)
            for i in range(ring)
            for p in range(size)
        ],
    )
    rest, rest_other = call(
        rest_kernel, "rest", (shape(count, 512),) * 2, [SMEM] + [VMEM] * 7 + [ANY], edge_scratch
    )(where, winds, obs_weight, from_low, from_high, sides, part_low, part_high, share)
    inner, rest = lax.optimization_barrier((inner, rest))
    inner_pieces = [inner, swap_probes(inner, 1), swap_probes(inner, 2)]
    chip = jnp.concatenate([rest, swap_probes(rest_other, 1)], axis=0) + arrived
    far = swap_probes(chip, 2)
    chip_other = swap_probes(chip, 1)
    inner_pieces, far = lax.optimization_barrier((inner_pieces, far))
    inner_pieces.append(swap_probes(inner_pieces[2], 1))
    edge_pieces = [chip, far, chip_other, swap_probes(far, 1)]
    inner_panel, inner_gram = call(
        inner_gram_kernel,
        "inner_gram",
        (shape(probes, inner.shape[1]), shape(probes, probes)),
        [SMEM] + [VMEM] * len(inner_pieces),
        (),
        COST,
    )(where, *inner_pieces)
    edge_panel, grams = call(
        gram_kernel,
        "gram",
        (shape(2, probes, 512), shape(ring, probes // 2, 2 * probes)),
        [SMEM, VMEM] + [VMEM] * len(edge_pieces),
        (),
        COST,
    )(where, inner_gram, *edge_pieces)
    grams = lax.all_to_all(grams, "lon", 0, 0, tiled=True)
    basis, upper = call(
        factor_kernel,
        "factor",
        (shape(blocks, count, 512), shape(probes, probes)),
        [SMEM, VMEM, VMEM, VMEM],
        [pltpu.VMEM((probes, probes), F32)],
        COST,
    )(where, grams, inner_panel, edge_panel)
    return basis.transpose(1, 0, 2), upper


def solution(mesh):
    in_specs = (P("probe", "lon", None, None), P(None, "lon", None, None), P("lon", None, None))
    out_specs = (P("probe", "lon", None), P())
    return jax.shard_map(body, mesh=mesh, in_specs=in_specs, out_specs=out_specs, check_vma=False)
```

```python
import functools

import jax
import jax.numpy as jnp
from jax import lax
from jax.experimental import pallas as pl
from jax.experimental.pallas import tpu as pltpu
from jax.sharding import PartitionSpec as P

F32 = jnp.float32
BF16 = jnp.bfloat16
HALF = 128
DIAG, EAST, WEST, SOUTH_UP, SOUTH_DOWN, NORTH_UP, NORTH_DOWN = range(7)
PLANES = 7


def halves(ref, *index):
    return [ref[index + (slice(None), slice(h * HALF, (h + 1) * HALF))] for h in (0, 1)]


def store(ref, value, *index):
    for h in (0, 1):
        ref[index + (slice(None), slice(h * HALF, (h + 1) * HALF))] = value[h]


class Lanes:
    def __init__(self):
        lane = lax.broadcasted_iota(jnp.int32, (8, HALF), 1)
        self.first = lane == 0
        self.last = lane == HALF - 1
        self.phase = lane & 3
        self.even = ((lane >> 2) & 1) == 0
        self.third = [lax.rem((lane + h * HALF) >> 2, 3) for h in (0, 1)]
        low = self.phase < 2
        self.near = [lax.rem(t + jnp.where(low, 2, 1), 3) for t in self.third]
        self.far = [lax.rem(t + jnp.where(low, 1, 2), 3) for t in self.third]

    def below(self, f):
        r0, r1 = pltpu.roll(f[0], 1, 1), pltpu.roll(f[1], 1, 1)
        return [r0, jnp.where(self.first, r0, r1)]

    def above(self, f):
        r0, r1 = pltpu.roll(f[0], HALF - 1, 1), pltpu.roll(f[1], HALF - 1, 1)
        return [jnp.where(self.last, r1, r0), r1]


def write_coefficients(coef, slot, u, u_next, v, lanes):
    v = [jnp.where(lanes.first, 0.0, v[0]), v[1]]
    south_up = [jnp.maximum(x, 0.0) for x in v]
    south_down = [jnp.maximum(-x, 0.0) for x in v]
    north = []
    for field in (south_up, south_down):
        r0, r1 = pltpu.roll(field[0], HALF - 1, 1), pltpu.roll(field[1], HALF - 1, 1)
        north.append([jnp.where(lanes.last, r1, r0), jnp.where(lanes.last, r0, r1)])
    east = [jnp.maximum(x, 0.0) for x in u]
    west = [jnp.maximum(-x, 0.0) for x in u]
    diag = [
        1.0 - jnp.maximum(u_next[h], 0.0) - west[h] - north[0][h] - south_down[h] for h in (0, 1)
    ]
    for plane, value in (
        (DIAG, diag),
        (EAST, east),
        (WEST, west),
        (SOUTH_UP, south_up),
        (SOUTH_DOWN, south_down),
        (NORTH_UP, north[0]),
        (NORTH_DOWN, north[1]),
    ):
        store(coef, value, plane, slot)


def stencil(lanes, field, r, get, forward):
    total = [None, None]

    def add(coefficient, value):
        for h in (0, 1):
            term = coefficient[h] * value[h]
            total[h] = term if total[h] is None else total[h] + term

    if r in field:
        here = field[r]
        add(get(DIAG, r), here)
        add(get(SOUTH_UP if forward else SOUTH_DOWN, r), lanes.below(here))
        add(get(NORTH_DOWN if forward else NORTH_UP, r), lanes.above(here))
    if r - 1 in field:
        add(get(EAST if forward else WEST, r), field[r - 1])
    if r + 1 in field:
        add(get(WEST if forward else EAST, r + 1), field[r + 1])
    return total


def block_weights(lanes, get, get_obs, first, last):
    state = [{}, {}]
    for r in range(max(first - 3, -1), min(last + 3, 4) + 1):
        if r == -1:
            own = get(WEST, 0)
            other = None
        elif r == 4:
            own = get(EAST, 4)
            other = None
        else:
            own = get(DIAG, r)
            if r > 0:
                own = [x + y for x, y in zip(own, get(EAST, r))]
            if r < 3:
                own = [x + y for x, y in zip(own, get(WEST, r + 1))]
            south, north = get(SOUTH_UP, r), get(NORTH_DOWN, r)
            inner_south = [jnp.where(lanes.phase == 0, 0.0, x) for x in south]
            inner_north = [jnp.where(lanes.phase == 3, 0.0, x) for x in north]
            own = [x + y + z for x, y, z in zip(own, inner_south, inner_north)]
            other = [
                jnp.where(lanes.phase == 0, x, jnp.where(lanes.phase == 3, y, 0.0))
                for x, y in zip(south, north)
            ]
        for colour in (0, 1):
            mine = lanes.even if colour == 0 else jnp.logical_not(lanes.even)
            state[colour][r] = [
                jnp.where(mine, own[h], 0.0 if other is None else other[h]) for h in (0, 1)
            ]
    wide = [{}, {}, {}]
    for r in range(max(first - 2, -2), min(last + 2, 5) + 1):
        obs = get_obs(r)
        pair = [stencil(lanes, state[colour], r, get, True) for colour in (0, 1)]
        pair = [[obs[h] * value[h] for h in (0, 1)] for value in pair]
        own = [jnp.where(lanes.even, pair[0][h], pair[1][h]) for h in (0, 1)]
        other = [jnp.where(lanes.even, pair[1][h], pair[0][h]) for h in (0, 1)]
        for colour in range(3):
            wide[colour][r] = [
                jnp.where(
                    lanes.third[h] == colour,
                    own[h],
                    jnp.where(lanes.near[h] == colour, other[h], 0.0),
                )
                for h in (0, 1)
            ]
    once = [
        {
            r: stencil(lanes, wide[colour], r, get, False)
            for r in range(max(first - 1, -3), min(last + 1, 6) + 1)
        }
        for colour in range(3)
    ]
    weights = {}
    for r in range(first, last + 1):
        twice = [stencil(lanes, once[colour], r, get, False) for colour in range(3)]

        def pick(index):
            return [
                jnp.where(
                    index[h] == 0, twice[0][h], jnp.where(index[h] == 1, twice[1][h], twice[2][h])
                )
                for h in (0, 1)
            ]

        own = pick(lanes.third)
        if 0 <= r <= 3:
            own = [x + 1.0 for x in own]
        weights[r, 0] = own
        if -3 <= r <= 6:
            weights[r, 1] = pick(lanes.near)
        if -1 <= r <= 4:
            weights[r, 2] = pick(lanes.far)
    return weights


def apply_weights(lanes, keys, read_weight, read_field, write, probes):
    sums = {}
    for r in sorted({r for r, _ in keys}):
        fields = [read_field(probe, r) for probe in probes]
        for part in range(3):
            if (r, part) not in keys:
                continue
            weight = read_weight(r, part)
            for n in range(len(probes)):
                for h in (0, 1):
                    term = weight[h] * fields[n][h]
                    key = (n, part, h)
                    sums[key] = sums[key] + term if key in sums else term
    low = lanes.phase < 2
    for n, probe in enumerate(probes):
        own, near, far = ([sums.get((n, part, h)) for h in (0, 1)] for part in range(3))
        if far[0] is None:
            down = [jnp.where(low, x, 0.0) for x in near]
            up = [jnp.where(low, 0.0, x) for x in near]
        else:
            down = [jnp.where(low, x, y) for x, y in zip(near, far)]
            up = [jnp.where(low, y, x) for x, y in zip(near, far)]
        for h in (0, 1):
            write(probe, 0, h, own[h])
            write(probe, 1, h, down[h])
            write(probe, 2, h, up[h])


def pooling(parity):
    row = lax.broadcasted_iota(jnp.int32, (256, HALF), 0)
    column = lax.broadcasted_iota(jnp.int32, (256, HALF), 1)
    return jnp.where((row >> 2) + 64 * parity == column, 1.0 / 16.0, 0.0).astype(BF16)


def split3(x):
    high = x.astype(BF16)
    rest = x - high.astype(F32)
    middle = rest.astype(BF16)
    low = (rest - middle.astype(F32)).astype(BF16)
    return high, middle, low


def pool_into(lanes, sums, rows, count, write):
    total = None
    for parity in (0, 1):
        matrix = pooling(parity)
        own, down, up = (
            [
                jnp.concatenate(
                    [
                        sums[2 * part + h, pl.ds(n * count * 8 + 2 * pair + parity, count, stride=8), :]
                        for n in range(rows)
                        for pair in range(4)
                    ],
                    axis=0,
                )
                for h in (0, 1)
            ]
            for part in range(3)
        )
        lane = lax.broadcasted_iota(jnp.int32, own[0].shape, 1)
        d0, d1 = (pltpu.roll(x, HALF - 4, 1) for x in down)
        u0, u1 = (pltpu.roll(x, 4, 1) for x in up)
        low = own[0] + (jnp.where(lane >= HALF - 4, d1, d0) + jnp.where(lane < 4, u1, u0))
        high = own[1] + (jnp.where(lane >= HALF - 4, d0, d1) + jnp.where(lane < 4, u0, u1))
        for part in split3(jnp.concatenate([low, high], axis=1)):
            term = jnp.dot(part, matrix, preferred_element_type=F32)
            total = term if total is None else total + term
    for n in range(rows):
        for pair in range(4):
            start = (n * 4 + pair) * count
            write(n, pair, total[start : start + count])


GROUP = 8


def weight_keys(first, last):
    reach = {0: (-4, 7), 1: (-3, 6), 2: (-1, 4)}
    return [
        (r, part)
        for part, (low, high) in reach.items()
        for r in range(max(first, low), min(last, high) + 1)
    ]


def fetch_all(copies):
    for copy in copies:
        copy.start()
    return copies


def pack_kernel(winds_hbm, obs_hbm, up, down, winds, obs, sems):
    lons = obs.shape[0]
    copies = fetch_all(
        [
            pltpu.make_async_copy(winds_hbm, winds, sems.at[0]),
            pltpu.make_async_copy(obs_hbm, obs, sems.at[1]),
        ]
    )
    for copy in copies:
        copy.wait()
    up[0:3] = winds[0, lons - 3 :]
    up[3:6] = winds[1, lons - 3 :]
    up[6:8] = obs[lons - 2 :]
    up[8:10] = obs[lons - 2 :]
    down[0:4] = winds[0, 0:4]
    down[4:7] = winds[1, 0:3]
    down[7:9] = obs[0:2]


def split_by_core(where, values, mine, other):
    first = lax.rem(where[0], 2) == 0
    for pair in range(mine.shape[1] // HALF):
        columns = slice(pair * HALF, (pair + 1) * HALF)
        a, b = values[0, pair], values[1, pair]
        mine[:, columns] = jnp.where(first, a, b)
        other[:, columns] = jnp.where(first, b, a)


def interior_kernel(
    where, winds, obs, field_hbm, mine, other, part_low, part_high, sides,
    coef, weights, sums, field, sems,
):
    count, lons = field.shape[0], field.shape[1]
    blocks = lons // 4
    field_copy = pltpu.make_async_copy(field_hbm, field, sems.at[0])
    field_copy.start()
    side_copies = [
        pltpu.make_async_copy(
            field_hbm.at[:, pl.ds(start, 4)], sides.at[:, pl.ds(4 * n, 4)], sems.at[1 + n]
        )
        for n, start in enumerate((0, lons - 4))
    ]
    for copy in side_copies:
        copy.start()
    lanes = Lanes()

    def coefficients(lon, carry):
        write_coefficients(
            coef,
            lon,
            halves(winds, 0, lon),
            halves(winds, 0, jnp.minimum(lon + 1, lons - 1)),
            halves(winds, 1, lon),
            lanes,
        )
        return carry

    lax.fori_loop(0, lons, coefficients, 0, unroll=8)

    def weigh(first, last, block, carry):
        base = block * 4

        def get(plane, r):
            return halves(coef, plane, base + r)

        result = block_weights(lanes, get, lambda r: halves(obs, base + r), first, last)
        for (r, part), value in result.items():
            store(weights, value, block, part, r + 4)
        return carry

    spans = ((0, 1, 2, 7), (1, blocks - 1, -4, 7), (blocks - 1, blocks, -4, -1))
    for start, stop, first, last in spans:
        lax.fori_loop(start, stop, functools.partial(weigh, first, last), 0, unroll=stop - start)
    field_copy.wait()
    groups = count // GROUP

    def sweep(first, last, step, carry):
        block = step // groups
        start = (step % groups) * GROUP

        def write(probe, part, h, value):
            row = pl.multiple_of((block * count + probe) * 8, 8)
            sums[2 * part + h, pl.ds(row, 8), :] = value

        apply_weights(
            lanes,
            weight_keys(first, last),
            lambda r, part: halves(weights, block, part, r + 4),
            lambda probe, r: halves(field, probe, block * 4 + r),
            write,
            [start + n for n in range(GROUP)],
        )
        return carry

    for start, stop, first, last in spans:
        lax.fori_loop(start * groups, stop * groups, functools.partial(sweep, first, last), 0)

    def put(n, pair, value):
        if n == 0:
            part_low[:, pair * HALF : (pair + 1) * HALF] = value
        elif n == blocks - 1:
            part_high[:, pair * HALF : (pair + 1) * HALF] = value
        else:
            values[divmod((n - 1) * 4 + pair, pieces)] = value

    values = {}
    pieces = mine.shape[1] // HALF
    pool_into(lanes, sums, blocks, count, put)
    split_by_core(where, values, mine, other)
    for copy in side_copies:
        copy.wait()


def edge_sums(winds, obs, from_low, from_high, field, coef, weights, sums, spans, jobs, put):
    count, lons = field.shape[0], obs.shape[0]
    lanes = Lanes()

    def wind(which, lon):
        if lon < 0:
            return halves(from_low, 3 * which + lon + 3)
        if lon >= lons:
            return halves(from_high, min(4 * which + lon - lons, 6))
        return halves(winds, which, lon)

    def weight_at(lon):
        if lon < 0:
            return halves(from_low, 6 + lon + 2)
        if lon >= lons:
            return halves(from_high, 7 + lon - lons)
        return halves(obs, lon)

    slots = {}
    for start, stop in spans:
        for lon in range(start, stop + 1):
            slots[lon] = len(slots)
            write_coefficients(
                coef, slots[lon], wind(0, lon), wind(0, min(lon + 1, stop)), wind(1, lon), lanes
            )
    for n, (base, first, last) in enumerate(jobs):
        result = block_weights(
            lanes,
            lambda plane, r: halves(coef, plane, slots[base + r]),
            lambda r: weight_at(base + r),
            first,
            last,
        )
        for (r, part), value in result.items():
            store(weights, value, n, part, r + 4)

    def sweep(step, carry):
        for n, (base, first, last) in enumerate(jobs):

            def write(probe, part, h, value):
                row = pl.multiple_of((n * count + probe) * 8, 8)
                sums[2 * part + h, pl.ds(row, 8), :] = value

            def read(probe, r):
                lon = base + r
                return halves(field, probe, lon if lon < 4 else lon - (lons - 8))

            apply_weights(
                lanes,
                weight_keys(first, last),
                lambda r, part: halves(weights, n, part, r + 4),
                read,
                write,
                [step * GROUP + k for k in range(GROUP)],
            )
        return carry

    lax.fori_loop(0, count // GROUP, sweep, 0)
    pool_into(lanes, sums, len(jobs), count, put)


def share_kernel(
    where, winds, obs, from_low, from_high, field, mine, other, coef, weights, sums
):
    lons = obs.shape[0]
    values = {}

    def put(n, pair, value):
        values[1 - n, pair] = value

    edge_sums(
        winds, obs, from_low, from_high, field, coef, weights, sums,
        ((-3, 3), (lons - 3, lons + 3)),
        ((-4, 4, 7), (lons, -4, -1)),
        put,
    )
    split_by_core(where, values, mine, other)


def rest_kernel(
    where, winds, obs, from_low, from_high, field, part_low, part_high, after,
    mine, other, coef, weights, sums,
):
    lons = obs.shape[0]
    values = {}

    def put(n, pair, value):
        columns = slice(pair * HALF, (pair + 1) * HALF)
        values[n, pair] = value + (part_low, part_high)[n][:, columns]

    edge_sums(
        winds, obs, from_low, from_high, field, coef, weights, sums,
        ((-2, 4), (lons - 5, lons + 1)),
        ((0, 0, 1), (lons - 4, 0, 3)),
        put,
    )
    split_by_core(where, values, mine, other)


def self_product(panel):
    return lax.dot_general(
        panel,
        panel,
        (((1,), (1,)), ((), ())),
        precision=lax.Precision.HIGHEST,
        preferred_element_type=F32,
    )


def assemble(where, chip, far, panel):
    rows = chip.shape[0] // 2
    for k in range(4):
        at = pl.multiple_of(lax.bitwise_xor(where[0], jnp.int32(k)) * rows, 8)
        panel[pl.ds(at, rows)] = (chip, far)[k // 2][(k % 2) * rows : (k % 2 + 1) * rows]


def gram_kernel(where, inner_chip, inner_far, edge_chip, edge_far, panel, out):
    width = inner_chip.shape[1]
    assemble(where, inner_chip, inner_far, panel.at[:, :width])
    assemble(where, edge_chip, edge_far, panel.at[:, width:])
    gram = self_product(panel[...])
    half = gram.shape[0] // 2
    out[...] = jnp.concatenate([gram[:half], gram[half:]], axis=1)


def copies_kernel(mine, other, out):
    total = mine[...] + other[...]
    for n in range(out.shape[0]):
        out[n] = total


def factor_kernel(
    where, grams, panel, panel_other, basis, upper, inverse
):
    packed = grams[0]
    for n in range(1, grams.shape[0]):
        packed = packed + grams[n]
    size = 2 * packed.shape[0]
    gram = jnp.concatenate([packed[:, :size], packed[:, size:]], axis=0)
    row = lax.broadcasted_iota(jnp.int32, (size, size), 0)
    column = lax.broadcasted_iota(jnp.int32, (size, size), 1)
    state = jnp.concatenate([gram, jnp.where(row == column, 1.0, 0.0).astype(F32)], axis=1)
    tiles = [state[8 * t : 8 * t + 8] for t in range(size // 8)]
    full = (8, 2 * size)
    sub = lax.broadcasted_iota(jnp.int32, full, 0)
    scales = []
    for own in range(size // 8):
        spread = {
            (t, j): jnp.broadcast_to(tiles[t][:, 8 * own + j : 8 * own + j + 1], full)
            for t in range(own, size // 8)
            for j in range(8)
        }
        pivots = {
            (i, j): jnp.broadcast_to(spread[own, j][i : i + 1], full)
            for i in range(8)
            for j in range(i + 1)
        }
        rows = [jnp.broadcast_to(tiles[own][j : j + 1], full) for j in range(8)]
        inverses = []
        for j in range(8):
            inverses.append(1.0 / pivots[j, j])
            scales.append(lax.rsqrt(pivots[j, j]))
            for i in range(j + 1, 8):
                ratio = pivots[i, j] * inverses[j]
                for m in range(i, 8):
                    pivots[m, i] = pivots[m, i] - ratio * pivots[m, j]
                rows[i] = rows[i] - ratio * rows[j]
                for t in range(own + 1, size // 8):
                    spread[t, i] = spread[t, i] - ratio * spread[t, j]
        for t in range(own + 1, size // 8):
            update = (spread[t, 0] * inverses[0]) * rows[0]
            for j in range(1, 8):
                update = update + (spread[t, j] * inverses[j]) * rows[j]
            tiles[t] = tiles[t] - update
        for j in range(8):
            tiles[own] = jnp.where(sub == j, rows[j], tiles[own])
    for t in range(size // 8):
        scale = scales[8 * t]
        for at in range(1, 8):
            scale = jnp.where(sub == at, scales[8 * t + at], scale)
        scaled = tiles[t] * scale
        column = lax.broadcasted_iota(jnp.int32, (8, size), 1)
        here = lax.broadcasted_iota(jnp.int32, (8, size), 0) + 8 * t
        upper[8 * t : 8 * t + 8] = jnp.where(column >= here, scaled[:, :size], 0.0)
        inverse[8 * t : 8 * t + 8] = scaled[:, size:]
    blocks, count, width = basis.shape
    own_rows = inverse[pl.ds(pl.multiple_of(where[0] * count, 8), count)]

    def project(columns):
        return jnp.dot(
            own_rows, columns, precision=lax.Precision.HIGHEST, preferred_element_type=F32
        )

    core = lax.rem(where[0], 2)
    half = (blocks - 2) // 2
    for side, part in ((core, panel), (1 - core, panel_other)):
        for n in range(half):
            basis[1 + side * half + n] = project(part[:, n * width : (n + 1) * width])
        basis[side * (blocks - 1)] = project(part[:, half * width :])


VMEM = pl.BlockSpec(memory_space=pltpu.VMEM)
SMEM = pl.BlockSpec(memory_space=pltpu.SMEM)
HBM = pl.BlockSpec(memory_space=pltpu.HBM)
ANY = pl.BlockSpec(memory_space=pl.ANY)
MIB = 1024 * 1024


def shape(*dims):
    return jax.ShapeDtypeStruct(dims, F32)


def call(kernel, name, out_shape, in_specs, scratch=(), flops=1_000_000):
    return pl.pallas_call(
        kernel,
        out_shape=out_shape,
        in_specs=in_specs,
        out_specs=jax.tree.map(lambda _: VMEM, out_shape),
        scratch_shapes=scratch,
        compiler_params=pltpu.CompilerParams(vmem_limit_bytes=32 * MIB),
        cost_estimate=pl.CostEstimate(flops=flops, bytes_accessed=100_000, transcendentals=0),
        name=name,
    )


def swap_probes(value, step):
    return lax.ppermute(value, "probe", [(i, i ^ step) for i in range(lax.axis_size("probe"))])


def body(increments, winds, obs_weight):
    count, lons, levels, lats = increments.shape
    blocks = lons // 4
    probes = count * lax.axis_size("probe")
    ring = lax.axis_size("lon")
    up = [(i, (i + 1) % ring) for i in range(ring)]
    down = [(i, (i - 1) % ring) for i in range(ring)]
    where = lax.axis_index("probe").reshape(1).astype(jnp.int32)
    dma = pltpu.SemaphoreType.DMA
    increments, winds, obs_weight = (
        pltpu.with_memory_space_constraint(x, pltpu.HBM) for x in (increments, winds, obs_weight)
    )
    pack_up, pack_down, winds, obs_weight = call(
        pack_kernel,
        "pack",
        (
            shape(10, levels, lats),
            shape(9, levels, lats),
            shape(2, lons, levels, lats),
            shape(lons, levels, lats),
        ),
        [HBM, HBM],
        [dma((2,))],
    )(winds, obs_weight)
    from_low = lax.ppermute(pack_up, "lon", up)
    from_high = lax.ppermute(pack_down, "lon", down)
    inner, inner_other, part_low, part_high, sides = call(
        interior_kernel,
        "interior",
        (
            shape(count, (blocks - 2) * 256),
            shape(count, (blocks - 2) * 256),
            shape(count, 512),
            shape(count, 512),
            shape(count, 8, levels, lats),
        ),
        [SMEM, VMEM, VMEM, HBM],
        [
            pltpu.VMEM((PLANES, lons, levels, lats), F32),
            pltpu.VMEM((blocks, 3, 12, levels, lats), F32),
            pltpu.VMEM((6, blocks * count * 8, HALF), F32),
            pltpu.VMEM((count, lons, levels, lats), F32),
            dma((3,)),
        ],
    )(where, winds, obs_weight, increments)
    edge_scratch = [
        pltpu.VMEM((PLANES, 14, levels, lats), F32),
        pltpu.VMEM((2, 3, 12, levels, lats), F32),
        pltpu.VMEM((6, 2 * count * 8, HALF), F32),
    ]
    share, share_other = call(
        share_kernel, "share", (shape(count, 512),) * 2, [SMEM] + [VMEM] * 5, edge_scratch
    )(where, winds, obs_weight, from_low, from_high, sides)
    share = jnp.concatenate([share, swap_probes(share_other, 1)], axis=0)
    size = lax.axis_size("probe")
    arrived = lax.ppermute(
        share,
        ("lon", "probe"),
        [
            (i * size + p, (up, down)[p & 1][i][1] * size + p)
            for i in range(ring)
            for p in range(size)
        ],
    )
    rest, rest_other = call(
        rest_kernel, "rest", (shape(count, 512),) * 2, [SMEM] + [VMEM] * 7 + [ANY], edge_scratch
    )(where, winds, obs_weight, from_low, from_high, sides, part_low, part_high, share)
    inner_chip = jnp.concatenate([inner, swap_probes(inner_other, 1)], axis=0)
    inner_chip, rest = lax.optimization_barrier((inner_chip, rest))
    inner_far = swap_probes(inner_chip, 2)
    edge_chip = jnp.concatenate([rest, swap_probes(rest_other, 1)], axis=0) + arrived
    edge_far = swap_probes(edge_chip, 2)
    inner_far, edge_far = lax.optimization_barrier((inner_far, edge_far))
    panel, gram = call(
        gram_kernel,
        "gram",
        (shape(probes, blocks * 256), shape(probes // 2, 2 * probes)),
        [SMEM] + [VMEM] * 4,
    )(where, inner_chip, inner_far, edge_chip, edge_far)
    panel, gram_other = lax.optimization_barrier((panel, swap_probes(gram, 1)))
    grams = call(copies_kernel, "copies", shape(ring, probes // 2, 2 * probes), [VMEM] * 2)(
        gram, gram_other
    )
    grams = lax.all_to_all(grams, "lon", 0, 0, tiled=True)
    basis, upper = call(
        factor_kernel,
        "factor",
        (shape(blocks, count, 512), shape(probes, probes)),
        [SMEM] + [VMEM] * 3,
        [pltpu.VMEM((probes, probes), F32)],
    )(where, grams, panel, swap_probes(panel, 1))
    return basis.transpose(1, 0, 2), upper


def solution(mesh):
    in_specs = (P("probe", "lon", None, None), P(None, "lon", None, None), P("lon", None, None))
    out_specs = (P("probe", "lon", None), P())
    return jax.shard_map(body, mesh=mesh, in_specs=in_specs, out_specs=out_specs, check_vma=False)
```

```python
import functools

import jax
import jax.numpy as jnp
from jax import lax
from jax.experimental import pallas as pl
from jax.experimental.pallas import tpu as pltpu
from jax.sharding import PartitionSpec as P

F32 = jnp.float32
BF16 = jnp.bfloat16
HALF = 128
DIAG, EAST, WEST, SOUTH_UP, SOUTH_DOWN, NORTH_UP, NORTH_DOWN = range(7)
PLANES = 7


def halves(ref, *index):
    return [ref[index + (slice(None), slice(h * HALF, (h + 1) * HALF))] for h in (0, 1)]


def store(ref, value, *index):
    for h in (0, 1):
        ref[index + (slice(None), slice(h * HALF, (h + 1) * HALF))] = value[h]


class Lanes:
    def __init__(self):
        lane = lax.broadcasted_iota(jnp.int32, (8, HALF), 1)
        self.first = lane == 0
        self.last = lane == HALF - 1
        self.phase = lane & 3
        self.even = ((lane >> 2) & 1) == 0
        self.third = [lax.rem((lane + h * HALF) >> 2, 3) for h in (0, 1)]
        low = self.phase < 2
        self.near = [lax.rem(t + jnp.where(low, 2, 1), 3) for t in self.third]
        self.far = [lax.rem(t + jnp.where(low, 1, 2), 3) for t in self.third]

    def below(self, f):
        r0, r1 = pltpu.roll(f[0], 1, 1), pltpu.roll(f[1], 1, 1)
        return [r0, jnp.where(self.first, r0, r1)]

    def above(self, f):
        r0, r1 = pltpu.roll(f[0], HALF - 1, 1), pltpu.roll(f[1], HALF - 1, 1)
        return [jnp.where(self.last, r1, r0), r1]


def write_coefficients(coef, slot, u, u_next, v, lanes):
    v = [jnp.where(lanes.first, 0.0, v[0]), v[1]]
    south_up = [jnp.maximum(x, 0.0) for x in v]
    south_down = [jnp.maximum(-x, 0.0) for x in v]
    north = []
    for field in (south_up, south_down):
        r0, r1 = pltpu.roll(field[0], HALF - 1, 1), pltpu.roll(field[1], HALF - 1, 1)
        north.append([jnp.where(lanes.last, r1, r0), jnp.where(lanes.last, r0, r1)])
    east = [jnp.maximum(x, 0.0) for x in u]
    west = [jnp.maximum(-x, 0.0) for x in u]
    diag = [
        1.0 - jnp.maximum(u_next[h], 0.0) - west[h] - north[0][h] - south_down[h] for h in (0, 1)
    ]
    for plane, value in (
        (DIAG, diag),
        (EAST, east),
        (WEST, west),
        (SOUTH_UP, south_up),
        (SOUTH_DOWN, south_down),
        (NORTH_UP, north[0]),
        (NORTH_DOWN, north[1]),
    ):
        store(coef, value, plane, slot)


def stencil(lanes, field, r, get, forward):
    total = [None, None]

    def add(coefficient, value):
        for h in (0, 1):
            term = coefficient[h] * value[h]
            total[h] = term if total[h] is None else total[h] + term

    if r in field:
        here = field[r]
        add(get(DIAG, r), here)
        add(get(SOUTH_UP if forward else SOUTH_DOWN, r), lanes.below(here))
        add(get(NORTH_DOWN if forward else NORTH_UP, r), lanes.above(here))
    if r - 1 in field:
        add(get(EAST if forward else WEST, r), field[r - 1])
    if r + 1 in field:
        add(get(WEST if forward else EAST, r + 1), field[r + 1])
    return total


def block_weights(lanes, get, get_obs, first, last):
    state = [{}, {}]
    for r in range(max(first - 3, -1), min(last + 3, 4) + 1):
        if r == -1:
            own = get(WEST, 0)
            other = None
        elif r == 4:
            own = get(EAST, 4)
            other = None
        else:
            own = get(DIAG, r)
            if r > 0:
                own = [x + y for x, y in zip(own, get(EAST, r))]
            if r < 3:
                own = [x + y for x, y in zip(own, get(WEST, r + 1))]
            south, north = get(SOUTH_UP, r), get(NORTH_DOWN, r)
            inner_south = [jnp.where(lanes.phase == 0, 0.0, x) for x in south]
            inner_north = [jnp.where(lanes.phase == 3, 0.0, x) for x in north]
            own = [x + y + z for x, y, z in zip(own, inner_south, inner_north)]
            other = [
                jnp.where(lanes.phase == 0, x, jnp.where(lanes.phase == 3, y, 0.0))
                for x, y in zip(south, north)
            ]
        for colour in (0, 1):
            mine = lanes.even if colour == 0 else jnp.logical_not(lanes.even)
            state[colour][r] = [
                jnp.where(mine, own[h], 0.0 if other is None else other[h]) for h in (0, 1)
            ]
    wide = [{}, {}, {}]
    for r in range(max(first - 2, -2), min(last + 2, 5) + 1):
        obs = get_obs(r)
        pair = [stencil(lanes, state[colour], r, get, True) for colour in (0, 1)]
        pair = [[obs[h] * value[h] for h in (0, 1)] for value in pair]
        own = [jnp.where(lanes.even, pair[0][h], pair[1][h]) for h in (0, 1)]
        other = [jnp.where(lanes.even, pair[1][h], pair[0][h]) for h in (0, 1)]
        for colour in range(3):
            wide[colour][r] = [
                jnp.where(
                    lanes.third[h] == colour,
                    own[h],
                    jnp.where(lanes.near[h] == colour, other[h], 0.0),
                )
                for h in (0, 1)
            ]
    once = [
        {
            r: stencil(lanes, wide[colour], r, get, False)
            for r in range(max(first - 1, -3), min(last + 1, 6) + 1)
        }
        for colour in range(3)
    ]
    weights = {}
    for r in range(first, last + 1):
        twice = [stencil(lanes, once[colour], r, get, False) for colour in range(3)]

        def pick(index):
            return [
                jnp.where(
                    index[h] == 0, twice[0][h], jnp.where(index[h] == 1, twice[1][h], twice[2][h])
                )
                for h in (0, 1)
            ]

        own = pick(lanes.third)
        if 0 <= r <= 3:
            own = [x + 1.0 for x in own]
        weights[r, 0] = own
        if -3 <= r <= 6:
            weights[r, 1] = pick(lanes.near)
        if -1 <= r <= 4:
            weights[r, 2] = pick(lanes.far)
    return weights


def apply_weights(lanes, keys, read_weight, read_field, write, probes):
    sums = {}
    for r in sorted({r for r, _ in keys}):
        fields = [read_field(probe, r) for probe in probes]
        for part in range(3):
            if (r, part) not in keys:
                continue
            weight = read_weight(r, part)
            for n in range(len(probes)):
                for h in (0, 1):
                    term = weight[h] * fields[n][h]
                    key = (n, part, h)
                    sums[key] = sums[key] + term if key in sums else term
    low = lanes.phase < 2
    for n, probe in enumerate(probes):
        own, near, far = ([sums.get((n, part, h)) for h in (0, 1)] for part in range(3))
        if far[0] is None:
            down = [jnp.where(low, x, 0.0) for x in near]
            up = [jnp.where(low, 0.0, x) for x in near]
        else:
            down = [jnp.where(low, x, y) for x, y in zip(near, far)]
            up = [jnp.where(low, y, x) for x, y in zip(near, far)]
        for h in (0, 1):
            write(probe, 0, h, own[h])
            write(probe, 1, h, down[h])
            write(probe, 2, h, up[h])


def pooling(parity):
    row = lax.broadcasted_iota(jnp.int32, (256, HALF), 0)
    column = lax.broadcasted_iota(jnp.int32, (256, HALF), 1)
    return jnp.where((row >> 2) + 64 * parity == column, 1.0 / 16.0, 0.0).astype(BF16)


def split3(x):
    high = x.astype(BF16)
    rest = x - high.astype(F32)
    middle = rest.astype(BF16)
    low = (rest - middle.astype(F32)).astype(BF16)
    return high, middle, low


def pool_into(lanes, sums, rows, count, write):
    total = None
    for parity in (0, 1):
        matrix = pooling(parity)
        own, down, up = (
            [
                jnp.concatenate(
                    [
                        sums[2 * part + h, pl.ds(n * count * 8 + 2 * pair + parity, count, stride=8), :]
                        for n in range(rows)
                        for pair in range(4)
                    ],
                    axis=0,
                )
                for h in (0, 1)
            ]
            for part in range(3)
        )
        lane = lax.broadcasted_iota(jnp.int32, own[0].shape, 1)
        d0, d1 = (pltpu.roll(x, HALF - 4, 1) for x in down)
        u0, u1 = (pltpu.roll(x, 4, 1) for x in up)
        low = own[0] + (jnp.where(lane >= HALF - 4, d1, d0) + jnp.where(lane < 4, u1, u0))
        high = own[1] + (jnp.where(lane >= HALF - 4, d0, d1) + jnp.where(lane < 4, u0, u1))
        for part in split3(jnp.concatenate([low, high], axis=1)):
            term = jnp.dot(part, matrix, preferred_element_type=F32)
            total = term if total is None else total + term
    for n in range(rows):
        for pair in range(4):
            start = (n * 4 + pair) * count
            write(n, pair, total[start : start + count])


GROUP = 8
EDGE_GROUP = 16


def weight_keys(first, last):
    reach = {0: (-4, 7), 1: (-3, 6), 2: (-1, 4)}
    return [
        (r, part)
        for part, (low, high) in reach.items()
        for r in range(max(first, low), min(last, high) + 1)
    ]


def fetch_all(copies):
    for copy in copies:
        copy.start()
    return copies


def pack_kernel(winds_hbm, obs_hbm, up, down, winds, obs, sems):
    lons = obs.shape[0]
    copies = fetch_all(
        [
            pltpu.make_async_copy(winds_hbm, winds, sems.at[0]),
            pltpu.make_async_copy(obs_hbm, obs, sems.at[1]),
        ]
    )
    for copy in copies:
        copy.wait()
    up[0:3] = winds[0, lons - 3 :]
    up[3:6] = winds[1, lons - 3 :]
    up[6:8] = obs[lons - 2 :]
    up[8:10] = obs[lons - 2 :]
    down[0:4] = winds[0, 0:4]
    down[4:7] = winds[1, 0:3]
    down[7:9] = obs[0:2]


def split_by_core(where, values, mine, other):
    first = lax.rem(where[0], 2) == 0
    for pair in range(mine.shape[1] // HALF):
        columns = slice(pair * HALF, (pair + 1) * HALF)
        a, b = values[0, pair], values[1, pair]
        mine[:, columns] = jnp.where(first, a, b)
        other[:, columns] = jnp.where(first, b, a)


def interior_kernel(
    where, winds, obs, field_hbm, mine, other, part_low, part_high, sides,
    coef, weights, sums, field, sems,
):
    count, lons = field.shape[0], field.shape[1]
    blocks = lons // 4
    field_copy = pltpu.make_async_copy(field_hbm, field, sems.at[0])
    field_copy.start()
    side_copies = [
        pltpu.make_async_copy(
            field_hbm.at[:, pl.ds(start, 4)], sides.at[:, pl.ds(4 * n, 4)], sems.at[1 + n]
        )
        for n, start in enumerate((0, lons - 4))
    ]
    for copy in side_copies:
        copy.start()
    lanes = Lanes()

    def coefficients(lon, carry):
        write_coefficients(
            coef,
            lon,
            halves(winds, 0, lon),
            halves(winds, 0, jnp.minimum(lon + 1, lons - 1)),
            halves(winds, 1, lon),
            lanes,
        )
        return carry

    lax.fori_loop(0, lons, coefficients, 0, unroll=8)

    def weigh(first, last, block, carry):
        base = block * 4

        def get(plane, r):
            return halves(coef, plane, base + r)

        result = block_weights(lanes, get, lambda r: halves(obs, base + r), first, last)
        for (r, part), value in result.items():
            store(weights, value, block, part, r + 4)
        return carry

    spans = ((0, 1, 2, 7), (1, blocks - 1, -4, 7), (blocks - 1, blocks, -4, -1))
    for start, stop, first, last in spans:
        lax.fori_loop(start, stop, functools.partial(weigh, first, last), 0, unroll=stop - start)
    field_copy.wait()
    groups = count // GROUP

    def sweep(first, last, step, carry):
        block = step // groups
        start = (step % groups) * GROUP

        def write(probe, part, h, value):
            row = pl.multiple_of((block * count + probe) * 8, 8)
            sums[2 * part + h, pl.ds(row, 8), :] = value

        apply_weights(
            lanes,
            weight_keys(first, last),
            lambda r, part: halves(weights, block, part, r + 4),
            lambda probe, r: halves(field, probe, block * 4 + r),
            write,
            [start + n for n in range(GROUP)],
        )
        return carry

    for start, stop, first, last in spans:
        lax.fori_loop(start * groups, stop * groups, functools.partial(sweep, first, last), 0)

    def put(n, pair, value):
        if n == 0:
            part_low[:, pair * HALF : (pair + 1) * HALF] = value
        elif n == blocks - 1:
            part_high[:, pair * HALF : (pair + 1) * HALF] = value
        else:
            values[divmod((n - 1) * 4 + pair, pieces)] = value

    values = {}
    pieces = mine.shape[1] // HALF
    pool_into(lanes, sums, blocks, count, put)
    split_by_core(where, values, mine, other)
    for copy in side_copies:
        copy.wait()


def edge_sums(winds, obs, from_low, from_high, field, coef, weights, sums, spans, jobs, put):
    count, lons = field.shape[0], obs.shape[0]
    lanes = Lanes()

    def wind(which, lon):
        if lon < 0:
            return halves(from_low, 3 * which + lon + 3)
        if lon >= lons:
            return halves(from_high, min(4 * which + lon - lons, 6))
        return halves(winds, which, lon)

    def weight_at(lon):
        if lon < 0:
            return halves(from_low, 6 + lon + 2)
        if lon >= lons:
            return halves(from_high, 7 + lon - lons)
        return halves(obs, lon)

    slots = {}
    for start, stop in spans:
        for lon in range(start, stop + 1):
            slots[lon] = len(slots)
            write_coefficients(
                coef, slots[lon], wind(0, lon), wind(0, min(lon + 1, stop)), wind(1, lon), lanes
            )
    for n, (base, first, last) in enumerate(jobs):
        result = block_weights(
            lanes,
            lambda plane, r: halves(coef, plane, slots[base + r]),
            lambda r: weight_at(base + r),
            first,
            last,
        )
        for (r, part), value in result.items():
            store(weights, value, n, part, r + 4)

    def sweep(step, carry):
        for n, (base, first, last) in enumerate(jobs):

            def write(probe, part, h, value):
                row = pl.multiple_of((n * count + probe) * 8, 8)
                sums[2 * part + h, pl.ds(row, 8), :] = value

            def read(probe, r):
                lon = base + r
                return halves(field, probe, lon if lon < 4 else lon - (lons - 8))

            apply_weights(
                lanes,
                weight_keys(first, last),
                lambda r, part: halves(weights, n, part, r + 4),
                read,
                write,
                [step * EDGE_GROUP + k for k in range(EDGE_GROUP)],
            )
        return carry

    lax.fori_loop(0, count // EDGE_GROUP, sweep, 0)
    pool_into(lanes, sums, len(jobs), count, put)


def share_kernel(
    where, winds, obs, from_low, from_high, field, mine, other, coef, weights, sums
):
    lons = obs.shape[0]
    values = {}

    def put(n, pair, value):
        values[1 - n, pair] = value

    edge_sums(
        winds, obs, from_low, from_high, field, coef, weights, sums,
        ((-3, 3), (lons - 3, lons + 3)),
        ((-4, 4, 7), (lons, -4, -1)),
        put,
    )
    split_by_core(where, values, mine, other)


def rest_kernel(
    where, winds, obs, from_low, from_high, field, part_low, part_high, after,
    mine, other, coef, weights, sums,
):
    lons = obs.shape[0]
    values = {}

    def put(n, pair, value):
        columns = slice(pair * HALF, (pair + 1) * HALF)
        values[n, pair] = value + (part_low, part_high)[n][:, columns]

    edge_sums(
        winds, obs, from_low, from_high, field, coef, weights, sums,
        ((-2, 4), (lons - 5, lons + 1)),
        ((0, 0, 1), (lons - 4, 0, 3)),
        put,
    )
    split_by_core(where, values, mine, other)


def self_product(panel):
    return lax.dot_general(
        panel,
        panel,
        (((1,), (1,)), ((), ())),
        precision=lax.Precision.HIGHEST,
        preferred_element_type=F32,
    )


def assemble(where, chip, far, panel):
    rows = chip.shape[0] // 2
    for k in range(4):
        at = pl.multiple_of(lax.bitwise_xor(where[0], jnp.int32(k)) * rows, 8)
        panel[pl.ds(at, rows)] = (chip, far)[k // 2][(k % 2) * rows : (k % 2 + 1) * rows]


def inner_gram_kernel(where, chip, far, out, panel):
    assemble(where, chip, far, panel)
    out[...] = self_product(panel[...])


def gram_kernel(where, inner_gram, inner_chip, inner_far, edge_chip, edge_far, panel, out):
    width = inner_chip.shape[1]
    assemble(where, edge_chip, edge_far, panel.at[:, width:])
    gram = self_product(panel[:, width:]) + inner_gram[...]
    half = gram.shape[0] // 2
    out[...] = jnp.concatenate([gram[:half], gram[half:]], axis=1)
    assemble(where, inner_chip, inner_far, panel.at[:, :width])


def copies_kernel(mine, other, out):
    total = mine[...] + other[...]
    for n in range(out.shape[0]):
        out[n] = total


def factor_kernel(
    where, grams, panel, panel_other, basis, upper, inverse
):
    packed = grams[0]
    for n in range(1, grams.shape[0]):
        packed = packed + grams[n]
    size = 2 * packed.shape[0]
    gram = jnp.concatenate([packed[:, :size], packed[:, size:]], axis=0)
    row = lax.broadcasted_iota(jnp.int32, (size, size), 0)
    column = lax.broadcasted_iota(jnp.int32, (size, size), 1)
    state = jnp.concatenate([gram, jnp.where(row == column, 1.0, 0.0).astype(F32)], axis=1)
    tiles = [state[8 * t : 8 * t + 8] for t in range(size // 8)]
    full = (8, 2 * size)
    sub = lax.broadcasted_iota(jnp.int32, full, 0)
    scales = []
    for own in range(size // 8):
        spread = {
            (t, j): jnp.broadcast_to(tiles[t][:, 8 * own + j : 8 * own + j + 1], full)
            for t in range(own, size // 8)
            for j in range(8)
        }
        pivots = {
            (i, j): jnp.broadcast_to(spread[own, j][i : i + 1], full)
            for i in range(8)
            for j in range(i + 1)
        }
        rows = [jnp.broadcast_to(tiles[own][j : j + 1], full) for j in range(8)]
        inverses = []
        for j in range(8):
            inverses.append(1.0 / pivots[j, j])
            scales.append(lax.rsqrt(pivots[j, j]))
            for i in range(j + 1, 8):
                ratio = pivots[i, j] * inverses[j]
                for m in range(i, 8):
                    pivots[m, i] = pivots[m, i] - ratio * pivots[m, j]
                rows[i] = rows[i] - ratio * rows[j]
                for t in range(own + 1, size // 8):
                    spread[t, i] = spread[t, i] - ratio * spread[t, j]
        for t in range(own + 1, size // 8):
            update = (spread[t, 0] * inverses[0]) * rows[0]
            for j in range(1, 8):
                update = update + (spread[t, j] * inverses[j]) * rows[j]
            tiles[t] = tiles[t] - update
        for j in range(8):
            tiles[own] = jnp.where(sub == j, rows[j], tiles[own])
    for t in range(size // 8):
        scale = scales[8 * t]
        for at in range(1, 8):
            scale = jnp.where(sub == at, scales[8 * t + at], scale)
        scaled = tiles[t] * scale
        column = lax.broadcasted_iota(jnp.int32, (8, size), 1)
        here = lax.broadcasted_iota(jnp.int32, (8, size), 0) + 8 * t
        upper[8 * t : 8 * t + 8] = jnp.where(column >= here, scaled[:, :size], 0.0)
        inverse[8 * t : 8 * t + 8] = scaled[:, size:]
    blocks, count, width = basis.shape
    own_rows = inverse[pl.ds(pl.multiple_of(where[0] * count, 8), count)]

    def project(columns):
        return jnp.dot(
            own_rows, columns, precision=lax.Precision.HIGHEST, preferred_element_type=F32
        )

    core = lax.rem(where[0], 2)
    half = (blocks - 2) // 2

    for side, part in ((core, panel), (1 - core, panel_other)):
        for n in range(half):
            basis[1 + side * half + n] = project(part[:, n * width : (n + 1) * width])
        basis[side * (blocks - 1)] = project(part[:, half * width :])


VMEM = pl.BlockSpec(memory_space=pltpu.VMEM)
SMEM = pl.BlockSpec(memory_space=pltpu.SMEM)
HBM = pl.BlockSpec(memory_space=pltpu.HBM)
ANY = pl.BlockSpec(memory_space=pl.ANY)
MIB = 1024 * 1024


def shape(*dims):
    return jax.ShapeDtypeStruct(dims, F32)


def call(kernel, name, out_shape, in_specs, scratch=(), flops=1_000_000):
    return pl.pallas_call(
        kernel,
        out_shape=out_shape,
        in_specs=in_specs,
        out_specs=jax.tree.map(lambda _: VMEM, out_shape),
        scratch_shapes=scratch,
        compiler_params=pltpu.CompilerParams(vmem_limit_bytes=32 * MIB),
        cost_estimate=pl.CostEstimate(flops=flops, bytes_accessed=100_000, transcendentals=0),
        name=name,
    )


def swap_probes(value, step):
    return lax.ppermute(value, "probe", [(i, i ^ step) for i in range(lax.axis_size("probe"))])


def body(increments, winds, obs_weight):
    count, lons, levels, lats = increments.shape
    blocks = lons // 4
    probes = count * lax.axis_size("probe")
    ring = lax.axis_size("lon")
    up = [(i, (i + 1) % ring) for i in range(ring)]
    down = [(i, (i - 1) % ring) for i in range(ring)]
    where = lax.axis_index("probe").reshape(1).astype(jnp.int32)
    dma = pltpu.SemaphoreType.DMA
    increments, winds, obs_weight = (
        pltpu.with_memory_space_constraint(x, pltpu.HBM) for x in (increments, winds, obs_weight)
    )
    pack_up, pack_down, winds, obs_weight = call(
        pack_kernel,
        "pack",
        (
            shape(10, levels, lats),
            shape(9, levels, lats),
            shape(2, lons, levels, lats),
            shape(lons, levels, lats),
        ),
        [HBM, HBM],
        [dma((2,))],
    )(winds, obs_weight)
    from_low = lax.ppermute(pack_up, "lon", up)
    from_high = lax.ppermute(pack_down, "lon", down)
    inner, inner_other, part_low, part_high, sides = call(
        interior_kernel,
        "interior",
        (
            shape(count, (blocks - 2) * 256),
            shape(count, (blocks - 2) * 256),
            shape(count, 512),
            shape(count, 512),
            shape(count, 8, levels, lats),
        ),
        [SMEM, VMEM, VMEM, HBM],
        [
            pltpu.VMEM((PLANES, lons, levels, lats), F32),
            pltpu.VMEM((blocks, 3, 12, levels, lats), F32),
            pltpu.VMEM((6, blocks * count * 8, HALF), F32),
            pltpu.VMEM((count, lons, levels, lats), F32),
            dma((3,)),
        ],
    )(where, winds, obs_weight, increments)
    edge_scratch = [
        pltpu.VMEM((PLANES, 14, levels, lats), F32),
        pltpu.VMEM((2, 3, 12, levels, lats), F32),
        pltpu.VMEM((6, 2 * count * 8, HALF), F32),
    ]
    share, share_other = call(
        share_kernel, "share", (shape(count, 512),) * 2, [SMEM] + [VMEM] * 5, edge_scratch
    )(where, winds, obs_weight, from_low, from_high, sides)
    share = jnp.concatenate([share, swap_probes(share_other, 1)], axis=0)
    size = lax.axis_size("probe")
    arrived = lax.ppermute(
        share,
        ("lon", "probe"),
        [
            (i * size + p, (up, down)[p & 1][i][1] * size + p)
            for i in range(ring)
            for p in range(size)
        ],
    )
    rest, rest_other = call(
        rest_kernel, "rest", (shape(count, 512),) * 2, [SMEM] + [VMEM] * 7 + [ANY], edge_scratch
    )(where, winds, obs_weight, from_low, from_high, sides, part_low, part_high, share)
    inner_chip = jnp.concatenate([inner, swap_probes(inner_other, 1)], axis=0)
    inner_far = swap_probes(inner_chip, 2)
    inner_gram = call(
        inner_gram_kernel,
        "inner_gram",
        shape(probes, probes),
        [SMEM, VMEM, VMEM],
        [pltpu.VMEM((probes, (blocks - 2) * 256), F32)],
    )(where, inner_chip, inner_far)
    edge_chip = jnp.concatenate([rest, swap_probes(rest_other, 1)], axis=0) + arrived
    edge_far = swap_probes(edge_chip, 2)
    panel, gram = call(
        gram_kernel,
        "gram",
        (shape(probes, blocks * 256), shape(probes // 2, 2 * probes)),
        [SMEM] + [VMEM] * 5,
    )(where, inner_gram, inner_chip, inner_far, edge_chip, edge_far)
    panel, gram_other = lax.optimization_barrier((panel, swap_probes(gram, 1)))
    grams = call(copies_kernel, "copies", shape(ring, probes // 2, 2 * probes), [VMEM] * 2)(
        gram, gram_other
    )
    grams = lax.all_to_all(grams, "lon", 0, 0, tiled=True)
    basis, upper = call(
        factor_kernel,
        "factor",
        (shape(blocks, count, 512), shape(probes, probes)),
        [SMEM] + [VMEM] * 3,
        [pltpu.VMEM((probes, probes), F32)],
    )(where, grams, panel, swap_probes(panel, 1))
    return basis.transpose(1, 0, 2), upper


def solution(mesh):
    in_specs = (P("probe", "lon", None, None), P(None, "lon", None, None), P("lon", None, None))
    out_specs = (P("probe", "lon", None), P())
    return jax.shard_map(body, mesh=mesh, in_specs=in_specs, out_specs=out_specs, check_vma=False)
```

```python
import functools

import jax
import jax.numpy as jnp
from jax import lax
from jax.experimental import pallas as pl
from jax.experimental.pallas import tpu as pltpu
from jax.sharding import PartitionSpec as P

F32 = jnp.float32
BF16 = jnp.bfloat16
HALF = 128
DIAG, EAST, WEST, SOUTH_UP, SOUTH_DOWN, NORTH_UP, NORTH_DOWN = range(7)
PLANES = 7


def halves(ref, *index):
    return [ref[index + (slice(None), slice(h * HALF, (h + 1) * HALF))] for h in (0, 1)]


def store(ref, value, *index):
    for h in (0, 1):
        ref[index + (slice(None), slice(h * HALF, (h + 1) * HALF))] = value[h]


class Lanes:
    def __init__(self):
        lane = lax.broadcasted_iota(jnp.int32, (8, HALF), 1)
        self.first = lane == 0
        self.last = lane == HALF - 1
        self.phase = lane & 3
        self.even = ((lane >> 2) & 1) == 0
        self.third = [lax.rem((lane + h * HALF) >> 2, 3) for h in (0, 1)]
        low = self.phase < 2
        self.near = [lax.rem(t + jnp.where(low, 2, 1), 3) for t in self.third]
        self.far = [lax.rem(t + jnp.where(low, 1, 2), 3) for t in self.third]

    def below(self, f):
        r0, r1 = pltpu.roll(f[0], 1, 1), pltpu.roll(f[1], 1, 1)
        return [r0, jnp.where(self.first, r0, r1)]

    def above(self, f):
        r0, r1 = pltpu.roll(f[0], HALF - 1, 1), pltpu.roll(f[1], HALF - 1, 1)
        return [jnp.where(self.last, r1, r0), r1]


def write_coefficients(coef, slot, u, u_next, v, lanes):
    v = [jnp.where(lanes.first, 0.0, v[0]), v[1]]
    south_up = [jnp.maximum(x, 0.0) for x in v]
    south_down = [jnp.maximum(-x, 0.0) for x in v]
    north = []
    for field in (south_up, south_down):
        r0, r1 = pltpu.roll(field[0], HALF - 1, 1), pltpu.roll(field[1], HALF - 1, 1)
        north.append([jnp.where(lanes.last, r1, r0), jnp.where(lanes.last, r0, r1)])
    east = [jnp.maximum(x, 0.0) for x in u]
    west = [jnp.maximum(-x, 0.0) for x in u]
    diag = [
        1.0 - jnp.maximum(u_next[h], 0.0) - west[h] - north[0][h] - south_down[h] for h in (0, 1)
    ]
    for plane, value in (
        (DIAG, diag),
        (EAST, east),
        (WEST, west),
        (SOUTH_UP, south_up),
        (SOUTH_DOWN, south_down),
        (NORTH_UP, north[0]),
        (NORTH_DOWN, north[1]),
    ):
        store(coef, value, plane, slot)


def stencil(lanes, field, r, get, forward):
    total = [None, None]

    def add(coefficient, value):
        for h in (0, 1):
            term = coefficient[h] * value[h]
            total[h] = term if total[h] is None else total[h] + term

    if r in field:
        here = field[r]
        add(get(DIAG, r), here)
        add(get(SOUTH_UP if forward else SOUTH_DOWN, r), lanes.below(here))
        add(get(NORTH_DOWN if forward else NORTH_UP, r), lanes.above(here))
    if r - 1 in field:
        add(get(EAST if forward else WEST, r), field[r - 1])
    if r + 1 in field:
        add(get(WEST if forward else EAST, r + 1), field[r + 1])
    return total


def block_weights(lanes, get, get_obs, first, last):
    state = [{}, {}]
    for r in range(max(first - 3, -1), min(last + 3, 4) + 1):
        if r == -1:
            own = get(WEST, 0)
            other = None
        elif r == 4:
            own = get(EAST, 4)
            other = None
        else:
            own = get(DIAG, r)
            if r > 0:
                own = [x + y for x, y in zip(own, get(EAST, r))]
            if r < 3:
                own = [x + y for x, y in zip(own, get(WEST, r + 1))]
            south, north = get(SOUTH_UP, r), get(NORTH_DOWN, r)
            inner_south = [jnp.where(lanes.phase == 0, 0.0, x) for x in south]
            inner_north = [jnp.where(lanes.phase == 3, 0.0, x) for x in north]
            own = [x + y + z for x, y, z in zip(own, inner_south, inner_north)]
            other = [
                jnp.where(lanes.phase == 0, x, jnp.where(lanes.phase == 3, y, 0.0))
                for x, y in zip(south, north)
            ]
        for colour in (0, 1):
            mine = lanes.even if colour == 0 else jnp.logical_not(lanes.even)
            state[colour][r] = [
                jnp.where(mine, own[h], 0.0 if other is None else other[h]) for h in (0, 1)
            ]
    wide = [{}, {}, {}]
    for r in range(max(first - 2, -2), min(last + 2, 5) + 1):
        obs = get_obs(r)
        pair = [stencil(lanes, state[colour], r, get, True) for colour in (0, 1)]
        pair = [[obs[h] * value[h] for h in (0, 1)] for value in pair]
        own = [jnp.where(lanes.even, pair[0][h], pair[1][h]) for h in (0, 1)]
        other = [jnp.where(lanes.even, pair[1][h], pair[0][h]) for h in (0, 1)]
        for colour in range(3):
            wide[colour][r] = [
                jnp.where(
                    lanes.third[h] == colour,
                    own[h],
                    jnp.where(lanes.near[h] == colour, other[h], 0.0),
                )
                for h in (0, 1)
            ]
    once = [
        {
            r: stencil(lanes, wide[colour], r, get, False)
            for r in range(max(first - 1, -3), min(last + 1, 6) + 1)
        }
        for colour in range(3)
    ]
    weights = {}
    for r in range(first, last + 1):
        twice = [stencil(lanes, once[colour], r, get, False) for colour in range(3)]

        def pick(index):
            return [
                jnp.where(
                    index[h] == 0, twice[0][h], jnp.where(index[h] == 1, twice[1][h], twice[2][h])
                )
                for h in (0, 1)
            ]

        own = pick(lanes.third)
        if 0 <= r <= 3:
            own = [x + 1.0 for x in own]
        weights[r, 0] = own
        if -3 <= r <= 6:
            weights[r, 1] = pick(lanes.near)
        if -1 <= r <= 4:
            weights[r, 2] = pick(lanes.far)
    return weights


def apply_weights(lanes, keys, read_weight, read_field, write, probes):
    sums = {}
    for r in sorted({r for r, _ in keys}):
        fields = [read_field(probe, r) for probe in probes]
        for part in range(3):
            if (r, part) not in keys:
                continue
            weight = read_weight(r, part)
            for n in range(len(probes)):
                for h in (0, 1):
                    term = weight[h] * fields[n][h]
                    key = (n, part, h)
                    sums[key] = sums[key] + term if key in sums else term
    low = lanes.phase < 2
    for n, probe in enumerate(probes):
        own, near, far = ([sums.get((n, part, h)) for h in (0, 1)] for part in range(3))
        if far[0] is None:
            down = [jnp.where(low, x, 0.0) for x in near]
            up = [jnp.where(low, 0.0, x) for x in near]
        else:
            down = [jnp.where(low, x, y) for x, y in zip(near, far)]
            up = [jnp.where(low, y, x) for x, y in zip(near, far)]
        for h in (0, 1):
            write(probe, 0, h, own[h])
            write(probe, 1, h, down[h])
            write(probe, 2, h, up[h])


def pooling(parity):
    row = lax.broadcasted_iota(jnp.int32, (256, HALF), 0)
    column = lax.broadcasted_iota(jnp.int32, (256, HALF), 1)
    return jnp.where((row >> 2) + 64 * parity == column, 1.0 / 16.0, 0.0).astype(BF16)


def split3(x):
    high = x.astype(BF16)
    rest = x - high.astype(F32)
    middle = rest.astype(BF16)
    low = (rest - middle.astype(F32)).astype(BF16)
    return high, middle, low


def pool_into(lanes, sums, rows, count, write):
    total = None
    for parity in (0, 1):
        matrix = pooling(parity)
        own, down, up = (
            [
                jnp.concatenate(
                    [
                        sums[2 * part + h, pl.ds(n * count * 8 + 2 * pair + parity, count, stride=8), :]
                        for n in range(rows)
                        for pair in range(4)
                    ],
                    axis=0,
                )
                for h in (0, 1)
            ]
            for part in range(3)
        )
        lane = lax.broadcasted_iota(jnp.int32, own[0].shape, 1)
        d0, d1 = (pltpu.roll(x, HALF - 4, 1) for x in down)
        u0, u1 = (pltpu.roll(x, 4, 1) for x in up)
        low = own[0] + (jnp.where(lane >= HALF - 4, d1, d0) + jnp.where(lane < 4, u1, u0))
        high = own[1] + (jnp.where(lane >= HALF - 4, d0, d1) + jnp.where(lane < 4, u0, u1))
        for part in split3(jnp.concatenate([low, high], axis=1)):
            term = jnp.dot(part, matrix, preferred_element_type=F32)
            total = term if total is None else total + term
    for n in range(rows):
        for pair in range(4):
            start = (n * 4 + pair) * count
            write(n, pair, total[start : start + count])


GROUP = 8
EDGE_GROUP = 16


def weight_keys(first, last):
    reach = {0: (-4, 7), 1: (-3, 6), 2: (-1, 4)}
    return [
        (r, part)
        for part, (low, high) in reach.items()
        for r in range(max(first, low), min(last, high) + 1)
    ]


def fetch_all(copies):
    for copy in copies:
        copy.start()
    return copies


def pack_kernel(
    where, winds_hbm, obs_hbm, field_hbm, up, down, winds, obs, lent, sems
):
    lons = obs.shape[0]
    outer = field_hbm.at[:, pl.ds(lax.rem(where[0], 2) * (lons - 4), 4)]
    copies = fetch_all(
        [
            pltpu.make_async_copy(winds_hbm, winds, sems.at[0]),
            pltpu.make_async_copy(obs_hbm, obs, sems.at[1]),
            pltpu.make_async_copy(outer, lent, sems.at[2]),
        ]
    )
    for copy in copies:
        copy.wait()
    up[0:3] = winds[0, lons - 3 :]
    up[3:6] = winds[1, lons - 3 :]
    up[6:8] = obs[lons - 2 :]
    up[8:10] = obs[lons - 2 :]
    down[0:4] = winds[0, 0:4]
    down[4:7] = winds[1, 0:3]
    down[7:9] = obs[0:2]


def split_by_core(where, values, mine, other):
    first = lax.rem(where[0], 2) == 0
    for pair in range(mine.shape[1] // HALF):
        columns = slice(pair * HALF, (pair + 1) * HALF)
        a, b = values[0, pair], values[1, pair]
        mine[:, columns] = jnp.where(first, a, b)
        other[:, columns] = jnp.where(first, b, a)


def interior_kernel(
    where, winds, obs, field_hbm, after, mine, other, part_low, part_high, sides,
    coef, weights, sums, field, sems,
):
    count, lons = field.shape[0], field.shape[1]
    blocks = lons // 4
    field_copy = pltpu.make_async_copy(field_hbm, field, sems.at[0])
    field_copy.start()
    side_copies = [
        pltpu.make_async_copy(
            field_hbm.at[:, pl.ds(start, 4)], sides.at[:, pl.ds(4 * n, 4)], sems.at[1 + n]
        )
        for n, start in enumerate((0, lons - 4))
    ]
    for copy in side_copies:
        copy.start()
    lanes = Lanes()

    def coefficients(lon, carry):
        write_coefficients(
            coef,
            lon,
            halves(winds, 0, lon),
            halves(winds, 0, jnp.minimum(lon + 1, lons - 1)),
            halves(winds, 1, lon),
            lanes,
        )
        return carry

    lax.fori_loop(0, lons, coefficients, 0, unroll=8)

    def weigh(first, last, block, carry):
        base = block * 4

        def get(plane, r):
            return halves(coef, plane, base + r)

        result = block_weights(lanes, get, lambda r: halves(obs, base + r), first, last)
        for (r, part), value in result.items():
            store(weights, value, block, part, r + 4)
        return carry

    spans = ((0, 1, 2, 7), (1, blocks - 1, -4, 7), (blocks - 1, blocks, -4, -1))
    for start, stop, first, last in spans:
        lax.fori_loop(start, stop, functools.partial(weigh, first, last), 0, unroll=stop - start)
    field_copy.wait()
    groups = count // GROUP

    def sweep(first, last, step, carry):
        block = step // groups
        start = (step % groups) * GROUP

        def write(probe, part, h, value):
            row = pl.multiple_of((block * count + probe) * 8, 8)
            sums[2 * part + h, pl.ds(row, 8), :] = value

        apply_weights(
            lanes,
            weight_keys(first, last),
            lambda r, part: halves(weights, block, part, r + 4),
            lambda probe, r: halves(field, probe, block * 4 + r),
            write,
            [start + n for n in range(GROUP)],
        )
        return carry

    for start, stop, first, last in spans:
        lax.fori_loop(start * groups, stop * groups, functools.partial(sweep, first, last), 0)

    def put(n, pair, value):
        if n == 0:
            part_low[:, pair * HALF : (pair + 1) * HALF] = value
        elif n == blocks - 1:
            part_high[:, pair * HALF : (pair + 1) * HALF] = value
        else:
            values[divmod((n - 1) * 4 + pair, pieces)] = value

    values = {}
    pieces = mine.shape[1] // HALF
    pool_into(lanes, sums, blocks, count, put)
    split_by_core(where, values, mine, other)
    for copy in side_copies:
        copy.wait()


def edge_sums(winds, obs, from_low, from_high, sources, coef, weights, sums, spans, jobs, put):
    count, lons = sources[0][0].shape[0], obs.shape[0]
    total = count * len(sources)
    lanes = Lanes()

    def wind(which, lon):
        if lon < 0:
            return halves(from_low, 3 * which + lon + 3)
        if lon >= lons:
            return halves(from_high, min(4 * which + lon - lons, 6))
        return halves(winds, which, lon)

    def weight_at(lon):
        if lon < 0:
            return halves(from_low, 6 + lon + 2)
        if lon >= lons:
            return halves(from_high, 7 + lon - lons)
        return halves(obs, lon)

    slots = {}
    for start, stop in spans:
        for lon in range(start, stop + 1):
            slots[lon] = len(slots)
            write_coefficients(
                coef, slots[lon], wind(0, lon), wind(0, min(lon + 1, stop)), wind(1, lon), lanes
            )
    for n, (base, first, last) in enumerate(jobs):
        result = block_weights(
            lanes,
            lambda plane, r: halves(coef, plane, slots[base + r]),
            lambda r: weight_at(base + r),
            first,
            last,
        )
        for (r, part), value in result.items():
            store(weights, value, n, part, r + 4)

    def sweep(source, step, carry):
        field, index = sources[source]
        for n, (base, first, last) in enumerate(jobs):

            def write(probe, part, h, value):
                row = pl.multiple_of((n * total + source * count + probe) * 8, 8)
                sums[2 * part + h, pl.ds(row, 8), :] = value

            apply_weights(
                lanes,
                weight_keys(first, last),
                lambda r, part: halves(weights, n, part, r + 4),
                lambda probe, r: halves(field, probe, index(base + r)),
                write,
                [step * EDGE_GROUP + k for k in range(EDGE_GROUP)],
            )
        return carry

    for source in range(len(sources)):
        lax.fori_loop(0, count // EDGE_GROUP, functools.partial(sweep, source), 0)
    pool_into(lanes, sums, len(jobs), total, put)


def share_kernel(
    where, winds, obs, from_low, from_high, field, borrowed, out, coef, weights, sums
):
    lons = obs.shape[0]
    core = lax.rem(where[0], 2)

    def put(n, pair, value):
        out[:, pair * HALF : (pair + 1) * HALF] = value

    @pl.when(core == 0)
    def _():
        edge_sums(
            winds, obs, from_low, from_high,
            ((field, lambda lon: lon - (lons - 8)), (borrowed, lambda lon: lon - (lons - 4))),
            coef, weights, sums, ((lons - 3, lons + 3),), ((lons, -4, -1),), put,
        )

    @pl.when(core == 1)
    def _():
        edge_sums(
            winds, obs, from_low, from_high,
            ((field, lambda lon: lon), (borrowed, lambda lon: lon)),
            coef, weights, sums, ((-3, 3),), ((-4, 4, 7),), put,
        )


def rest_kernel(
    where, winds, obs, from_low, from_high, field, part_low, part_high, after, after_inner,
    mine, other, coef, weights, sums,
):
    lons = obs.shape[0]
    values = {}

    def put(n, pair, value):
        columns = slice(pair * HALF, (pair + 1) * HALF)
        values[n, pair] = value + (part_low, part_high)[n][:, columns]

    edge_sums(
        winds, obs, from_low, from_high,
        ((field, lambda lon: lon if lon < 4 else lon - (lons - 8)),),
        coef, weights, sums,
        ((-2, 4), (lons - 5, lons + 1)),
        ((0, 0, 1), (lons - 4, 0, 3)),
        put,
    )
    split_by_core(where, values, mine, other)


def self_product(panel):
    return lax.dot_general(
        panel,
        panel,
        (((1,), (1,)), ((), ())),
        precision=lax.Precision.HIGHEST,
        preferred_element_type=F32,
    )


def assemble(where, chip, far, panel):
    rows = chip.shape[0] // 2
    for k in range(4):
        at = pl.multiple_of(lax.bitwise_xor(where[0], jnp.int32(k)) * rows, 8)
        panel[pl.ds(at, rows)] = (chip, far)[k // 2][(k % 2) * rows : (k % 2 + 1) * rows]


def inner_gram_kernel(where, chip, far, out, panel):
    assemble(where, chip, far, panel)
    out[...] = self_product(panel[...])


def gram_kernel(where, inner_gram, inner_chip, inner_far, edge_chip, edge_far, panel, out):
    width = inner_chip.shape[1]
    assemble(where, edge_chip, edge_far, panel.at[:, width:])
    gram = self_product(panel[:, width:]) + inner_gram[...]
    half = gram.shape[0] // 2
    out[...] = jnp.concatenate([gram[:half], gram[half:]], axis=1)
    assemble(where, inner_chip, inner_far, panel.at[:, :width])


def copies_kernel(mine, other, out):
    total = mine[...] + other[...]
    for n in range(out.shape[0]):
        out[n] = total


def factor_kernel(
    where, grams, panel, panel_other, basis, upper, inverse
):
    packed = grams[0]
    for n in range(1, grams.shape[0]):
        packed = packed + grams[n]
    size = 2 * packed.shape[0]
    gram = jnp.concatenate([packed[:, :size], packed[:, size:]], axis=0)
    row = lax.broadcasted_iota(jnp.int32, (size, size), 0)
    column = lax.broadcasted_iota(jnp.int32, (size, size), 1)
    state = jnp.concatenate([gram, jnp.where(row == column, 1.0, 0.0).astype(F32)], axis=1)
    tiles = [state[8 * t : 8 * t + 8] for t in range(size // 8)]
    full = (8, 2 * size)
    sub = lax.broadcasted_iota(jnp.int32, full, 0)
    scales = []
    for own in range(size // 8):
        spread = {
            (t, j): jnp.broadcast_to(tiles[t][:, 8 * own + j : 8 * own + j + 1], full)
            for t in range(own, size // 8)
            for j in range(8)
        }
        pivots = {
            (i, j): jnp.broadcast_to(spread[own, j][i : i + 1], full)
            for i in range(8)
            for j in range(i + 1)
        }
        rows = [jnp.broadcast_to(tiles[own][j : j + 1], full) for j in range(8)]
        inverses = []
        for j in range(8):
            inverses.append(1.0 / pivots[j, j])
            scales.append(lax.rsqrt(pivots[j, j]))
            for i in range(j + 1, 8):
                ratio = pivots[i, j] * inverses[j]
                for m in range(i, 8):
                    pivots[m, i] = pivots[m, i] - ratio * pivots[m, j]
                rows[i] = rows[i] - ratio * rows[j]
                for t in range(own + 1, size // 8):
                    spread[t, i] = spread[t, i] - ratio * spread[t, j]
        for t in range(own + 1, size // 8):
            update = (spread[t, 0] * inverses[0]) * rows[0]
            for j in range(1, 8):
                update = update + (spread[t, j] * inverses[j]) * rows[j]
            tiles[t] = tiles[t] - update
        for j in range(8):
            tiles[own] = jnp.where(sub == j, rows[j], tiles[own])
    for t in range(size // 8):
        scale = scales[8 * t]
        for at in range(1, 8):
            scale = jnp.where(sub == at, scales[8 * t + at], scale)
        scaled = tiles[t] * scale
        column = lax.broadcasted_iota(jnp.int32, (8, size), 1)
        here = lax.broadcasted_iota(jnp.int32, (8, size), 0) + 8 * t
        upper[8 * t : 8 * t + 8] = jnp.where(column >= here, scaled[:, :size], 0.0)
        inverse[8 * t : 8 * t + 8] = scaled[:, size:]
    blocks, count, width = basis.shape
    own_rows = inverse[pl.ds(pl.multiple_of(where[0] * count, 8), count)]

    def project(columns):
        return jnp.dot(
            own_rows, columns, precision=lax.Precision.HIGHEST, preferred_element_type=F32
        )

    core = lax.rem(where[0], 2)
    half = (blocks - 2) // 2

    for side, part in ((core, panel), (1 - core, panel_other)):
        for n in range(half):
            basis[1 + side * half + n] = project(part[:, n * width : (n + 1) * width])
        basis[side * (blocks - 1)] = project(part[:, half * width :])


VMEM = pl.BlockSpec(memory_space=pltpu.VMEM)
SMEM = pl.BlockSpec(memory_space=pltpu.SMEM)
HBM = pl.BlockSpec(memory_space=pltpu.HBM)
ANY = pl.BlockSpec(memory_space=pl.ANY)
MIB = 1024 * 1024


def shape(*dims):
    return jax.ShapeDtypeStruct(dims, F32)


def call(kernel, name, out_shape, in_specs, scratch=(), flops=1_000_000):
    return pl.pallas_call(
        kernel,
        out_shape=out_shape,
        in_specs=in_specs,
        out_specs=jax.tree.map(lambda _: VMEM, out_shape),
        scratch_shapes=scratch,
        compiler_params=pltpu.CompilerParams(vmem_limit_bytes=32 * MIB),
        cost_estimate=pl.CostEstimate(flops=flops, bytes_accessed=100_000, transcendentals=0),
        name=name,
    )


def swap_probes(value, step):
    return lax.ppermute(value, "probe", [(i, i ^ step) for i in range(lax.axis_size("probe"))])


def body(increments, winds, obs_weight):
    count, lons, levels, lats = increments.shape
    blocks = lons // 4
    probes = count * lax.axis_size("probe")
    ring = lax.axis_size("lon")
    up = [(i, (i + 1) % ring) for i in range(ring)]
    down = [(i, (i - 1) % ring) for i in range(ring)]
    where = lax.axis_index("probe").reshape(1).astype(jnp.int32)
    dma = pltpu.SemaphoreType.DMA
    increments, winds, obs_weight = (
        pltpu.with_memory_space_constraint(x, pltpu.HBM) for x in (increments, winds, obs_weight)
    )
    pack_up, pack_down, winds, obs_weight, lent = call(
        pack_kernel,
        "pack",
        (
            shape(10, levels, lats),
            shape(9, levels, lats),
            shape(2, lons, levels, lats),
            shape(lons, levels, lats),
            shape(count, 4, levels, lats),
        ),
        [SMEM, HBM, HBM, HBM],
        [dma((3,))],
    )(where, winds, obs_weight, increments)
    borrowed = swap_probes(lent, 1)
    from_low = lax.ppermute(pack_up, "lon", up)
    from_high = lax.ppermute(pack_down, "lon", down)
    inner, inner_other, part_low, part_high, sides = call(
        interior_kernel,
        "interior",
        (
            shape(count, (blocks - 2) * 256),
            shape(count, (blocks - 2) * 256),
            shape(count, 512),
            shape(count, 512),
            shape(count, 8, levels, lats),
        ),
        [SMEM, VMEM, VMEM, HBM, ANY],
        [
            pltpu.VMEM((PLANES, lons, levels, lats), F32),
            pltpu.VMEM((blocks, 3, 12, levels, lats), F32),
            pltpu.VMEM((6, blocks * count * 8, HALF), F32),
            pltpu.VMEM((count, lons, levels, lats), F32),
            dma((3,)),
        ],
    )(where, winds, obs_weight, increments, borrowed)
    edge_scratch = [
        pltpu.VMEM((PLANES, 14, levels, lats), F32),
        pltpu.VMEM((2, 3, 12, levels, lats), F32),
        pltpu.VMEM((6, 2 * count * 8, HALF), F32),
    ]
    share = call(
        share_kernel, "share", shape(2 * count, 512), [SMEM] + [VMEM] * 6, edge_scratch
    )(where, winds, obs_weight, from_low, from_high, sides, borrowed)
    size = lax.axis_size("probe")
    arrived = lax.ppermute(
        share,
        ("lon", "probe"),
        [
            (i * size + p, (up, down)[p & 1][i][1] * size + p)
            for i in range(ring)
            for p in range(size)
        ],
    )
    inner_chip = jnp.concatenate([inner, swap_probes(inner_other, 1)], axis=0)
    rest, rest_other = call(
        rest_kernel, "rest", (shape(count, 512),) * 2, [SMEM] + [VMEM] * 7 + [ANY, ANY], edge_scratch
    )(where, winds, obs_weight, from_low, from_high, sides, part_low, part_high, share, inner_chip)
    inner_far = swap_probes(inner_chip, 2)
    inner_gram = call(
        inner_gram_kernel,
        "inner_gram",
        shape(probes, probes),
        [SMEM, VMEM, VMEM],
        [pltpu.VMEM((probes, (blocks - 2) * 256), F32)],
    )(where, inner_chip, inner_far)
    edge_chip = jnp.concatenate([rest, swap_probes(rest_other, 1)], axis=0) + arrived
    edge_far = swap_probes(edge_chip, 2)
    panel, gram = call(
        gram_kernel,
        "gram",
        (shape(probes, blocks * 256), shape(probes // 2, 2 * probes)),
        [SMEM] + [VMEM] * 5,
    )(where, inner_gram, inner_chip, inner_far, edge_chip, edge_far)
    panel, gram_other = lax.optimization_barrier((panel, swap_probes(gram, 1)))
    grams = call(copies_kernel, "copies", shape(ring, probes // 2, 2 * probes), [VMEM] * 2)(
        gram, gram_other
    )
    grams = lax.all_to_all(grams, "lon", 0, 0, tiled=True)
    basis, upper = call(
        factor_kernel,
        "factor",
        (shape(blocks, count, 512), shape(probes, probes)),
        [SMEM] + [VMEM] * 3,
        [pltpu.VMEM((probes, probes), F32)],
    )(where, grams, panel, swap_probes(panel, 1))
    return basis.transpose(1, 0, 2), upper


def solution(mesh):
    in_specs = (P("probe", "lon", None, None), P(None, "lon", None, None), P("lon", None, None))
    out_specs = (P("probe", "lon", None), P())
    return jax.shard_map(body, mesh=mesh, in_specs=in_specs, out_specs=out_specs, check_vma=False)
```

```python
import functools

import jax
import jax.numpy as jnp
from jax import lax
from jax.experimental import pallas as pl
from jax.experimental.pallas import tpu as pltpu
from jax.sharding import PartitionSpec as P

F32 = jnp.float32
BF16 = jnp.bfloat16
HALF = 128
DIAG, EAST, WEST, SOUTH_UP, SOUTH_DOWN, NORTH_UP, NORTH_DOWN = range(7)
PLANES = 7


def halves(ref, *index):
    return [ref[index + (slice(None), slice(h * HALF, (h + 1) * HALF))] for h in (0, 1)]


def store(ref, value, *index):
    for h in (0, 1):
        ref[index + (slice(None), slice(h * HALF, (h + 1) * HALF))] = value[h]


class Lanes:
    def __init__(self):
        lane = lax.broadcasted_iota(jnp.int32, (8, HALF), 1)
        self.first = lane == 0
        self.last = lane == HALF - 1
        self.phase = lane & 3
        self.even = ((lane >> 2) & 1) == 0
        self.third = [lax.rem((lane + h * HALF) >> 2, 3) for h in (0, 1)]
        low = self.phase < 2
        self.near = [lax.rem(t + jnp.where(low, 2, 1), 3) for t in self.third]
        self.far = [lax.rem(t + jnp.where(low, 1, 2), 3) for t in self.third]

    def below(self, f):
        r0, r1 = pltpu.roll(f[0], 1, 1), pltpu.roll(f[1], 1, 1)
        return [r0, jnp.where(self.first, r0, r1)]

    def above(self, f):
        r0, r1 = pltpu.roll(f[0], HALF - 1, 1), pltpu.roll(f[1], HALF - 1, 1)
        return [jnp.where(self.last, r1, r0), r1]


def write_coefficients(coef, slot, u, u_next, v, lanes):
    v = [jnp.where(lanes.first, 0.0, v[0]), v[1]]
    south_up = [jnp.maximum(x, 0.0) for x in v]
    south_down = [jnp.maximum(-x, 0.0) for x in v]
    north = []
    for field in (south_up, south_down):
        r0, r1 = pltpu.roll(field[0], HALF - 1, 1), pltpu.roll(field[1], HALF - 1, 1)
        north.append([jnp.where(lanes.last, r1, r0), jnp.where(lanes.last, r0, r1)])
    east = [jnp.maximum(x, 0.0) for x in u]
    west = [jnp.maximum(-x, 0.0) for x in u]
    diag = [
        1.0 - jnp.maximum(u_next[h], 0.0) - west[h] - north[0][h] - south_down[h] for h in (0, 1)
    ]
    for plane, value in (
        (DIAG, diag),
        (EAST, east),
        (WEST, west),
        (SOUTH_UP, south_up),
        (SOUTH_DOWN, south_down),
        (NORTH_UP, north[0]),
        (NORTH_DOWN, north[1]),
    ):
        store(coef, value, plane, slot)


def stencil(lanes, field, r, get, forward):
    total = [None, None]

    def add(coefficient, value):
        for h in (0, 1):
            term = coefficient[h] * value[h]
            total[h] = term if total[h] is None else total[h] + term

    if r in field:
        here = field[r]
        add(get(DIAG, r), here)
        add(get(SOUTH_UP if forward else SOUTH_DOWN, r), lanes.below(here))
        add(get(NORTH_DOWN if forward else NORTH_UP, r), lanes.above(here))
    if r - 1 in field:
        add(get(EAST if forward else WEST, r), field[r - 1])
    if r + 1 in field:
        add(get(WEST if forward else EAST, r + 1), field[r + 1])
    return total


def block_weights(lanes, get, get_obs, first, last):
    state = [{}, {}]
    for r in range(max(first - 3, -1), min(last + 3, 4) + 1):
        if r == -1:
            own = get(WEST, 0)
            other = None
        elif r == 4:
            own = get(EAST, 4)
            other = None
        else:
            own = get(DIAG, r)
            if r > 0:
                own = [x + y for x, y in zip(own, get(EAST, r))]
            if r < 3:
                own = [x + y for x, y in zip(own, get(WEST, r + 1))]
            south, north = get(SOUTH_UP, r), get(NORTH_DOWN, r)
            inner_south = [jnp.where(lanes.phase == 0, 0.0, x) for x in south]
            inner_north = [jnp.where(lanes.phase == 3, 0.0, x) for x in north]
            own = [x + y + z for x, y, z in zip(own, inner_south, inner_north)]
            other = [
                jnp.where(lanes.phase == 0, x, jnp.where(lanes.phase == 3, y, 0.0))
                for x, y in zip(south, north)
            ]
        for colour in (0, 1):
            mine = lanes.even if colour == 0 else jnp.logical_not(lanes.even)
            state[colour][r] = [
                jnp.where(mine, own[h], 0.0 if other is None else other[h]) for h in (0, 1)
            ]
    wide = [{}, {}, {}]
    for r in range(max(first - 2, -2), min(last + 2, 5) + 1):
        obs = get_obs(r)
        pair = [stencil(lanes, state[colour], r, get, True) for colour in (0, 1)]
        pair = [[obs[h] * value[h] for h in (0, 1)] for value in pair]
        own = [jnp.where(lanes.even, pair[0][h], pair[1][h]) for h in (0, 1)]
        other = [jnp.where(lanes.even, pair[1][h], pair[0][h]) for h in (0, 1)]
        for colour in range(3):
            wide[colour][r] = [
                jnp.where(
                    lanes.third[h] == colour,
                    own[h],
                    jnp.where(lanes.near[h] == colour, other[h], 0.0),
                )
                for h in (0, 1)
            ]
    once = [
        {
            r: stencil(lanes, wide[colour], r, get, False)
            for r in range(max(first - 1, -3), min(last + 1, 6) + 1)
        }
        for colour in range(3)
    ]
    weights = {}
    for r in range(first, last + 1):
        twice = [stencil(lanes, once[colour], r, get, False) for colour in range(3)]

        def pick(index):
            return [
                jnp.where(
                    index[h] == 0, twice[0][h], jnp.where(index[h] == 1, twice[1][h], twice[2][h])
                )
                for h in (0, 1)
            ]

        own = pick(lanes.third)
        if 0 <= r <= 3:
            own = [x + 1.0 for x in own]
        weights[r, 0] = own
        if -3 <= r <= 6:
            weights[r, 1] = pick(lanes.near)
        if -1 <= r <= 4:
            weights[r, 2] = pick(lanes.far)
    return weights


def apply_weights(lanes, keys, read_weight, read_field, write, probes):
    sums = {}
    for r in sorted({r for r, _ in keys}):
        fields = [read_field(probe, r) for probe in probes]
        for part in range(3):
            if (r, part) not in keys:
                continue
            weight = read_weight(r, part)
            for n in range(len(probes)):
                for h in (0, 1):
                    term = weight[h] * fields[n][h]
                    key = (n, part, h)
                    sums[key] = sums[key] + term if key in sums else term
    low = lanes.phase < 2
    for n, probe in enumerate(probes):
        own, near, far = ([sums.get((n, part, h)) for h in (0, 1)] for part in range(3))
        if far[0] is None:
            down = [jnp.where(low, x, 0.0) for x in near]
            up = [jnp.where(low, 0.0, x) for x in near]
        else:
            down = [jnp.where(low, x, y) for x, y in zip(near, far)]
            up = [jnp.where(low, y, x) for x, y in zip(near, far)]
        for h in (0, 1):
            write(probe, 0, h, own[h])
            write(probe, 1, h, down[h])
            write(probe, 2, h, up[h])


def pooling(parity):
    row = lax.broadcasted_iota(jnp.int32, (256, HALF), 0)
    column = lax.broadcasted_iota(jnp.int32, (256, HALF), 1)
    return jnp.where((row >> 2) + 64 * parity == column, 1.0 / 16.0, 0.0).astype(BF16)


def split3(x):
    high = x.astype(BF16)
    rest = x - high.astype(F32)
    middle = rest.astype(BF16)
    low = (rest - middle.astype(F32)).astype(BF16)
    return high, middle, low


def pool_into(lanes, sums, rows, count, write):
    total = None
    for parity in (0, 1):
        matrix = pooling(parity)
        own, down, up = (
            [
                jnp.concatenate(
                    [
                        sums[2 * part + h, pl.ds(n * count * 8 + 2 * pair + parity, count, stride=8), :]
                        for n in range(rows)
                        for pair in range(4)
                    ],
                    axis=0,
                )
                for h in (0, 1)
            ]
            for part in range(3)
        )
        lane = lax.broadcasted_iota(jnp.int32, own[0].shape, 1)
        d0, d1 = (pltpu.roll(x, HALF - 4, 1) for x in down)
        u0, u1 = (pltpu.roll(x, 4, 1) for x in up)
        low = own[0] + (jnp.where(lane >= HALF - 4, d1, d0) + jnp.where(lane < 4, u1, u0))
        high = own[1] + (jnp.where(lane >= HALF - 4, d0, d1) + jnp.where(lane < 4, u0, u1))
        for part in split3(jnp.concatenate([low, high], axis=1)):
            term = jnp.dot(part, matrix, preferred_element_type=F32)
            total = term if total is None else total + term
    for n in range(rows):
        for pair in range(4):
            start = (n * 4 + pair) * count
            write(n, pair, total[start : start + count])


GROUP = 8
EDGE_GROUP = 16


def weight_keys(first, last):
    reach = {0: (-4, 7), 1: (-3, 6), 2: (-1, 4)}
    return [
        (r, part)
        for part, (low, high) in reach.items()
        for r in range(max(first, low), min(last, high) + 1)
    ]


def fetch_all(copies):
    for copy in copies:
        copy.start()
    return copies


def pack_kernel(
    where, winds_hbm, obs_hbm, field_hbm, up, down, winds, obs, lent, sems
):
    lons = obs.shape[0]
    outer = field_hbm.at[:, pl.ds(lax.rem(where[0], 2) * (lons - 4), 4)]
    copies = fetch_all(
        [
            pltpu.make_async_copy(winds_hbm, winds, sems.at[0]),
            pltpu.make_async_copy(obs_hbm, obs, sems.at[1]),
            pltpu.make_async_copy(outer, lent, sems.at[2]),
        ]
    )
    for copy in copies:
        copy.wait()
    up[0:3] = winds[0, lons - 3 :]
    up[3:6] = winds[1, lons - 3 :]
    up[6:8] = obs[lons - 2 :]
    up[8:10] = obs[lons - 2 :]
    down[0:4] = winds[0, 0:4]
    down[4:7] = winds[1, 0:3]
    down[7:9] = obs[0:2]


def split_by_core(where, values, mine, other):
    first = lax.rem(where[0], 2) == 0
    for pair in range(mine.shape[1] // HALF):
        columns = slice(pair * HALF, (pair + 1) * HALF)
        a, b = values[0, pair], values[1, pair]
        mine[:, columns] = jnp.where(first, a, b)
        other[:, columns] = jnp.where(first, b, a)


def interior_kernel(
    where, winds, obs, field_hbm, after, mine, other, part_low, part_high, sides,
    coef, weights, sums, field, sems,
):
    count, lons = field.shape[0], field.shape[1]
    blocks = lons // 4
    field_copy = pltpu.make_async_copy(field_hbm, field, sems.at[0])
    field_copy.start()
    side_copies = [
        pltpu.make_async_copy(
            field_hbm.at[:, pl.ds(start, 4)], sides.at[:, pl.ds(4 * n, 4)], sems.at[1 + n]
        )
        for n, start in enumerate((0, lons - 4))
    ]
    for copy in side_copies:
        copy.start()
    lanes = Lanes()

    def coefficients(lon, carry):
        write_coefficients(
            coef,
            lon,
            halves(winds, 0, lon),
            halves(winds, 0, jnp.minimum(lon + 1, lons - 1)),
            halves(winds, 1, lon),
            lanes,
        )
        return carry

    lax.fori_loop(0, lons, coefficients, 0, unroll=8)

    def weigh(first, last, block, carry):
        base = block * 4

        def get(plane, r):
            return halves(coef, plane, base + r)

        result = block_weights(lanes, get, lambda r: halves(obs, base + r), first, last)
        for (r, part), value in result.items():
            store(weights, value, block, part, r + 4)
        return carry

    spans = ((0, 1, 2, 7), (1, blocks - 1, -4, 7), (blocks - 1, blocks, -4, -1))
    for start, stop, first, last in spans:
        lax.fori_loop(start, stop, functools.partial(weigh, first, last), 0, unroll=stop - start)
    field_copy.wait()
    groups = count // GROUP

    def sweep(first, last, step, carry):
        block = step // groups
        start = (step % groups) * GROUP

        def write(probe, part, h, value):
            row = pl.multiple_of((block * count + probe) * 8, 8)
            sums[2 * part + h, pl.ds(row, 8), :] = value

        apply_weights(
            lanes,
            weight_keys(first, last),
            lambda r, part: halves(weights, block, part, r + 4),
            lambda probe, r: halves(field, probe, block * 4 + r),
            write,
            [start + n for n in range(GROUP)],
        )
        return carry

    for start, stop, first, last in spans:
        lax.fori_loop(start * groups, stop * groups, functools.partial(sweep, first, last), 0)

    def put(n, pair, value):
        if n == 0:
            part_low[:, pair * HALF : (pair + 1) * HALF] = value
        elif n == blocks - 1:
            part_high[:, pair * HALF : (pair + 1) * HALF] = value
        else:
            values[divmod((n - 1) * 4 + pair, pieces)] = value

    values = {}
    pieces = mine.shape[1] // HALF
    pool_into(lanes, sums, blocks, count, put)
    split_by_core(where, values, mine, other)
    for copy in side_copies:
        copy.wait()


def edge_sums(winds, obs, from_low, from_high, sources, coef, weights, sums, spans, jobs, put):
    count, lons = sources[0][0].shape[0], obs.shape[0]
    total = count * len(sources)
    lanes = Lanes()

    def wind(which, lon):
        if lon < 0:
            return halves(from_low, 3 * which + lon + 3)
        if lon >= lons:
            return halves(from_high, min(4 * which + lon - lons, 6))
        return halves(winds, which, lon)

    def weight_at(lon):
        if lon < 0:
            return halves(from_low, 6 + lon + 2)
        if lon >= lons:
            return halves(from_high, 7 + lon - lons)
        return halves(obs, lon)

    slots = {}
    for start, stop in spans:
        for lon in range(start, stop + 1):
            slots[lon] = len(slots)
            write_coefficients(
                coef, slots[lon], wind(0, lon), wind(0, min(lon + 1, stop)), wind(1, lon), lanes
            )
    for n, (base, first, last) in enumerate(jobs):
        result = block_weights(
            lanes,
            lambda plane, r: halves(coef, plane, slots[base + r]),
            lambda r: weight_at(base + r),
            first,
            last,
        )
        for (r, part), value in result.items():
            store(weights, value, n, part, r + 4)

    def sweep(source, step, carry):
        field, index = sources[source]
        for n, (base, first, last) in enumerate(jobs):

            def write(probe, part, h, value):
                row = pl.multiple_of((n * total + source * count + probe) * 8, 8)
                sums[2 * part + h, pl.ds(row, 8), :] = value

            apply_weights(
                lanes,
                weight_keys(first, last),
                lambda r, part: halves(weights, n, part, r + 4),
                lambda probe, r: halves(field, probe, index(base + r)),
                write,
                [step * EDGE_GROUP + k for k in range(EDGE_GROUP)],
            )
        return carry

    for source in range(len(sources)):
        lax.fori_loop(0, count // EDGE_GROUP, functools.partial(sweep, source), 0)
    pool_into(lanes, sums, len(jobs), total, put)


def share_kernel(
    where, winds, obs, from_low, from_high, field, borrowed, out, coef, weights, sums
):
    lons = obs.shape[0]
    core = lax.rem(where[0], 2)

    def put(n, pair, value):
        out[:, pair * HALF : (pair + 1) * HALF] = value

    @pl.when(core == 0)
    def _():
        edge_sums(
            winds, obs, from_low, from_high,
            ((field, lambda lon: lon - (lons - 8)), (borrowed, lambda lon: lon - (lons - 4))),
            coef, weights, sums, ((lons - 3, lons + 3),), ((lons, -4, -1),), put,
        )

    @pl.when(core == 1)
    def _():
        edge_sums(
            winds, obs, from_low, from_high,
            ((field, lambda lon: lon), (borrowed, lambda lon: lon)),
            coef, weights, sums, ((-3, 3),), ((-4, 4, 7),), put,
        )


def rest_kernel(
    where, winds, obs, from_low, from_high, field, part_low, part_high, after, after_inner,
    mine, other, coef, weights, sums,
):
    lons = obs.shape[0]
    values = {}

    def put(n, pair, value):
        columns = slice(pair * HALF, (pair + 1) * HALF)
        values[n, pair] = value + (part_low, part_high)[n][:, columns]

    edge_sums(
        winds, obs, from_low, from_high,
        ((field, lambda lon: lon if lon < 4 else lon - (lons - 8)),),
        coef, weights, sums,
        ((-2, 4), (lons - 5, lons + 1)),
        ((0, 0, 1), (lons - 4, 0, 3)),
        put,
    )
    split_by_core(where, values, mine, other)


def self_product(panel):
    return lax.dot_general(
        panel,
        panel,
        (((1,), (1,)), ((), ())),
        precision=lax.Precision.HIGHEST,
        preferred_element_type=F32,
    )


def assemble(where, chip, far, panel):
    rows = chip.shape[0] // 2
    for k in range(4):
        at = pl.multiple_of(lax.bitwise_xor(where[0], jnp.int32(k)) * rows, 8)
        panel[pl.ds(at, rows)] = (chip, far)[k // 2][(k % 2) * rows : (k % 2 + 1) * rows]


def inner_gram_kernel(where, chip, far, out, panel):
    assemble(where, chip, far, panel)
    out[...] = self_product(panel[...])


def gram_kernel(where, inner_gram, inner_chip, inner_far, edge_chip, edge_far, panel, out):
    width = inner_chip.shape[1]
    assemble(where, edge_chip, edge_far, panel.at[:, width:])
    gram = self_product(panel[:, width:]) + inner_gram[...]
    half = gram.shape[0] // 2
    quarters = (gram[:half, :half], gram[half:, :half], gram[half:, half:])
    rows = out.shape[0] // 3
    for n, quarter in enumerate(quarters):
        out[n * rows : (n + 1) * rows] = jnp.concatenate(
            [quarter[k : k + rows] for k in range(0, half, rows)], axis=1
        )
    assemble(where, inner_chip, inner_far, panel.at[:, :width])


def copies_kernel(mine, other, out):
    total = mine[...] + other[...]
    for n in range(out.shape[0]):
        out[n] = total


def factor_kernel(
    where, grams, panel, panel_other, basis, upper, inverse
):
    packed = grams[0]
    for n in range(1, grams.shape[0]):
        packed = packed + grams[n]
    rows = packed.shape[0] // 3
    half = upper.shape[0] // 2
    size = 2 * half
    first, cross, second = (
        jnp.concatenate(
            [packed[n * rows : (n + 1) * rows, k : k + half] for k in range(0, HALF, half)], axis=0
        )
        for n in range(3)
    )
    gram = jnp.concatenate(
        [
            jnp.concatenate([first, cross.T], axis=1),
            jnp.concatenate([cross, second], axis=1),
        ],
        axis=0,
    )
    row = lax.broadcasted_iota(jnp.int32, (size, size), 0)
    column = lax.broadcasted_iota(jnp.int32, (size, size), 1)
    state = jnp.concatenate([gram, jnp.where(row == column, 1.0, 0.0).astype(F32)], axis=1)
    tiles = [state[8 * t : 8 * t + 8] for t in range(size // 8)]
    full = (8, 2 * size)
    sub = lax.broadcasted_iota(jnp.int32, full, 0)
    scales = []
    for own in range(size // 8):
        spread = {
            (t, j): jnp.broadcast_to(tiles[t][:, 8 * own + j : 8 * own + j + 1], full)
            for t in range(own, size // 8)
            for j in range(8)
        }
        pivots = {
            (i, j): jnp.broadcast_to(spread[own, j][i : i + 1], full)
            for i in range(8)
            for j in range(i + 1)
        }
        rows = [jnp.broadcast_to(tiles[own][j : j + 1], full) for j in range(8)]
        inverses = []
        for j in range(8):
            inverses.append(1.0 / pivots[j, j])
            scales.append(lax.rsqrt(pivots[j, j]))
            for i in range(j + 1, 8):
                ratio = pivots[i, j] * inverses[j]
                for m in range(i, 8):
                    pivots[m, i] = pivots[m, i] - ratio * pivots[m, j]
                rows[i] = rows[i] - ratio * rows[j]
                for t in range(own + 1, size // 8):
                    spread[t, i] = spread[t, i] - ratio * spread[t, j]
        for t in range(own + 1, size // 8):
            update = (spread[t, 0] * inverses[0]) * rows[0]
            for j in range(1, 8):
                update = update + (spread[t, j] * inverses[j]) * rows[j]
            tiles[t] = tiles[t] - update
        for j in range(8):
            tiles[own] = jnp.where(sub == j, rows[j], tiles[own])
    for t in range(size // 8):
        scale = scales[8 * t]
        for at in range(1, 8):
            scale = jnp.where(sub == at, scales[8 * t + at], scale)
        scaled = tiles[t] * scale
        column = lax.broadcasted_iota(jnp.int32, (8, size), 1)
        here = lax.broadcasted_iota(jnp.int32, (8, size), 0) + 8 * t
        upper[8 * t : 8 * t + 8] = jnp.where(column >= here, scaled[:, :size], 0.0)
        inverse[8 * t : 8 * t + 8] = scaled[:, size:]
    blocks, count, width = basis.shape
    own_rows = inverse[pl.ds(pl.multiple_of(where[0] * count, 8), count)]

    def project(columns):
        return jnp.dot(
            own_rows, columns, precision=lax.Precision.HIGHEST, preferred_element_type=F32
        )

    core = lax.rem(where[0], 2)
    half = (blocks - 2) // 2

    for side, part in ((core, panel), (1 - core, panel_other)):
        for n in range(half):
            basis[1 + side * half + n] = project(part[:, n * width : (n + 1) * width])
        basis[side * (blocks - 1)] = project(part[:, half * width :])


VMEM = pl.BlockSpec(memory_space=pltpu.VMEM)
SMEM = pl.BlockSpec(memory_space=pltpu.SMEM)
HBM = pl.BlockSpec(memory_space=pltpu.HBM)
ANY = pl.BlockSpec(memory_space=pl.ANY)
MIB = 1024 * 1024


def shape(*dims):
    return jax.ShapeDtypeStruct(dims, F32)


def call(kernel, name, out_shape, in_specs, scratch=(), flops=1_000_000):
    return pl.pallas_call(
        kernel,
        out_shape=out_shape,
        in_specs=in_specs,
        out_specs=jax.tree.map(lambda _: VMEM, out_shape),
        scratch_shapes=scratch,
        compiler_params=pltpu.CompilerParams(vmem_limit_bytes=32 * MIB),
        cost_estimate=pl.CostEstimate(flops=flops, bytes_accessed=100_000, transcendentals=0),
        name=name,
    )


def swap_probes(value, step):
    return lax.ppermute(value, "probe", [(i, i ^ step) for i in range(lax.axis_size("probe"))])


def body(increments, winds, obs_weight):
    count, lons, levels, lats = increments.shape
    blocks = lons // 4
    probes = count * lax.axis_size("probe")
    ring = lax.axis_size("lon")
    up = [(i, (i + 1) % ring) for i in range(ring)]
    down = [(i, (i - 1) % ring) for i in range(ring)]
    where = lax.axis_index("probe").reshape(1).astype(jnp.int32)
    dma = pltpu.SemaphoreType.DMA
    increments, winds, obs_weight = (
        pltpu.with_memory_space_constraint(x, pltpu.HBM) for x in (increments, winds, obs_weight)
    )
    pack_up, pack_down, winds, obs_weight, lent = call(
        pack_kernel,
        "pack",
        (
            shape(10, levels, lats),
            shape(9, levels, lats),
            shape(2, lons, levels, lats),
            shape(lons, levels, lats),
            shape(count, 4, levels, lats),
        ),
        [SMEM, HBM, HBM, HBM],
        [dma((3,))],
    )(where, winds, obs_weight, increments)
    borrowed = swap_probes(lent, 1)
    from_low = lax.ppermute(pack_up, "lon", up)
    from_high = lax.ppermute(pack_down, "lon", down)
    inner, inner_other, part_low, part_high, sides = call(
        interior_kernel,
        "interior",
        (
            shape(count, (blocks - 2) * 256),
            shape(count, (blocks - 2) * 256),
            shape(count, 512),
            shape(count, 512),
            shape(count, 8, levels, lats),
        ),
        [SMEM, VMEM, VMEM, HBM, ANY],
        [
            pltpu.VMEM((PLANES, lons, levels, lats), F32),
            pltpu.VMEM((blocks, 3, 12, levels, lats), F32),
            pltpu.VMEM((6, blocks * count * 8, HALF), F32),
            pltpu.VMEM((count, lons, levels, lats), F32),
            dma((3,)),
        ],
    )(where, winds, obs_weight, increments, borrowed)
    edge_scratch = [
        pltpu.VMEM((PLANES, 14, levels, lats), F32),
        pltpu.VMEM((2, 3, 12, levels, lats), F32),
        pltpu.VMEM((6, 2 * count * 8, HALF), F32),
    ]
    share = call(
        share_kernel, "share", shape(2 * count, 512), [SMEM] + [VMEM] * 6, edge_scratch
    )(where, winds, obs_weight, from_low, from_high, sides, borrowed)
    size = lax.axis_size("probe")
    arrived = lax.ppermute(
        share,
        ("lon", "probe"),
        [
            (i * size + p, (up, down)[p & 1][i][1] * size + p)
            for i in range(ring)
            for p in range(size)
        ],
    )
    inner_chip = jnp.concatenate([inner, swap_probes(inner_other, 1)], axis=0)
    rest, rest_other = call(
        rest_kernel, "rest", (shape(count, 512),) * 2, [SMEM] + [VMEM] * 7 + [ANY, ANY], edge_scratch
    )(where, winds, obs_weight, from_low, from_high, sides, part_low, part_high, share, inner_chip)
    inner_far = swap_probes(inner_chip, 2)
    inner_gram = call(
        inner_gram_kernel,
        "inner_gram",
        shape(probes, probes),
        [SMEM, VMEM, VMEM],
        [pltpu.VMEM((probes, (blocks - 2) * 256), F32)],
    )(where, inner_chip, inner_far)
    edge_chip = jnp.concatenate([rest, swap_probes(rest_other, 1)], axis=0) + arrived
    edge_far = swap_probes(edge_chip, 2)
    packing = (3 * (probes // 2) ** 2 // HALF, HALF)
    panel, gram = call(
        gram_kernel,
        "gram",
        (shape(probes, blocks * 256), shape(*packing)),
        [SMEM] + [VMEM] * 5,
    )(where, inner_gram, inner_chip, inner_far, edge_chip, edge_far)
    panel, gram_other = lax.optimization_barrier((panel, swap_probes(gram, 1)))
    grams = call(copies_kernel, "copies", shape(ring, *packing), [VMEM] * 2)(
        gram, gram_other
    )
    grams = lax.all_to_all(grams, "lon", 0, 0, tiled=True)
    basis, upper = call(
        factor_kernel,
        "factor",
        (shape(blocks, count, 512), shape(probes, probes)),
        [SMEM] + [VMEM] * 3,
        [pltpu.VMEM((probes, probes), F32)],
    )(where, grams, panel, swap_probes(panel, 1))
    return basis.transpose(1, 0, 2), upper


def solution(mesh):
    in_specs = (P("probe", "lon", None, None), P(None, "lon", None, None), P("lon", None, None))
    out_specs = (P("probe", "lon", None), P())
    return jax.shard_map(body, mesh=mesh, in_specs=in_specs, out_specs=out_specs, check_vma=False)
```
